32 devices in a mesh: dp: 4 (over z), row: 2 (over y), col: 4 (over x, core).
Axes of the slice: x: 2, y: 2, z: 4, core: 2. Of those that a mesh axis runs over, the one named last changes fastest.
Arguments:
- x_prompt: bfloat16 [4, 2048, 768], P('dp', 'row', 'col'), may hold values from -6 to 6
- x_cont: bfloat16 [4, 256, 768], P('dp', 'row', 'col'), may hold values from -6 to 6
- seg_ids: int32 [4, 256], P('dp', 'row'), may hold values from 0 to 128, as said below
- layer_map: int32 [6], replicated, may hold values from 0 to 2, as said below
- w_qkv: bfloat16 [3, 768, 3, 768], P(None, ('dp', 'row'), None, 'col'), may hold values from -0.21875 to 0.21875
- bias_qv: bfloat16 [3, 2, 768], P(None, None, 'col'), may hold values from -3 to 3
- w_out: bfloat16 [3, 768, 768], P(None, ('dp', 'row'), 'col'), may hold values from -1.75 to 1.75
- b_out: bfloat16 [3, 768], P(None, 'col'), may hold values from -2 to 2
- w_up: bfloat16 [3, 768, 3072], P(None, ('dp', 'row'), 'col'), may hold values from -0.21875 to 0.21875
- b_up: bfloat16 [3, 3072], P(None, 'col'), may hold values from -3 to 3
- w_down: bfloat16 [3, 768, 3072], P(None, ('dp', 'row'), 'col'), may hold values from -0.109375 to 0.109375
- b_down: bfloat16 [3, 768], P(None, 'col'), may hold values from -2 to 2
- ln1_gain: bfloat16 [3, 768], P(None, 'col'), may hold values from 0.099609375 to 1.8984375
- ln1_bias: bfloat16 [3, 768], P(None, 'col'), may hold values from -2 to 2
- ln2_gain: bfloat16 [3, 768], P(None, 'col'), may hold values from 0.099609375 to 1.8984375
- ln2_bias: bfloat16 [3, 768], P(None, 'col'), may hold values from -2 to 2
- cot_prompt: bfloat16 [4, 2048, 768], P('dp', 'row', 'col'), may hold values from -6 to 6
- cot_cont: bfloat16 [4, 256, 768], P('dp', 'row', 'col'), may hold values from -6 to 6
Outputs:
- y_prompt: bfloat16 [4, 2048, 768], P('dp', 'row', 'col')
- y_cont: bfloat16 [4, 256, 768], P('dp', 'row', 'col')
- dx_prompt: bfloat16 [4, 2048, 768], P('dp', 'row', 'col')
- dx_cont: bfloat16 [4, 256, 768], P('dp', 'row', 'col')
- grad_w_qkv: float32 [3, 768, 3, 768], P(None, ('dp', 'row'), None, 'col')
- grad_bias_qv: float32 [3, 2, 768], P(None, None, 'col')
- grad_w_out: float32 [3, 768, 768], P(None, ('dp', 'row'), 'col')
- grad_b_out: float32 [3, 768], P(None, 'col')
- grad_w_up: float32 [3, 768, 3072], P(None, ('dp', 'row'), 'col')
- grad_b_up: float32 [3, 3072], P(None, 'col')
- grad_w_down: float32 [3, 768, 3072], P(None, ('dp', 'row'), 'col')
- grad_b_down: float32 [3, 768], P(None, 'col')
- grad_ln1_gain: float32 [3, 768], P(None, 'col')
- grad_ln1_bias: float32 [3, 768], P(None, 'col')
- grad_ln2_gain: float32 [3, 768], P(None, 'col')
- grad_ln2_bias: float32 [3, 768], P(None, 'col')
The draws below stay inside these ranges and needn't reach their ends.
Inputs may be any that keep to these rules, and one draw needn't show every extreme that they name: `seg_ids`: A token's id is the index, within its group's continuation tokens, of the first token of its continuation: ids never fall along a group, each aligned block of 128 continuation tokens starts a new continuation, no continuation crosses such a block, and the last such block of every group is one whole continuation. `layer_map`: every one of the 3 blocks is used by some layer.
All inputs are finite; a program needn't handle non-finite values.
Results may differ from the reference program's by a relative error of at most 0.023.
Values may be sent and summed in bfloat16 or wider, within the bound.
No kernel may reach another device: no remote copies, remote signals or barrier semaphores. Data moves between devices by JAX's collectives and lax.ppermute only.
A program may use at most 576 MiB of HBM per device.

```python
import jax
import jax.numpy as jnp
from jax import lax

D = 768
HEADS = 12
HD = 64
FF = 3072
PROMPT = 2048
CTOK_DEV = 128
LAYERS = 6
NBLOCK = 3
GROUPS = 4
CTOK = 256


def draw_seg_ids(key, part):
    positions = jnp.arange(CTOK, dtype=jnp.int32)
    spacing = max(CTOK_DEV // 3, 2)
    cut_here = jax.random.randint(key, (GROUPS, CTOK), 0, spacing) == 0
    cut_here = cut_here & (positions < CTOK - CTOK_DEV)[None, :]
    cut_here = cut_here | (positions % CTOK_DEV == 0)[None, :]
    start_pos = jnp.where(cut_here, positions[None, :], 0)
    return lax.cummax(start_pos, axis=1).astype(jnp.int32)


def draw_layer_map(key, part):
    first_ids = jax.random.permutation(jax.random.fold_in(key, 11), NBLOCK).astype(jnp.int32)
    rest_ids = jax.random.randint(jax.random.fold_in(key, 12), (LAYERS - NBLOCK,), 0, NBLOCK).astype(jnp.int32)
    return jnp.concatenate([first_ids, rest_ids])


def block_levels(stream_key, shape, pieces, smallest, largest):
    def one(dim, parts):
        draws = jax.random.uniform(jax.random.fold_in(jax.random.fold_in(stream_key, 6), dim), (parts,), jnp.float32, smallest / len(pieces), largest / len(pieces))
        return jnp.repeat(jnp.exp(draws), shape[dim] // parts).reshape((-1,) + (1,) * (len(shape) - dim - 1))

    factor_of = one(*pieces[0])
    for cut in pieces[1:]:
        factor_of = factor_of * one(*cut)
    return factor_of


def scatter_about(stream_key, shape, width, limit, shards=(), held_as=jnp.bfloat16):
    array = jax.random.normal(stream_key, shape, jnp.float32) * width
    if len(shards) > 0:
        array = block_levels(stream_key, shape, shards, -0.22, 0.18) * array
    return jnp.clip(array, min=-limit, max=limit).astype(held_as)


def setup_inputs(seed: int = 0) -> dict:
    key_of = jax.random.split(jax.random.key(seed), 19)
    return {
        "x_prompt": scatter_about(key_of[0], (GROUPS, PROMPT, D), 1.0, 6.0, ((0, 4), (1, 2), (2, 4))),
        "x_cont": scatter_about(key_of[1], (GROUPS, CTOK, D), 1.0, 6.0, ((0, 4), (1, 2), (2, 4))),
        "seg_ids": draw_seg_ids(jax.random.fold_in(key_of[18], 71), 0),
        "layer_map": draw_layer_map(jax.random.fold_in(key_of[18], 71), 0),
        "w_qkv": scatter_about(key_of[4], (NBLOCK, D, 3, D), D ** -0.5, 0.21875, ((1, 8), (3, 4))),
        "bias_qv": scatter_about(key_of[5], (NBLOCK, 2, D), 0.5, 3.0, ((2, 4),)),
        "w_out": scatter_about(key_of[6], (NBLOCK, D, D), (max(D // 64, 1)) ** -0.5, 1.75, ((1, 8), (2, 4))),
        "b_out": scatter_about(key_of[7], (NBLOCK, D), 0.3, 2.0, ((1, 4),)),
        "w_up": scatter_about(key_of[8], (NBLOCK, D, FF), D ** -0.5, 0.21875, ((1, 8), (2, 4))),
        "b_up": scatter_about(key_of[9], (NBLOCK, FF), 0.5, 3.0, ((1, 4),)),
        "w_down": scatter_about(key_of[10], (NBLOCK, D, FF), FF ** -0.5, 0.109375, ((1, 8), (2, 4))),
        "b_down": scatter_about(key_of[11], (NBLOCK, D), 0.3, 2.0, ((1, 4),)),
        "ln1_gain": jnp.clip(1.0 + 0.18 * jax.random.normal(key_of[12], (NBLOCK, D), jnp.float32), 0.099609375, 1.8984375).astype(jnp.bfloat16),
        "ln1_bias": scatter_about(key_of[13], (NBLOCK, D), 0.3, 2.0, ((1, 4),)),
        "ln2_gain": jnp.clip(1.0 + 0.18 * jax.random.normal(key_of[14], (NBLOCK, D), jnp.float32), 0.099609375, 1.8984375).astype(jnp.bfloat16),
        "ln2_bias": scatter_about(key_of[15], (NBLOCK, D), 0.3, 2.0, ((1, 4),)),
        "cot_prompt": scatter_about(key_of[16], (GROUPS, PROMPT, D), 1.0, 6.0, ((0, 4), (1, 2), (2, 4))),
        "cot_cont": scatter_about(key_of[17], (GROUPS, CTOK, D), 1.0, 6.0, ((0, 4), (1, 2), (2, 4))),
    }


@jax.custom_vjp
def low(v):
    return lax.optimization_barrier(v.astype(jnp.bfloat16)).astype(jnp.float32)

@jax.custom_vjp
def low_back(v):
    return v

def low_keep(v):
    return (low(v), None)

def low_pass(kept, grad):
    return (grad,)

def back_keep(v):
    return (v, None)

def back_low(kept, grad):
    return (low(grad),)
low.defvjp(low_keep, low_pass)
low_back.defvjp(back_keep, back_low)
NORM_EPS = 1e-05
MASK_FILL = -1000000000.0
GELU_COEF = 0.7978845608028654

def matmul(left_side, right_side):
    return jnp.dot(left_side, right_side, precision=lax.Precision.HIGHEST, preferred_element_type=jnp.float32)

def round_both(values):
    return low(low_back(values))

def layer_norm(hidden, gain_row, shift_row):
    row_mean = lax.optimization_barrier(jnp.mean(hidden, axis=-1, keepdims=True))
    row_square = lax.optimization_barrier(jnp.mean(hidden * hidden, axis=-1, keepdims=True))
    inverse = lax.rsqrt(row_square - row_mean * row_mean + NORM_EPS)
    return (hidden - row_mean) * inverse * gain_row + shift_row

def gelu_tanh(values):
    return 0.5 * values * (1.0 + jnp.tanh(GELU_COEF * (values + 0.044715 * values * values * values)))

def attend(queries, key_rows, value_rows, allowed):
    seq_len = queries.shape[0]

    def split_heads(values):
        return values.reshape(seq_len, HEADS, HD).transpose(1, 0, 2)

    def one_head(head_args):
        head_q, head_k, head_v = head_args
        scores = low_back(matmul(head_q, head_k.T) * HD ** (-0.5))
        scores = jnp.where(allowed, scores, MASK_FILL)
        row_max = lax.optimization_barrier(jnp.max(scores, axis=-1, keepdims=True))
        exp_scores = jnp.exp(scores - row_max)
        attn_prob = exp_scores / lax.optimization_barrier(jnp.sum(exp_scores, axis=-1, keepdims=True))
        return matmul(low(attn_prob), head_v)
    outputs = lax.map(jax.checkpoint(one_head), (split_heads(queries), split_heads(key_rows), split_heads(value_rows)))
    return outputs.transpose(1, 0, 2).reshape(seq_len, D)

def one_layer(hidden, allowed, weights):
    w_qkv, bias_qv, w_out, b_out, w_up, b_up, w_down, b_down, ln1_gain, ln1_bias, ln2_gain, ln2_bias = weights
    seq_len = hidden.shape[0]
    normed = low(layer_norm(hidden, ln1_gain, ln1_bias))
    qkv_bias = jnp.stack([bias_qv[0], jnp.zeros_like(bias_qv[0]), bias_qv[1]])
    mixed_qkv = matmul(normed, w_qkv.reshape(D, 3 * D)).reshape(seq_len, 3, D)
    mixed_qkv = round_both(mixed_qkv + qkv_bias)
    attn_out = round_both(attend(mixed_qkv[:, 0], mixed_qkv[:, 1], mixed_qkv[:, 2], allowed))
    hidden = hidden + low_back(matmul(attn_out, w_out.T) + b_out)
    normed = low(layer_norm(hidden, ln2_gain, ln2_bias))
    up_proj = low_back(matmul(normed, w_up) + b_up)
    activation = low(gelu_tanh(up_proj))
    return hidden + low_back(matmul(activation, w_down.T) + b_down)

def run_group(params, layer_map, prompt_rows, cont_rows, seg_row):
    hidden = jnp.concatenate([prompt_rows, cont_rows], axis=0)
    seq_len = hidden.shape[0]
    positions = jnp.arange(seq_len, dtype=jnp.int32)
    segment = jnp.concatenate([jnp.full((PROMPT,), -1, jnp.int32), seg_row.astype(jnp.int32)])
    is_prompt = positions < PROMPT
    allowed = (positions[None, :] <= positions[:, None]) & (is_prompt[None, :] | (segment[None, :] == segment[:, None]))
    for layer_pos in range(LAYERS):
        block_index = layer_map[layer_pos]
        hidden = one_layer(hidden, allowed, tuple((member[block_index] for member in params)))
    return hidden

def reference(x_prompt, x_cont, seg_ids, layer_map, w_qkv, bias_qv, w_out, b_out, w_up, b_up, w_down, b_down, ln1_gain, ln1_bias, ln2_gain, ln2_bias, cot_prompt, cot_cont):
    params = tuple((member.astype(jnp.float32) for member in (w_qkv, bias_qv, w_out, b_out, w_up, b_up, w_down, b_down, ln1_gain, ln1_bias, ln2_gain, ln2_bias)))

    def forward(weights, prompt_in, cont_in):

        def per_group(group_args):
            return run_group(weights, layer_map, group_args[0], group_args[1], group_args[2])
        outputs = lax.map(jax.checkpoint(per_group), (prompt_in, cont_in, seg_ids))
        return (outputs[:, :PROMPT], outputs[:, PROMPT:])
    (y_prompt, y_cont), pull_back = jax.vjp(forward, params, x_prompt.astype(jnp.float32), x_cont.astype(jnp.float32))
    gradients, dx_prompt, dx_cont = pull_back((cot_prompt.astype(jnp.float32), cot_cont.astype(jnp.float32)))
    return (y_prompt.astype(jnp.bfloat16), y_cont.astype(jnp.bfloat16), dx_prompt.astype(jnp.bfloat16), dx_cont.astype(jnp.bfloat16), gradients[0], gradients[1], gradients[2], gradients[3], gradients[4], gradients[5], gradients[6], gradients[7], gradients[8], gradients[9], gradients[10], gradients[11])
```

```python
import functools

import jax
import jax.numpy as jnp
from jax import lax
from jax.experimental import pallas as pl
from jax.experimental.pallas import tpu as pltpu
from jax.sharding import Mesh
from jax.sharding import PartitionSpec as P

D = 768
HD = 64
LAYERS = 6
NB = 3
HEADS_COL = 3
PACK = 1792
NORM_EPS = 1e-05
MASK_FILL = -1000000000.0
GELU_COEF = 0.7978845608028654
F32 = jnp.float32
BF16 = jnp.bfloat16
MIB = 1024 * 1024


def nn(a, b):
    return lax.dot_general(a, b, (((1,), (0,)), ((), ())), preferred_element_type=F32)


def nt(a, b):
    return lax.dot_general(a, b, (((1,), (1,)), ((), ())), preferred_element_type=F32)


def tn(a, b):
    return lax.dot_general(a, b, (((0,), (0,)), ((), ())), preferred_element_type=F32)


def stats(hidden):
    mean = jnp.sum(hidden, axis=1, keepdims=True) * (1.0 / D)
    square = jnp.sum(hidden * hidden, axis=1, keepdims=True) * (1.0 / D)
    inverse = lax.rsqrt(square - mean * mean + NORM_EPS)
    return (hidden - mean) * inverse, inverse


def norm_back(grad, gain, centered, inverse):
    scaled = grad * gain
    first = jnp.sum(scaled, axis=1, keepdims=True) * (1.0 / D)
    second = jnp.sum(scaled * centered, axis=1, keepdims=True) * (1.0 / D)
    return inverse * (scaled - first - centered * second)


def colsum(value):
    return jnp.sum(value, axis=0, keepdims=True)


def to_row(column):
    rows = column.shape[0]
    return jnp.transpose(jnp.broadcast_to(column, (rows, 128)))[0:1, :]


class Row:
    def __init__(self, ref, layer):
        self.ref, self.base = ref, layer * 8

    def __getitem__(self, j):
        return self.ref[self.base + j]


def strip(kernel, layer, count, deps):
    def run(sc, *refs):
        kernel(Row(sc, layer), *refs[:count], *refs[count + deps :])

    return run


def params(limit, **more):
    return pltpu.CompilerParams(vmem_limit_bytes=limit * MIB, **more)


def cost(flops, nbytes, trans=0):
    return pl.CostEstimate(flops=int(flops), bytes_accessed=int(nbytes), transcendentals=int(trans))


def weight_copies(mine, other, my_x, wout, wud, sems):
    copies = []
    for s in range(4):
        src = (mine if s % 2 == 0 else other).at[my_x ^ (s // 2)]
        copies.append(
            (
                pltpu.make_async_copy(src.at[:, pl.ds(1536, 256)], wout.at[s], sems.at[0, s]),
                pltpu.make_async_copy(src.at[:, pl.ds(0, 1536)], wud.at[s], sems.at[1, s]),
            )
        )
    return copies


def start_weights(sc, packs, wout, wud, sems, out_first):
    def go(pair):
        copies = weight_copies(pair[0], pair[1], sc[4], wout, wud, sems)
        order = (0, 1) if out_first else (1, 0)
        for kind in order:
            for s in range(4):
                copies[s][kind].start()

    if len(packs) == 1:
        go(packs[0])
    else:
        for k, pair in enumerate(packs):
            pl.when(sc[1] == k)(functools.partial(go, pair))


def mlp_fwd_kernel(ranks, last, prompt, sc, *refs):
    h_ref, o0, o1, o2, o3, vec_ref, bup_ref, nvec_ref = refs[:8]
    packs = [(refs[8 + 2 * k], refs[9 + 2 * k]) for k in range(ranks)]
    outs = refs[8 + 2 * ranks :]
    h1_ref, u_hbm, m_hbm, h_out = outs[:4]
    wout, wud, sems, u_ref, m_ref, osem = outs[-6:]
    start_weights(sc, packs, wout, wud, sems, True)
    waits = weight_copies(packs[0][0], packs[0][1], sc[4], wout, wud, sems)
    total = h_ref[...] + vec_ref[0, 0:1, :]
    for s, o_ref in enumerate((o0, o1, o2, o3)):
        waits[s][0].wait()
        total = total + nt(o_ref[...], wout[s])
    h1_ref[...] = total
    centered, _ = stats(total)
    a2 = (centered * vec_ref[0, 2:3, :] + vec_ref[0, 3:4, :]).astype(BF16)
    h_out[...] = total + vec_ref[0, 1:2, :]
    stores = []
    for s in range(4):
        waits[s][1].wait()
        bias = bup_ref[0, pl.ds(sc[3] ^ s, 1), 0, :]
        up = nn(a2, wud[s, :, 0:768]) + bias
        u_ref[s] = up.astype(BF16)
        act = 0.5 * up * (1.0 + jnp.tanh(GELU_COEF * (up + 0.044715 * up * up * up)))
        act = act.astype(BF16)
        m_ref[s] = act
        stores.append(pltpu.make_async_copy(u_ref.at[s], u_hbm.at[s], osem.at[0, s]))
        stores.append(pltpu.make_async_copy(m_ref.at[s], m_hbm.at[s], osem.at[1, s]))
        stores[-2].start()
        stores[-1].start()
        h_out[...] += nt(act, wud[s, :, 768:1536])
    if last:
        y_refs = outs[4:8]
        send_features(sc, h_out, y_refs)
    else:
        a_ref, ap_ref = outs[4:6]
        centered, _ = stats(h_out[...])
        nxt = (centered * nvec_ref[0, 4:5, :] + nvec_ref[0, 5:6, :]).astype(BF16)
        a_ref[...] = nxt
        ap_ref[...] = nxt[:prompt]
    for copy in stores:
        copy.wait()


def send_features(sc, value, refs):
    width = refs[0].shape[1]
    for s, ref in enumerate(refs):
        for c in range(4):

            def put(ref=ref, c=c):
                ref[...] = value[:, c * width : (c + 1) * width].astype(BF16)

            pl.when((sc[3] ^ s) == c)(put)


def whole_spec(shape):
    return pl.BlockSpec(shape, lambda i, sc: (0,) * len(shape))


def vec_specs(layer):
    at = layer * 8
    return [
        pl.BlockSpec((1, 8, D), lambda i, sc: (sc[at], 0, 0)),
        pl.BlockSpec((1, 4, 1, D), lambda i, sc: (sc[at], 0, 0, 0)),
        pl.BlockSpec((1, 8, D), lambda i, sc: (sc[at + 2], 0, 0)),
    ]


WSCR = [
    pltpu.VMEM((4, D, 256), BF16),
    pltpu.VMEM((4, D, 1536), BF16),
    pltpu.SemaphoreType.DMA((2, 4)),
]
ANY = pl.BlockSpec(memory_space=pl.ANY)
HBM = pl.BlockSpec(memory_space=pltpu.HBM)


def mlp_fwd(layer, sc, hidden, o_parts, vecs, bup, packs, prompt, last, width, deps=()):
    tok = hidden.shape[0]
    shapes = [
        jax.ShapeDtypeStruct((tok, D), F32),
        jax.ShapeDtypeStruct((4, tok, D), BF16),
        jax.ShapeDtypeStruct((4, tok, D), BF16),
        jax.ShapeDtypeStruct((tok, D), F32),
    ]
    if last:
        shapes += [jax.ShapeDtypeStruct((tok, width), BF16)] * 4
    else:
        shapes += [jax.ShapeDtypeStruct((tok, D), BF16), jax.ShapeDtypeStruct((prompt, D), BF16)]
    out_specs = [whole_spec(v.shape) for v in shapes]
    out_specs[1] = out_specs[2] = HBM
    ins = [hidden, *o_parts, vecs, bup, vecs, *[w for pair in packs for w in pair]]
    kernel = functools.partial(mlp_fwd_kernel, len(packs), last, prompt)
    return pl.pallas_call(
        strip(kernel, layer, len(ins), len(deps)),
        grid_spec=pltpu.PrefetchScalarGridSpec(
            num_scalar_prefetch=1,
            grid=(1,),
            in_specs=[whole_spec((tok, D))]
            + [whole_spec((tok, 256))] * 4
            + vec_specs(layer)
            + [ANY] * (2 * len(packs) + len(deps)),
            out_specs=out_specs,
            scratch_shapes=WSCR
            + [
                pltpu.VMEM((4, tok, D), BF16),
                pltpu.VMEM((4, tok, D), BF16),
                pltpu.SemaphoreType.DMA((2, 4)),
            ],
        ),
        out_shape=shapes,
        compiler_params=params(44),
        cost_estimate=cost(2 * tok * D * 6912, 16e6, tok * 3072),
        name="mlp_fwd",
    )(sc, *ins, *deps)


def mlp_bwd_kernel(ranks, others, first, prompt, sc, *refs):
    if first:
        g_ref, refs = refs[0], refs[1:]
    else:
        nin = 4 + 2 * others
        g_ref, hn_ref, p0_ref, rx_ref = refs[:4]
        rest = refs[4:nin]
        refs = refs[nin:]
    h1_ref, u_hbm, vec_ref, nvec_ref = refs[:4]
    packs = [(refs[4 + 2 * k], refs[5 + 2 * k]) for k in range(ranks)]
    outs = refs[4 + 2 * ranks :]
    gm_ref, du_ref, a2_ref, g1_ref, go_ref, d0, d1, d2, d3, small_ref = outs[:10]
    wout, wud, sems, u_ref, usem = outs[10:]
    loads = [pltpu.make_async_copy(u_hbm.at[s], u_ref.at[s], usem.at[s]) for s in range(4)]
    start_weights(sc, packs, wout, wud, sems, False)
    for copy in loads:
        copy.start()
    waits = weight_copies(packs[0][0], packs[0][1], sc[4], wout, wud, sems)
    small_ref[...] = jnp.zeros_like(small_ref)
    if first:
        grad = g_ref[...]
    else:
        g1_ref[...] = p0_ref[...].astype(F32) + rx_ref[...].astype(F32)
        for ref in rest:
            g1_ref[0:prompt, :] += ref[...].astype(F32)
        da1 = g1_ref[...]
        centered, inverse = stats(hn_ref[...])
        small_ref[8:9, :] = colsum(da1 * centered)
        small_ref[9:10, :] = colsum(da1)
        grad = g_ref[...] + norm_back(da1, nvec_ref[0, 4:5, :], centered, inverse)
    gm = grad.astype(BF16)
    gm_ref[...] = gm
    small_ref[4:5, :] = colsum(gm.astype(F32))
    for s in range(4):
        waits[s][1].wait()
        dm = nn(gm, wud[s, :, 768:1536])
        loads[s].wait()
        up = u_ref[s].astype(F32)
        square = up * up
        tanh = jnp.tanh(GELU_COEF * up * (1.0 + 0.044715 * square))
        slope = 0.5 * (1.0 + tanh) + 0.5 * up * (1.0 - tanh * tanh) * (
            GELU_COEF * (1.0 + 3.0 * 0.044715 * square)
        )
        du = (dm * slope).astype(BF16)
        du_ref[s] = du
        small_ref[s : s + 1, :] = colsum(du.astype(F32))
        term = nt(du, wud[s, :, 0:768])
        if s == 0:
            g1_ref[...] = term
        else:
            g1_ref[...] += term
    da2 = g1_ref[...]
    centered, inverse = stats(h1_ref[...])
    gain = vec_ref[0, 2:3, :]
    a2_ref[...] = (centered * gain + vec_ref[0, 3:4, :]).astype(BF16)
    small_ref[6:7, :] = colsum(da2 * centered)
    small_ref[7:8, :] = colsum(da2)
    grad = grad + norm_back(da2, gain, centered, inverse)
    g1_ref[...] = grad
    go = grad.astype(BF16)
    go_ref[...] = go
    small_ref[5:6, :] = colsum(go.astype(F32))
    for s, ref in enumerate((d0, d1, d2, d3)):
        waits[s][0].wait()
        ref[...] = nn(go, wout[s]).astype(BF16)


def mlp_bwd(layer, sc, grad, back, h1, up, vecs, packs, prompt, deps=()):
    tok = grad.shape[0]
    first = back is None
    others = 0 if first else len(back[3])
    small = jax.ShapeDtypeStruct((tok, D), BF16)
    shapes = [
        small,
        jax.ShapeDtypeStruct((4, tok, D), BF16),
        small,
        jax.ShapeDtypeStruct((tok, D), F32),
        small,
    ]
    shapes += [jax.ShapeDtypeStruct((tok, 256), BF16)] * 4
    shapes += [jax.ShapeDtypeStruct((16, D), F32)]
    extra = [] if first else [back[0], back[1], back[2], *back[3]]
    specs = vec_specs(layer)
    ins = [grad, *extra, h1, up, vecs, vecs, *[w for pair in packs for w in pair]]
    kernel = functools.partial(mlp_bwd_kernel, len(packs), others // 2, first, prompt)
    return pl.pallas_call(
        strip(kernel, layer, len(ins), len(deps)),
        grid_spec=pltpu.PrefetchScalarGridSpec(
            num_scalar_prefetch=1,
            grid=(1,),
            in_specs=[whole_spec(v.shape) for v in [grad, *extra, h1]]
            + [HBM, specs[0], specs[2]]
            + [ANY] * (2 * len(packs) + len(deps)),
            out_specs=[whole_spec(s.shape) for s in shapes],
            scratch_shapes=WSCR + [pltpu.VMEM((4, tok, D), BF16), pltpu.SemaphoreType.DMA((4,))],
        ),
        out_shape=shapes,
        compiler_params=params(48),
        cost_estimate=cost(2 * tok * D * 6912, 16e6, tok * 3072),
        name="mlp_bwd",
    )(sc, *ins, *deps)


def attn_fwd_kernel(dims, sc, *refs):
    rows, piece, cpiece, chunk, cont = dims
    npc = 4 * rows
    own, oth = refs[:4], refs[4:npc]
    w_ref, b_ref, prow, pcol, crow, ccol, srow, scol = refs[npc : npc + 8]
    outs = refs[npc + 8 :]
    o_refs = outs[:4]
    q_ref, kv_ref, lse_ref, lsec_ref, m_s, l_s, acc_s = outs[4:]
    head = pl.program_id(0)
    base_b = chunk * rows
    base_c = 2 * chunk * rows
    weight = w_ref[0]
    bias = b_ref[0]
    for s in range(4):
        mixed = nn(own[s][...], weight) + bias
        low_q = (mixed[:, 0:128].astype(BF16).astype(F32) * 0.125).astype(BF16)
        low_kv = mixed[:, 128:256].astype(BF16)
        q_ref[0, s * piece : (s + 1) * piece, :] = low_q[0:piece]
        q_ref[0, chunk + s * piece : chunk + (s + 1) * piece, :] = low_q[piece : 2 * piece]
        q_ref[0, 2 * chunk + s * cpiece : 2 * chunk + (s + 1) * cpiece, :] = low_q[2 * piece :]
        kv_ref[0, s * piece : (s + 1) * piece, :] = low_kv[0:piece]
        kv_ref[0, base_b + s * piece : base_b + (s + 1) * piece, :] = low_kv[piece : 2 * piece]
        kv_ref[0, base_c + s * cpiece : base_c + (s + 1) * cpiece, :] = low_kv[2 * piece :]
    for t in range(1, rows):
        for s in range(4):
            low_kv = (nn(oth[(t - 1) * 4 + s][...], weight[:, 128:256]) + bias[:, 128:256]).astype(BF16)
            at = t * chunk + s * piece
            kv_ref[0, at : at + piece, :] = low_kv[0:piece]
            kv_ref[0, base_b + at : base_b + at + piece, :] = low_kv[piece : 2 * piece]
    lanes = lax.broadcasted_iota(jnp.int32, (1, 128), 1)
    upper = lanes >= 64
    sub = min(128, chunk)

    def begin(query, keys, mask):
        scores = nt(query, keys)
        if mask is not None:
            size = mask.shape[1]
            tail = jnp.where(mask, scores[:, -size:], MASK_FILL)
            if size == scores.shape[1]:
                scores = tail
            else:
                scores = jnp.concatenate([scores[:, :-size], tail], axis=1)
        top = jnp.max(scores, axis=1, keepdims=True)
        prob = jnp.exp(scores - top)
        return top, jnp.sum(prob, axis=1, keepdims=True), nn(prob.astype(BF16), keys)

    def put(out, row, size):
        low = jnp.where(upper, out, 0.0)

        def first_head():
            value = pltpu.roll(low, 64, 1).astype(BF16)
            store(value, row, size, 0, False)

        def second_head():
            store(low.astype(BF16), row, size, 0, True)

        def third_head():
            store(pltpu.roll(low, 64, 1).astype(BF16), row, size, 1, False)

        pl.when(head == 0)(first_head)
        pl.when(head == 1)(second_head)
        pl.when(head == 2)(third_head)

    def store(value, row, size, half, add):
        s, at = row
        lo = half * 128
        if add:
            o_refs[s][at : at + size, lo : lo + 128] = (
                o_refs[s][at : at + size, lo : lo + 128] + value
            )
        else:
            o_refs[s][at : at + size, lo : lo + 128] = value

    for i in range(chunk // sub):
        at = i * sub
        mask = prow[0:1, :] <= pcol[at : at + sub, :]
        top, total, acc = begin(q_ref[0, at : at + sub, :], kv_ref[0, 0:chunk, :], mask)
        m_s[at : at + sub, :], l_s[at : at + sub, :], acc_s[at : at + sub, :] = top, total, acc
        at_b = chunk + at
        top, total, acc = begin(
            q_ref[0, at_b : at_b + sub, :], kv_ref[0, 0 : base_b + chunk, :], mask
        )
        m_s[at_b : at_b + sub, :], l_s[at_b : at_b + sub, :] = top, total
        acc_s[at_b : at_b + sub, :] = acc
    my_row = sc[5]
    for t in range(1, rows):
        before = lax.rem(my_row + t, rows) < my_row
        q_at = jnp.where(before, 0, chunk)
        k_at = jnp.where(before, t * chunk, base_b + t * chunk)
        keys = kv_ref[0, pl.ds(pl.multiple_of(k_at, 128), chunk), :]
        for i in range(chunk // sub):
            at = pl.ds(pl.multiple_of(q_at + i * sub, 128), sub)
            scores = nt(q_ref[0, at, :], keys)
            old = m_s[at, :]
            top = jnp.maximum(old, jnp.max(scores, axis=1, keepdims=True))
            scale = jnp.exp(old - top)
            prob = jnp.exp(scores - top)
            m_s[at, :] = top
            l_s[at, :] = l_s[at, :] * scale + jnp.sum(prob, axis=1, keepdims=True)
            acc_s[at, :] = acc_s[at, :] * scale + nn(prob.astype(BF16), keys)
    for half in range(2):
        for s in range(4):
            at = half * chunk + s * piece
            total = l_s[at : at + piece, :]
            put(acc_s[at : at + piece, :] / total, (s, half * piece), piece)
        for i in range(chunk // sub):
            at = half * chunk + i * sub
            column = m_s[at : at + sub, :] + jnp.log(l_s[at : at + sub, :])
            lse_ref[0, half, :, i * sub : (i + 1) * sub] = to_row(column)
    mask = (crow[0:1, :] <= ccol[...]) & (srow[0:1, :] == scol[...])
    query = q_ref[0, 2 * chunk : 2 * chunk + cont, :]
    top, total, acc = begin(query, kv_ref[0], mask)
    out = acc / total
    for s in range(4):
        put(out[s * cpiece : (s + 1) * cpiece], (s, 2 * piece), cpiece)
    lsec_ref[0] = to_row(top + jnp.log(total))


def attn_inputs(pos):
    return [pl.BlockSpec(v.shape, lambda i, sc: (0, 0)) for v in pos]


def attn_fwd(layer, sc, own, oth, w_all, b_all, pos, dims, deps=()):
    rows, piece, cpiece, chunk, cont = dims
    tok = own[0].shape[0]
    nq, nk = 2 * chunk + cont, 2 * chunk * rows + cont
    shapes = [jax.ShapeDtypeStruct((tok, 256), BF16)] * 4 + [
        jax.ShapeDtypeStruct((3, nq, 128), BF16),
        jax.ShapeDtypeStruct((3, nk, 128), BF16),
        jax.ShapeDtypeStruct((3, 2, 1, chunk), F32),
        jax.ShapeDtypeStruct((3, 1, cont), F32),
    ]
    out_specs = [whole_spec((tok, 256))] * 4 + [
        pl.BlockSpec((1, nq, 128), lambda i, sc: (i, 0, 0)),
        pl.BlockSpec((1, nk, 128), lambda i, sc: (i, 0, 0)),
        pl.BlockSpec((1, 2, 1, chunk), lambda i, sc: (i, 0, 0, 0)),
        pl.BlockSpec((1, 1, cont), lambda i, sc: (i, 0, 0)),
    ]
    at = layer * 8
    count = len(own) + len(oth) + 2 + len(pos)
    return pl.pallas_call(
        strip(functools.partial(attn_fwd_kernel, dims), layer, count, len(deps)),
        grid_spec=pltpu.PrefetchScalarGridSpec(
            num_scalar_prefetch=1,
            grid=(3,),
            in_specs=[whole_spec(v.shape) for v in [*own, *oth]]
            + [
                pl.BlockSpec((1, D, 256), lambda i, sc: (sc[at], 0, i)),
                pl.BlockSpec((1, 1, 256), lambda i, sc: (sc[at], 0, i)),
            ]
            + attn_inputs(pos)
            + [ANY] * len(deps),
            out_specs=out_specs,
            scratch_shapes=[
                pltpu.VMEM((2 * chunk, 1), F32),
                pltpu.VMEM((2 * chunk, 1), F32),
                pltpu.VMEM((2 * chunk, 128), F32),
            ],
        ),
        out_shape=shapes,
        compiler_params=params(52),
        cost_estimate=cost(2 * nq * D * 768 * 2 + 8 * 3 * nq * nk * 64, 12e6, 3 * nq * nk),
        name="attn_fwd",
    )(sc, *own, *oth, w_all, b_all, *pos, *deps)


def attn_bwd_kernel(dims, sc, *refs):
    rows, piece, cpiece, chunk, cont = dims
    do_refs, o_refs = refs[:4], refs[4:8]
    q_ref, kv_ref, lse_ref, lsec_ref, w_ref = refs[8:13]
    prow, pcol, crow, ccol, srow, scol = refs[13:19]
    outs = refs[19:]
    npc = 4 * rows
    own_out, oth_out = outs[:4], outs[4:npc]
    dq_out, dkv_out, bias_out = outs[npc : npc + 3]
    do_s, drow, drowc, dq_s, dkv_s, da_s = outs[npc + 3 :]
    head = pl.program_id(0)
    base_b = chunk * rows
    base_c = 2 * chunk * rows
    tok = 2 * piece + cpiece
    upper = lax.broadcasted_iota(jnp.int32, (1, 128), 1) >= 64

    def take(ref):
        value = ref[...].astype(F32)
        left, right = value[:, 0:128], value[:, 128:256]
        pick = jnp.where(head == 2, pltpu.roll(right, 64, 1), left)
        pick = jnp.where(head == 0, pltpu.roll(left, 64, 1), pick)
        return jnp.where(upper, pick, 0.0)

    for s in range(4):
        dout = take(do_refs[s])
        low = dout.astype(BF16)
        do_s[s * piece : (s + 1) * piece, :] = low[0:piece]
        do_s[chunk + s * piece : chunk + (s + 1) * piece, :] = low[piece : 2 * piece]
        do_s[2 * chunk + s * cpiece : 2 * chunk + (s + 1) * cpiece, :] = low[2 * piece :]
        dot = dout * take(o_refs[s])
        dq_s[s * piece : (s + 1) * piece, :] = dot[0:piece]
        dq_s[chunk + s * piece : chunk + (s + 1) * piece, :] = dot[piece : 2 * piece]
        dq_s[2 * chunk + s * cpiece : 2 * chunk + (s + 1) * cpiece, :] = dot[2 * piece :]
    sub = min(128, chunk)
    for half in range(2):
        for i in range(chunk // sub):
            at = half * chunk + i * sub
            column = jnp.sum(dq_s[at : at + sub, :], axis=1, keepdims=True)
            drow[half, :, i * sub : (i + 1) * sub] = to_row(column)
    column = jnp.sum(dq_s[2 * chunk :, :], axis=1, keepdims=True)
    drowc[...] = to_row(column)
    dq_s[...] = jnp.zeros_like(dq_s)
    dkv_s[...] = jnp.zeros_like(dkv_s)

    def pair(q_at, k_at, lse, dot, mask):
        query = q_ref[0, q_at, :]
        keys = kv_ref[0, k_at, :]
        dout = do_s[q_at, :]
        prob = jnp.exp(nt(keys, query) - lse)
        if mask is not None:
            prob = jnp.where(mask, prob, 0.0)
        dprob = nt(keys, dout)
        dscore = (prob * (dprob - dot)).astype(BF16)
        dkv_s[k_at, :] += nn(prob.astype(BF16), dout) + nn(dscore, query)
        dq_s[q_at, :] += tn(dscore, keys)

    kb = min(256, chunk)
    at_a, at_b = pl.ds(0, chunk), pl.ds(chunk, chunk)
    lse_a, lse_b, dot_a, dot_b = lse_ref[0, 0], lse_ref[0, 1], drow[0], drow[1]
    for j in range(chunk // kb):
        mask = pcol[j * kb : (j + 1) * kb, :] <= prow[0:1, :]
        pair(at_a, pl.ds(j * kb, kb), lse_a, dot_a, mask)
        pair(at_b, pl.ds(base_b + j * kb, kb), lse_b, dot_b, mask)
    for j in range(base_b // kb):
        pair(at_b, pl.ds(j * kb, kb), lse_b, dot_b, None)
    my_row = sc[5]
    for t in range(1, rows):
        before = lax.rem(my_row + t, rows) < my_row
        which = jnp.where(before, 0, 1)
        q_at = pl.ds(pl.multiple_of(which * chunk, 128), chunk)
        k_base = jnp.where(before, t * chunk, base_b + t * chunk)
        for j in range(chunk // kb):
            k_at = pl.ds(pl.multiple_of(k_base + j * kb, 128), kb)
            pair(q_at, k_at, lse_ref[0, which], drow[which], None)
    at_c = pl.ds(2 * chunk, cont)
    for j in range(base_c // 512):
        pair(at_c, pl.ds(j * 512, 512), lsec_ref[0], drowc[...], None)
    mask = (ccol[...] <= crow[0:1, :]) & (scol[...] == srow[0:1, :])
    pair(at_c, pl.ds(base_c, cont), lsec_ref[0], drowc[...], mask)

    weight = w_ref[0]
    lower = jnp.logical_not(upper)
    dq_all = jnp.where(lower, dq_s[...] * 0.125, 0.0).astype(BF16)
    q_sum = colsum(dq_all.astype(F32))
    kv_sum = jnp.zeros((1, 128), F32)

    def gather3(value, where):
        return jnp.concatenate([value[a : a + n] for a, n in where], axis=0)

    def emit(slot, count, ref, term):
        at = pl.ds(slot, count)

        def set_first():
            da_s[at, :] = term

        def add_next():
            da_s[at, :] += term

        def finish():
            ref[...] = (da_s[at, :] + term).astype(BF16)

        pl.when(head == 0)(set_first)
        pl.when(head == 1)(add_next)
        pl.when(head == 2)(finish)

    for s in range(4):
        dq = gather3(
            dq_all,
            [(s * piece, piece), (chunk + s * piece, piece), (2 * chunk + s * cpiece, cpiece)],
        )
        dkv = jnp.concatenate(
            [
                dkv_s[s * piece : (s + 1) * piece, :],
                dkv_s[base_b + s * piece : base_b + (s + 1) * piece, :],
                dkv_s[base_c + s * cpiece : base_c + (s + 1) * cpiece, :],
            ],
            axis=0,
        ).astype(BF16)
        kv_sum = kv_sum + colsum(dkv.astype(F32))
        both = jnp.concatenate([dq, dkv], axis=1)
        dq_out[s, 0] = both
        emit(s * tok, tok, own_out[s], nt(both, weight))
    for t in range(1, rows):
        for s in range(4):
            at = t * chunk + s * piece
            dkv = jnp.concatenate(
                [dkv_s[at : at + piece, :], dkv_s[base_b + at : base_b + at + piece, :]], axis=0
            ).astype(BF16)
            kv_sum = kv_sum + colsum(dkv.astype(F32))
            k = (t - 1) * 4 + s
            dkv_out[k, 0] = dkv
            emit(4 * tok + k * 2 * piece, 2 * piece, oth_out[k], nt(dkv, weight[:, 128:256]))
    bias_out[0] = jnp.broadcast_to(jnp.concatenate([q_sum, kv_sum], axis=1), (8, 256))


def attn_bwd(layer, sc, do_parts, o_parts, q, kv, lse, lsec, w_all, pos, dims, deps=()):
    rows, piece, cpiece, chunk, cont = dims
    tok = 2 * piece + cpiece
    nq, nk = 2 * chunk + cont, 2 * chunk * rows + cont
    noth = 4 * (rows - 1)
    shapes = (
        [jax.ShapeDtypeStruct((tok, D), BF16)] * 4
        + [jax.ShapeDtypeStruct((2 * piece, D), BF16)] * noth
        + [
            jax.ShapeDtypeStruct((4, 3, tok, 256), BF16),
            jax.ShapeDtypeStruct((noth, 3, 2 * piece, 128), BF16),
            jax.ShapeDtypeStruct((3, 8, 256), F32),
        ]
    )
    out_specs = [whole_spec(s.shape) for s in shapes[: 4 + noth]] + [
        pl.BlockSpec((4, 1, tok, 256), lambda i, sc: (0, i, 0, 0)),
        pl.BlockSpec((noth, 1, 2 * piece, 128), lambda i, sc: (0, i, 0, 0)),
        pl.BlockSpec((1, 8, 256), lambda i, sc: (i, 0, 0)),
    ]
    at = layer * 8
    return pl.pallas_call(
        strip(functools.partial(attn_bwd_kernel, dims), layer, 13 + len(pos), len(deps)),
        grid_spec=pltpu.PrefetchScalarGridSpec(
            num_scalar_prefetch=1,
            grid=(3,),
            in_specs=[whole_spec((tok, 256))] * 8
            + [
                pl.BlockSpec((1, nq, 128), lambda i, sc: (i, 0, 0)),
                pl.BlockSpec((1, nk, 128), lambda i, sc: (i, 0, 0)),
                pl.BlockSpec((1, 2, 1, chunk), lambda i, sc: (i, 0, 0, 0)),
                pl.BlockSpec((1, 1, cont), lambda i, sc: (i, 0, 0)),
                pl.BlockSpec((1, D, 256), lambda i, sc: (sc[at], 0, i)),
            ]
            + attn_inputs(pos)
            + [ANY] * len(deps),
            out_specs=out_specs,
            scratch_shapes=[
                pltpu.VMEM((nq, 128), BF16),
                pltpu.VMEM((2, 1, chunk), F32),
                pltpu.VMEM((1, cont), F32),
                pltpu.VMEM((nq, 128), F32),
                pltpu.VMEM((nk, 128), F32),
                pltpu.VMEM((4 * tok + noth * 2 * piece, D), F32),
            ],
        ),
        out_shape=shapes,
        compiler_params=params(56),
        cost_estimate=cost(2 * nq * D * 768 * 2 + 20 * 3 * nq * nk * 64, 14e6, 3 * nq * nk),
        name="attn_bwd",
    )(sc, *do_parts, *o_parts, q, kv, lse, lsec, w_all, *pos, *deps)


def dw_qkv_kernel(rows, sc, *refs):
    npc = 4 * rows
    noth = npc - 4
    srcs, (dq_hbm, dkv_hbm) = refs[:npc], refs[npc : npc + 2]
    new_ref, token = refs[npc + 2 : npc + 4]
    own, oth, dq_s, dkv_s, asem, dsem = refs[npc + 4 :]
    token[...] = jnp.zeros_like(token)
    head = pl.program_id(0)

    def rows_of(k):
        dst = own.at[k] if k < 4 else oth.at[k - 4]
        return pltpu.make_async_copy(srcs[k], dst, asem.at[k])

    def grads_of(h):
        return [
            pltpu.make_async_copy(dq_hbm.at[:, h], dq_s.at[:, h], dsem.at[0, h]),
            pltpu.make_async_copy(dkv_hbm.at[:, h], dkv_s.at[:, h], dsem.at[1, h]),
        ]

    def begin():
        for copy in grads_of(0):
            copy.start()
        for k in range(npc):
            rows_of(k).start()
        for h in (1, 2):
            for copy in grads_of(h):
                copy.start()
        for k in range(npc):
            rows_of(k).wait()

    pl.when(head == 0)(begin)
    for copy in grads_of(head):
        copy.wait()
    total = tn(own[0], dq_s[0, head])
    for s in range(1, 4):
        total = total + tn(own[s], dq_s[s, head])
    right = tn(oth[0], dkv_s[0, head])
    for k in range(1, noth):
        right = right + tn(oth[k], dkv_s[k, head])
    new_ref[:, 0:128] = total[:, 0:128].astype(BF16)
    new_ref[:, 128:256] = (total[:, 128:256] + right).astype(BF16)


def dw_qkv(layer, sc, own, oth, dq, dkv, deps=()):
    rows = (4 + len(oth)) // 4
    tok, two = own[0].shape[0], oth[0].shape[0]
    noth = len(oth)
    ins = [*own, *oth, dq, dkv]
    return pl.pallas_call(
        strip(functools.partial(dw_qkv_kernel, rows), layer, len(ins), len(deps)),
        grid_spec=pltpu.PrefetchScalarGridSpec(
            num_scalar_prefetch=1,
            grid=(3,),
            in_specs=[HBM] * len(ins) + [ANY] * len(deps),
            out_specs=[pl.BlockSpec((D, 256), lambda i, sc: (0, i)), whole_spec((8, 128))],
            scratch_shapes=[
                pltpu.VMEM((4, tok, D), BF16),
                pltpu.VMEM((noth, two, D), BF16),
                pltpu.VMEM((4, 3, tok, 256), BF16),
                pltpu.VMEM((noth, 3, two, 128), BF16),
                pltpu.SemaphoreType.DMA((4 * rows,)),
                pltpu.SemaphoreType.DMA((2, 3)),
            ],
        ),
        out_shape=[
            jax.ShapeDtypeStruct((D, D), BF16),
            jax.ShapeDtypeStruct((8, 128), F32),
        ],
        compiler_params=params(40),
        cost_estimate=cost(2 * 3 * D * (4 * tok * 256 + noth * two * 128), 10e6),
        name="dw_qkv",
    )(sc, *ins, *deps)


def dw_terms(refs, scratch, act, sems, tile, first):
    a2_h, gm_h, go_h, du_ref, act_h, o0, o1, o2, o3 = refs
    a2, gm, go = scratch

    def load(k, src, dst):
        return pltpu.make_async_copy(src, dst, sems.at[k])

    loads = [load(0, a2_h, a2), load(1, gm_h, gm), load(2, go_h, go)]

    def tile_load(s):
        return load(3 + s, act_h.at[s], act.at[s])

    def begin():
        for copy in loads:
            copy.start()
        for s in range(4):
            tile_load(s).start()
        for copy in loads:
            copy.wait()

    pl.when(first)(begin)
    pl.when(tile == 0)(lambda: tile_load(0).wait())
    for s in range(1, 4):
        pl.when(tile == s)(lambda s=s: tile_load(s).wait())

    def run(put):
        for j in range(3):
            put(j * 256, tn(a2[...], du_ref[0, :, j * 256 : (j + 1) * 256]))
            put(768 + j * 256, tn(gm[...], act[tile, :, j * 256 : (j + 1) * 256]))
        for s, ref in enumerate((o0, o1, o2, o3)):
            pl.when(tile == s)(lambda ref=ref: put(1536, tn(go[...], ref[...])))

    return run


def dw_mlp_kernel(sc, *refs):
    old_ref, new_ref, token = refs[9:12]
    a2, gm, go, act, sems = refs[12:]
    token[...] = jnp.zeros_like(token)
    tile = pl.program_id(0)
    keep = sc[6] == 0
    run = dw_terms(refs[:9], (a2, gm, go), act, sems, tile, tile == 0)

    def put(lo, value):
        size = value.shape[1]
        old = old_ref[0, 0, :, lo : lo + size].astype(F32)
        new_ref[0, 0, :, lo : lo + size] = (value + jnp.where(keep, old, 0.0)).astype(BF16)

    run(put)


def dw_specs(tok):
    return (
        [HBM] * 3
        + [pl.BlockSpec((1, tok, D), lambda i, sc: (i, 0, 0)), HBM]
        + [whole_spec((tok, 256))] * 4
    )


def dw_scratch(tok):
    return [pltpu.VMEM((tok, D), BF16)] * 3 + [
        pltpu.VMEM((4, tok, D), BF16),
        pltpu.SemaphoreType.DMA((7,)),
    ]


def dw_mlp(layer, sc, a2, gm, go, du, act, o_parts, acc, deps=()):
    tok = a2.shape[0]
    at = layer * 8
    acc_spec = pl.BlockSpec((1, 1, D, PACK), lambda i, sc: (sc[at + 1], i, 0, 0))
    ins = [a2, gm, go, du, act, *o_parts, acc]
    return pl.pallas_call(
        strip(dw_mlp_kernel, layer, len(ins), len(deps)),
        grid_spec=pltpu.PrefetchScalarGridSpec(
            num_scalar_prefetch=1,
            grid=(4,),
            in_specs=dw_specs(tok) + [acc_spec] + [ANY] * len(deps),
            out_specs=[acc_spec, whole_spec((8, 128))],
            scratch_shapes=dw_scratch(tok),
        ),
        out_shape=[jax.ShapeDtypeStruct(acc.shape, acc.dtype), jax.ShapeDtypeStruct((8, 128), F32)],
        input_output_aliases={len(ins): 0},
        compiler_params=params(40),
        cost_estimate=cost(2 * tok * D * 4 * PACK, 30e6),
        name="dw_mlp",
    )(sc, *ins, *deps)


def dw_last_kernel(rank, sc, *refs):
    send_ref, keep_ref, acc, token = refs[10:14]
    a2, gm, go, act, sems, done, other, dsem, osem = refs[14:]
    token[...] = jnp.zeros_like(token)
    step = pl.program_id(0)
    tile = last_tile(step)
    same = sc[1] == rank
    keep = sc[6] == 0
    used = jnp.logical_or(jnp.logical_not(same), keep)

    def load(i):
        return pltpu.make_async_copy(acc.at[rank, last_tile(i)], done.at[i % 2], dsem.at[i % 2])

    def start_two():
        load(0).start()
        load(1).start()

    pl.when(step == 0)(start_two)
    run = dw_terms(refs[:9], (a2, gm, go), act, sems, tile, step == 0)
    load(step).wait()

    def fetch_other():
        copy = pltpu.make_async_copy(acc.at[sc[1], tile], other, osem)
        copy.start()
        copy.wait()

    pl.when(jnp.logical_not(same))(fetch_other)

    def put(lo, value):
        size = value.shape[1]
        cols = slice(lo, lo + size)
        old = jnp.where(used, done[step % 2, :, cols].astype(F32), 0.0)
        total = (old + jnp.where(same, value, 0.0)).astype(BF16)

        def to_send():
            send_ref[0, :, cols] = total

        def to_keep():
            keep_ref[0, :, cols] = total

        pl.when(step < 2)(to_send)
        pl.when(step >= 2)(to_keep)

        def add_other():
            before = jnp.where(keep, other[:, cols].astype(F32), 0.0)
            other[:, cols] = (value + before).astype(BF16)

        pl.when(jnp.logical_not(same))(add_other)

    run(put)

    def store_other():
        copy = pltpu.make_async_copy(other, acc.at[sc[1], tile], osem)
        copy.start()
        copy.wait()

    pl.when(jnp.logical_not(same))(store_other)
    pl.when(step < 2)(lambda: load(step + 2).start())


def last_tile(step):
    return jnp.where(step < 2, 2 * step + 1, 2 * step - 4)


def dw_last(layer, sc, a2, gm, go, du, act, o_parts, acc, deps=()):
    tok = a2.shape[0]
    ins = [a2, gm, go, du, act, *o_parts, acc]
    specs = dw_specs(tok)
    specs[3] = pl.BlockSpec((1, tok, D), lambda i, sc: (last_tile(i), 0, 0))
    two = jax.ShapeDtypeStruct((2, D, PACK), BF16)
    return pl.pallas_call(
        strip(functools.partial(dw_last_kernel, layer), layer, len(ins), len(deps)),
        grid_spec=pltpu.PrefetchScalarGridSpec(
            num_scalar_prefetch=1,
            grid=(4,),
            in_specs=specs + [HBM] + [ANY] * len(deps),
            out_specs=[
                pl.BlockSpec((1, D, PACK), lambda i, sc: (jnp.minimum(i, 1), 0, 0)),
                pl.BlockSpec((1, D, PACK), lambda i, sc: (jnp.maximum(i - 2, 0), 0, 0)),
                HBM,
                whole_spec((8, 128)),
            ],
            scratch_shapes=dw_scratch(tok)
            + [
                pltpu.VMEM((2, D, PACK), BF16),
                pltpu.VMEM((D, PACK), BF16),
                pltpu.SemaphoreType.DMA((2,)),
                pltpu.SemaphoreType.DMA(()),
            ],
        ),
        out_shape=[two, two, jax.ShapeDtypeStruct(acc.shape, acc.dtype), jax.ShapeDtypeStruct((8, 128), F32)],
        input_output_aliases={len(ins): 2},
        compiler_params=params(52),
        cost_estimate=cost(2 * tok * D * 4 * PACK, 30e6),
        name="dw_last",
    )(sc, *ins, *deps)


def blank(shape, dtype):
    def body(out):
        del out

    return pl.pallas_call(
        body,
        out_shape=jax.ShapeDtypeStruct(shape, dtype),
        out_specs=pl.BlockSpec(memory_space=pl.ANY),
        name="blank",
    )()


SWAP = [(0, 1), (1, 0)]


def swap_core(value):
    return lax.ppermute(value, "core", SWAP)


def swap_x(value):
    return lax.ppermute(value, "x", SWAP)


def shift_row(value, t):
    rows = lax.axis_size("row")
    return lax.ppermute(value, "row", [(i, (i - t) % rows) for i in range(rows)])


def shift_row_x(value, t):
    rows = lax.axis_size("row")
    pairs = [(i * 2 + j, ((i - t) % rows) * 2 + (1 - j)) for i in range(rows) for j in range(2)]
    return lax.ppermute(value, ("row", "x"), pairs)


def spread(low, low_prompt):
    rows = lax.axis_size("row")
    from_x = swap_x(low)
    far = []
    for t in range(1, rows):
        far += [shift_row(low_prompt, t), shift_row_x(low_prompt, t)]
    own = [low, swap_core(low), from_x, swap_core(from_x)]
    oth = []
    for t in range(1, rows):
        near, diag = far[2 * t - 2], far[2 * t - 1]
        oth += [near, swap_core(near), diag, swap_core(diag)]
    return own, oth


def exchange_heads(parts):
    flip = {1: [1, 0, 3, 2], 2: [2, 3, 0, 1], 3: [3, 2, 1, 0]}
    out = [parts[0]]
    for s in (1, 2, 3):
        pairs = [(c, flip[s][c]) for c in range(4)]
        out.append(lax.ppermute(parts[s], ("x", "core"), pairs))
    return out


def add_low(a, b):
    return (a.astype(F32) + b.astype(F32)).astype(BF16)


def add_kernel(refs_in, refs_out):
    for k, out in enumerate(refs_out):
        out[...] = add_low(refs_in[2 * k][...], refs_in[2 * k + 1][...])


def add_pairs(pairs):
    flat = [v for pair in pairs for v in pair]
    count = len(flat)
    return pl.pallas_call(
        lambda *refs: add_kernel(refs[:count], refs[count:]),
        out_shape=[jax.ShapeDtypeStruct(a.shape, a.dtype) for a, _ in pairs],
        compiler_params=params(24),
        cost_estimate=cost(1e6, 4e6),
        name="add_pairs",
    )(*flat)


def collect(own, oth):
    rows = lax.axis_size("row")
    pieces = [*own, *oth]
    pairs = [(pieces[k], swap_core(pieces[k + 1])) for k in range(0, len(pieces), 2)]
    sums = add_pairs(pairs)
    got = swap_x(sums[1])
    rest = []
    for t in range(1, rows):
        rest += [shift_row(sums[2 * t], -t), shift_row_x(sums[2 * t + 1], -t)]
    return sums[0], got, rest


def pick_kernel(sc_at, sc, src, *rest):
    out, sem = rest[-2:]
    copy = pltpu.make_async_copy(src.at[sc[sc_at]], out, sem)
    copy.start()
    copy.wait()


def pick(src, sc, at, deps=()):
    return pl.pallas_call(
        functools.partial(pick_kernel, at),
        grid_spec=pltpu.PrefetchScalarGridSpec(
            num_scalar_prefetch=1,
            grid=(1,),
            in_specs=[ANY] * (1 + len(deps)),
            out_specs=ANY,
            scratch_shapes=[pltpu.SemaphoreType.DMA(())],
        ),
        out_shape=jax.ShapeDtypeStruct(src.shape[1:], src.dtype),
        name="pick",
    )(sc, src, *deps)


def zig(j, rows):
    return j if j < rows else 2 * rows - 1 - j


def split_kernel(piece, cpiece, sc, even, odd, cont, *outs):
    for s, out in enumerate(outs):
        place = sc[3] ^ s
        at = pl.ds(pl.multiple_of(place * piece, piece), piece)

        def fill(first, second, out=out, at=at):
            out[0:piece, :] = first[at, :]
            out[piece : 2 * piece, :] = second[at, :]

        pl.when(sc[7] == 0)(functools.partial(fill, even, odd))
        pl.when(sc[7] == 1)(functools.partial(fill, odd, even))
        out[2 * piece :, :] = cont[pl.ds(pl.multiple_of(place * cpiece, cpiece), cpiece), :]


def merge_kernel(piece, cpiece, sc, p0, p1, p2, p3, even, odd, cont):
    for s, part in enumerate((p0, p1, p2, p3)):
        place = sc[3] ^ s
        at = pl.ds(pl.multiple_of(place * piece, piece), piece)

        def fill(first, second, part=part, at=at):
            first[at, :] = part[0:piece, :]
            second[at, :] = part[piece : 2 * piece, :]

        pl.when(sc[7] == 0)(functools.partial(fill, even, odd))
        pl.when(sc[7] == 1)(functools.partial(fill, odd, even))
        cont[pl.ds(pl.multiple_of(place * cpiece, cpiece), cpiece), :] = part[2 * piece :, :]


def join_kernel(prompt, normed, sc, p0, p1, p2, p3, vec_ref, h_ref, *outs):
    width = p0.shape[1]
    for s, part in enumerate((p0, p1, p2, p3)):
        value = part[...].astype(F32)
        for c in range(4):

            def put(value=value, c=c):
                h_ref[:, c * width : (c + 1) * width] = value

            pl.when((sc[3] ^ s) == c)(put)
    if normed:
        a_ref, ap_ref = outs
        centered, _ = stats(h_ref[...])
        low = (centered * vec_ref[0, 4:5, :] + vec_ref[0, 5:6, :]).astype(BF16)
        a_ref[...] = low
        ap_ref[...] = low[:prompt]


def simple_call(kernel, sc, ins, shapes, specs=None, name="small"):
    return pl.pallas_call(
        lambda sc_ref, *refs: kernel(Row(sc_ref, 0), *refs),
        grid_spec=pltpu.PrefetchScalarGridSpec(
            num_scalar_prefetch=1,
            grid=(1,),
            in_specs=specs or [whole_spec(v.shape) for v in ins],
            out_specs=[whole_spec(v.shape) for v in shapes],
        ),
        out_shape=shapes,
        compiler_params=params(24),
        cost_estimate=cost(1e6, 3e6),
        name=name,
    )(sc, *ins)


def enter(prompt, cont, sc, vecs, normed):
    rows = lax.axis_size("row")
    half, width = prompt.shape[0] // 2, prompt.shape[1]
    piece, cpiece = half // 4, cont.shape[0] // 4
    tok = 2 * piece + cpiece
    even = prompt[:half]
    odd = prompt[half:]
    if rows > 2:
        even = lax.ppermute(even, "row", [(i, zig(2 * i, rows)) for i in range(rows)])
    odd = lax.ppermute(odd, "row", [(i, zig(2 * i + 1, rows)) for i in range(rows)])
    part = jax.ShapeDtypeStruct((tok, width), BF16)
    parts = simple_call(
        functools.partial(split_kernel, piece, cpiece), sc, [even, odd, cont], [part] * 4, name="split"
    )
    parts = exchange_heads(parts)
    shapes = [jax.ShapeDtypeStruct((tok, D), F32)]
    if normed:
        shapes += [jax.ShapeDtypeStruct((tok, D), BF16), jax.ShapeDtypeStruct((2 * piece, D), BF16)]
    specs = [whole_spec((tok, width))] * 4 + [pl.BlockSpec((1, 8, D), lambda i, sc: (sc[0], 0, 0))]
    return simple_call(
        functools.partial(join_kernel, 2 * piece, normed), sc, [*parts, vecs], shapes, specs, "join"
    )


def leave(parts, sc, prompt_rows):
    rows = lax.axis_size("row")
    parts = exchange_heads(parts)
    width = parts[0].shape[1]
    half = prompt_rows // 2
    piece = half // 4
    cpiece = parts[0].shape[0] - 2 * piece
    shapes = [jax.ShapeDtypeStruct((n, width), BF16) for n in (half, half, 4 * cpiece)]
    even, odd, cont = simple_call(
        functools.partial(merge_kernel, piece, cpiece), sc, parts, shapes, name="merge"
    )
    if rows > 2:
        even = lax.ppermute(even, "row", [(zig(2 * i, rows), i) for i in range(rows)])
    odd = lax.ppermute(odd, "row", [(zig(2 * i + 1, rows), i) for i in range(rows)])
    return jnp.concatenate([even, odd], axis=0)[None], cont[None]


def final_kernel(prompt, others, sc, *refs):
    g_ref, h_ref, p0_ref, rx_ref = refs[:4]
    rest = refs[4 : 4 + others]
    vec_ref = refs[4 + others]
    outs, small, da_ref, out_ref = refs[5 + others : 9 + others], refs[9 + others], refs[10 + others], refs[11 + others]
    da_ref[...] = p0_ref[...].astype(F32) + rx_ref[...].astype(F32)
    for ref in rest:
        da_ref[0:prompt, :] += ref[...].astype(F32)
    da1 = da_ref[...]
    centered, inverse = stats(h_ref[...])
    small[0:1, :] = colsum(da1 * centered)
    small[1:2, :] = colsum(da1)
    out_ref[...] = g_ref[...] + norm_back(da1, vec_ref[0, 4:5, :], centered, inverse)
    send_features(sc, out_ref, outs)


def final_norm(sc, grad, back, vecs, prompt, width):
    tok = grad.shape[0]
    h_in, base, got, rest = back
    ins = [grad, h_in, base, got, *rest, vecs]
    shapes = [jax.ShapeDtypeStruct((tok, width), BF16)] * 4 + [
        jax.ShapeDtypeStruct((8, D), F32),
        jax.ShapeDtypeStruct((tok, D), F32),
        jax.ShapeDtypeStruct((tok, D), F32),
    ]
    specs = [whole_spec(v.shape) for v in ins[:-1]] + [
        pl.BlockSpec((1, 8, D), lambda i, sc: (sc[0], 0, 0))
    ]
    return simple_call(
        functools.partial(final_kernel, prompt, len(rest)), sc, ins, shapes, specs, "final_norm"
    )


class Reduce:

    def __init__(self, value, plan, out):
        self.value, self.plan, self.out = value, list(plan), out
        self.pending = None
        self.send()

    def halves(self, axis, bit):
        where = {"dp": 0, "row": 1}[axis]
        size = self.value.shape[where]
        step = size // 2
        shape = self.value.shape
        split = self.value.reshape(shape[:where] + (2, step) + shape[where + 1 :])
        mine = (lax.axis_index(axis) // bit) % 2
        take = functools.partial(lax.dynamic_index_in_dim, split, axis=where, keepdims=False)
        return take(mine), take(1 - mine)

    def send(self):
        if not self.plan:
            return
        axis, bit = self.plan.pop(0)
        count = lax.axis_size(axis)
        keep, send = self.halves(axis, bit)
        got = lax.ppermute(send, axis, [(i, i ^ bit) for i in range(count)])
        self.pending = (keep, got)

    def step(self):
        if self.pending is None:
            return self.value
        keep, got = self.pending
        self.pending = None
        total = keep.astype(F32) + got.astype(F32)
        self.value = total if not self.plan else total.astype(BF16)
        self.send()
        return self.value

    def finish(self):
        while self.pending is not None:
            self.step()
        return self.value[0, 0].astype(F32)


def bits_of(axis):
    count = lax.axis_size(axis)
    bits, bit = [], count // 2
    while bit:
        bits.append((axis, bit))
        bit //= 2
    return bits


def reorder(value):
    shape = value.shape
    value = value.reshape((2, 2) + shape[1:])
    value = jnp.where(lax.axis_index("core") == 1, value[:, ::-1], value)
    value = jnp.where(lax.axis_index("x") == 1, value[::-1], value)
    return value.reshape(shape)


def sum_small(value):
    rows, dps = lax.axis_size("row"), lax.axis_size("dp")
    x, core = lax.axis_index("x"), lax.axis_index("core")
    value = value.reshape(2, 2, -1)
    take = lax.dynamic_index_in_dim
    send = take(value, 1 - core, 1, keepdims=False)
    value = take(value, core, 1, keepdims=False) + swap_core(send)
    send = take(value, 1 - x, 0, keepdims=False)
    value = take(value, x, 0, keepdims=False) + swap_x(send)
    for axis, count in (("row", rows), ("dp", dps)):
        bit = 1
        while bit < count:
            value = value + lax.ppermute(value, axis, [(i, i ^ bit) for i in range(count)])
            bit *= 2
    return value


def per_device(
    x_prompt,
    x_cont,
    seg_ids,
    layer_map,
    w_qkv,
    bias_qv,
    w_out,
    b_out,
    w_up,
    b_up,
    w_down,
    b_down,
    ln1_gain,
    ln1_bias,
    ln2_gain,
    ln2_bias,
    cot_prompt,
    cot_cont,
):
    rows, dps = lax.axis_size("row"), lax.axis_size("dp")
    prompt_row, cont = x_prompt.shape[1], x_cont.shape[1]
    width = x_prompt.shape[2]
    chunk = prompt_row // 2
    piece, cpiece = chunk // 4, cont // 4
    prompt = 2 * piece
    dims = (rows, piece, cpiece, chunk, cont)
    my_row, my_x = lax.axis_index("row"), lax.axis_index("x")
    my_col = my_x * 2 + lax.axis_index("core")

    layer_map = layer_map.astype(jnp.int32)
    places = jnp.arange(LAYERS, dtype=jnp.int32)
    first_use = [jnp.min(jnp.where(layer_map == b, places, 99)) for b in range(NB)]
    rank_of = [sum((first_use[o] < first_use[b]).astype(jnp.int32) for o in range(NB) if o != b) for b in range(NB)]
    block_at = [sum(b * (rank_of[b] == k).astype(jnp.int32) for b in range(NB)) for k in range(NB)]
    block_of = [layer_map[i] for i in range(LAYERS)]
    rank_layer = [
        sum(rank_of[b] * (block_of[i] == b).astype(jnp.int32) for b in range(NB)) for i in range(LAYERS)
    ]

    def scalars(layer):
        fresh = jnp.int32(1)
        for later in range(layer + 1, LAYERS):
            fresh = fresh * (rank_layer[later] != rank_layer[layer]).astype(jnp.int32)
        after = min(layer + 1, LAYERS - 1)
        return [block_of[layer], rank_layer[layer], block_of[after], my_col, my_x, my_row, fresh, my_row % 2]

    sc = jnp.stack([v for i in range(LAYERS) for v in scalars(i)] + block_at).astype(jnp.int32)

    heads = w_qkv.reshape(NB, -1, 3, HEADS_COL, HD)
    zero = jnp.zeros_like(heads[:, :, 0])
    packed = jnp.stack([heads[:, :, 0], zero, heads[:, :, 1], heads[:, :, 2]], axis=3)
    packed = packed.reshape(NB, -1, D)
    wqkv_all = lax.all_gather(packed, ("dp", "row"), axis=1, tiled=True)
    pair = bias_qv.astype(F32).reshape(NB, 2, HEADS_COL, HD)
    none = jnp.zeros((NB, HEADS_COL, 2, HD), F32)
    bqkv = jnp.concatenate([pair[:, 0][:, :, None], none, pair[:, 1][:, :, None]], axis=2).reshape(NB, 1, D)

    def flat(value):
        return value.reshape(NB, -1)

    narrow = jnp.concatenate(
        [flat(v) for v in (b_out, b_down, ln2_gain, ln2_bias, ln1_gain, ln1_bias, b_up)], axis=1
    )
    narrow = jnp.stack(exchange_heads([narrow] * 4))
    narrow = reorder(narrow.astype(F32))
    vecs = narrow[:, :, : 6 * width].reshape(4, NB, 6, width).transpose(1, 2, 0, 3).reshape(NB, 6, D)
    vecs = jnp.concatenate([vecs, jnp.zeros((NB, 2, D), F32)], axis=1)
    bup = narrow[:, :, 6 * width :].transpose(1, 0, 2).reshape(NB, 4, 1, D)

    pack_local = jnp.concatenate(
        [w_up, w_down, w_out, jnp.zeros(w_out.shape[:2] + (64,), BF16)], axis=2
    )

    def gather_pack(k, deps):
        local = pick(pack_local, sc, LAYERS * 8 + k, deps)
        mine = lax.all_gather(local, ("x", "dp", "row"), axis=0, tiled=True).reshape(2, D, PACK)
        return mine, swap_core(mine)

    def places_of(size):
        index = jnp.arange(4 * size, dtype=jnp.int32)
        return size * ((index // size) ^ my_col) + index % size

    ppos, cpos = places_of(piece), places_of(cpiece)
    seg = reorder(seg_ids[0].astype(jnp.int32).reshape(4, cpiece)).reshape(cont)
    pos = [ppos[None], ppos[:, None], cpos[None], cpos[:, None], seg[None], seg[:, None]]

    hidden, low, low_prompt = enter(x_prompt[0], x_cont[0], sc, vecs, True)
    packs = [gather_pack(0, [wqkv_all])]
    saved = []
    for i in range(LAYERS):
        last = i == LAYERS - 1
        own, oth = spread(low, low_prompt)
        res = attn_fwd(i, sc, own, oth, wqkv_all, bqkv, pos, dims)
        o_send, (q, kv, lse, lsec) = res[:4], res[4:]
        if i + 1 < NB:
            packs.append(gather_pack(i + 1, [lsec]))
        o_got = exchange_heads(o_send)
        avail = packs[: min(i, NB - 1) + 1]
        res = mlp_fwd(i, sc, hidden, o_got, vecs, bup, avail, prompt, last, width)
        saved.append((hidden, own, oth, o_send, q, kv, lse, lsec, o_got, res[0], res[1], res[2]))
        hidden = res[3]
        if not last:
            low, low_prompt = res[4], res[5]
    y_prompt, y_cont = leave(res[4:8], sc, prompt_row)

    grad = enter(cot_prompt[0], cot_cont[0], sc, vecs, False)[0]
    acc_pack = blank((NB, 4, D, PACK), BF16)
    back = None
    small = [None] * LAYERS
    small_qkv = [None] * LAYERS
    sums = []
    done_pack = [None] * NB
    done_qkv = [None] * NB
    dws = [None] * LAYERS
    steps = bits_of("row") + bits_of("dp")
    fence = []
    sent = None
    for i in reversed(range(LAYERS)):
        h_in, own, oth, o_send, q, kv, lse, lsec, o_got, h1, up, act = saved[i]
        res = mlp_bwd(i, sc, grad, back, h1, up, vecs, packs, prompt, fence)
        gm, du, a2, grad, go = res[:5]
        do_send, small[i] = res[5:9], res[9]
        do_got = exchange_heads(do_send)
        if i < NB:
            send, keep, acc_pack, token = dw_last(i, sc, a2, gm, go, du, act, o_got, acc_pack)
            sent = (keep, swap_core(send))
        else:
            acc_pack, token = dw_mlp(i, sc, a2, gm, go, du, act, o_got, acc_pack)
        res = attn_bwd(i, sc, do_got, o_send, q, kv, lse, lsec, wqkv_all, pos, dims, [token])
        da_own, da_oth = res[:4], res[4 : 4 * rows]
        dq, dkv, small_qkv[i] = res[4 * rows :]
        base, got, rest = collect(da_own, da_oth)
        dws[i], token = dw_qkv(i, sc, own, oth, dq, dkv)
        fence = [token]
        for part in sums:
            fence.append(part.step())
        if i < NB:
            keep, recv = sent
            far = add_low(keep[1], recv[1])
            near = (keep[0], recv[0], swap_x(far))
            fence.append(far)
            value = sum(
                jnp.where(rank_layer[l] == i, dws[l].astype(F32), 0.0) for l in range(i, LAYERS)
            )
            shape = (dps, rows, D // (dps * rows), D)
            done_qkv[i] = Reduce(value.astype(BF16).reshape(shape), steps, None)
            sums.append(done_qkv[i])
            done_pack[i] = near
        back = (h_in, base, got, rest)
        if i + 1 < NB:
            near = done_pack[i + 1]
            value = (near[0].astype(F32) + near[1].astype(F32) + near[2].astype(F32)).astype(BF16)
            shape = (dps, rows, D // (dps * rows), PACK)
            done_pack[i + 1] = Reduce(value.reshape(shape), steps, None)
            sums.append(done_pack[i + 1])
            fence.append(value)

    res = final_norm(sc, grad, back, vecs, prompt, width)
    dx_prompt, dx_cont = leave(res[:4], sc, prompt_row)
    last_gain, last_shift = res[4][0:1], res[4][1:2]
    near = done_pack[0]
    value = (near[0].astype(F32) + near[1].astype(F32) + near[2].astype(F32)).astype(BF16)
    done_pack[0] = Reduce(value.reshape(dps, rows, D // (dps * rows), PACK), steps, None)
    done_pack = [part.finish() for part in done_pack]
    done_qkv = [part.finish() for part in done_qkv]

    pieces = []
    for i in range(LAYERS):
        ups = reorder(small[i][0:4])
        nxt = small[i - 1] if i > 0 else None
        gain1 = last_gain if i == 0 else nxt[8:9]
        shift1 = last_shift if i == 0 else nxt[9:10]
        vec6 = jnp.concatenate([small[i][5:6], small[i][4:5], small[i][6:8], gain1, shift1], axis=0)
        vec6 = vec6.reshape(6, 4, width).transpose(1, 0, 2).reshape(4, 6 * width)
        sums = small_qkv[i][:, 0, :].reshape(HEADS_COL, 4, HD)
        mine = jnp.concatenate([sums[:, 0].reshape(-1), sums[:, 3].reshape(-1)])
        spot = (jnp.arange(4) == my_col)[:, None]
        qv = jnp.where(spot, mine[None], 0.0)
        pieces.append(jnp.concatenate([vec6, ups, qv], axis=1))
    stacked = jnp.stack(pieces)
    by_block = jnp.stack(
        [
            sum(jnp.where(block_of[i] == b, stacked[i], 0.0) for i in range(LAYERS))
            for b in range(NB)
        ],
        axis=1,
    )
    mine = sum_small(by_block).reshape(NB, -1)
    g_vec = mine[:, : 6 * width].reshape(NB, 6, width)
    g_bup = mine[:, 6 * width : 6 * width + D]
    g_qv = mine[:, 6 * width + D :].reshape(NB, 2, width)

    def by_rank(parts):
        return jnp.stack(
            [sum(jnp.where(rank_of[b] == k, parts[k], 0.0) for k in range(NB)) for b in range(NB)]
        )

    g_pack = by_rank(done_pack)
    g_heads = by_rank(done_qkv).reshape(NB, -1, HEADS_COL, 4, HD)
    g_qkv = jnp.stack([g_heads[:, :, :, j].reshape(NB, -1, width) for j in (0, 2, 3)], axis=2)
    return (
        y_prompt,
        y_cont,
        dx_prompt,
        dx_cont,
        g_qkv,
        g_qv,
        g_pack[:, :, 1536 : 1536 + width],
        g_vec[:, 0],
        g_pack[:, :, 0:768],
        g_bup,
        g_pack[:, :, 768:1536],
        g_vec[:, 1],
        g_vec[:, 4],
        g_vec[:, 5],
        g_vec[:, 2],
        g_vec[:, 3],
    )


def solution(mesh):
    dps, rows = mesh.shape["dp"], mesh.shape["row"]
    fine = Mesh(mesh.devices.reshape(dps, rows, 2, 2), ("dp", "row", "x", "core"))
    col = ("x", "core")
    both = ("dp", "row")
    tokens = P("dp", "row", col)
    narrow = P(None, col)
    wide = P(None, both, col)
    in_specs = (
        tokens,
        tokens,
        P("dp", "row"),
        P(),
        P(None, both, None, col),
        P(None, None, col),
        wide,
        narrow,
        wide,
        narrow,
        wide,
        narrow,
        narrow,
        narrow,
        narrow,
        narrow,
        tokens,
        tokens,
    )
    out_specs = (
        tokens,
        tokens,
        tokens,
        tokens,
        P(None, both, None, col),
        P(None, None, col),
        wide,
        narrow,
        wide,
        narrow,
        wide,
        narrow,
        narrow,
        narrow,
        narrow,
        narrow,
    )
    return jax.shard_map(
        per_device, mesh=fine, in_specs=in_specs, out_specs=out_specs, check_vma=False
    )
```

```python
import functools

import jax
import jax.numpy as jnp
from jax import lax
from jax.experimental import pallas as pl
from jax.experimental.pallas import tpu as pltpu
from jax.sharding import Mesh
from jax.sharding import PartitionSpec as P

D = 768
HD = 64
LAYERS = 6
NB = 3
HEADS_COL = 3
PACK = 1792
NORM_EPS = 1e-05
MASK_FILL = -1000000000.0
GELU_COEF = 0.7978845608028654
F32 = jnp.float32
BF16 = jnp.bfloat16
MIB = 1024 * 1024


def nn(a, b):
    return lax.dot_general(a, b, (((1,), (0,)), ((), ())), preferred_element_type=F32)


def nt(a, b):
    return lax.dot_general(a, b, (((1,), (1,)), ((), ())), preferred_element_type=F32)


def tn(a, b):
    return lax.dot_general(a, b, (((0,), (0,)), ((), ())), preferred_element_type=F32)


def stats(hidden):
    mean = jnp.sum(hidden, axis=1, keepdims=True) * (1.0 / D)
    square = jnp.sum(hidden * hidden, axis=1, keepdims=True) * (1.0 / D)
    inverse = lax.rsqrt(square - mean * mean + NORM_EPS)
    return (hidden - mean) * inverse, inverse


def norm_back(grad, gain, centered, inverse):
    scaled = grad * gain
    first = jnp.sum(scaled, axis=1, keepdims=True) * (1.0 / D)
    second = jnp.sum(scaled * centered, axis=1, keepdims=True) * (1.0 / D)
    return inverse * (scaled - first - centered * second)


def colsum(value):
    return jnp.sum(value, axis=0, keepdims=True)


def to_row(column):
    rows = column.shape[0]
    return jnp.transpose(jnp.broadcast_to(column, (rows, 128)))[0:1, :]


class Row:
    def __init__(self, ref, layer):
        self.ref, self.base = ref, layer * 8

    def __getitem__(self, j):
        return self.ref[self.base + j]


def strip(kernel, layer, count, deps):
    def run(sc, *refs):
        kernel(Row(sc, layer), *refs[:count], *refs[count + deps :])

    return run


def params(limit, **more):
    return pltpu.CompilerParams(vmem_limit_bytes=limit * MIB, **more)


def cost(flops, nbytes, trans=0):
    return pl.CostEstimate(flops=int(flops), bytes_accessed=int(nbytes), transcendentals=int(trans))


class Weights:

    def __init__(self, sc, packs, wout, wud, sems):
        self.sc, self.packs, self.sems = sc, packs, sems
        self.dst = ((wout, 1536, 256), (wud, 0, 1536))
        self.parts, self.size = packs[0].shape[1], packs[0].shape[2]

    def start(self, order):
        if len(self.packs) == 1:
            self.start_from(self.packs[0], order)
        else:
            for k, src in enumerate(self.packs):
                pl.when(self.sc[1] == k)(functools.partial(self.start_from, src, order))

    def start_from(self, src, order):
        for kind in order:
            dst, lo, size = self.dst[kind]
            for s in range(4):
                for j in range(self.parts):
                    rows = pl.ds(j * self.size, self.size)
                    pltpu.make_async_copy(
                        src.at[self.sc[3] ^ s, j, :, pl.ds(lo, size)],
                        dst.at[s, rows],
                        self.sems.at[kind, s],
                    ).start()

    def wait(self, kind, s):
        dst = self.dst[kind][0].at[s]
        pltpu.make_async_copy(dst, dst, self.sems.at[kind, s]).wait()


def mlp_fwd_kernel(ranks, last, prompt, sc, *refs):
    h_ref, o0, o1, o2, o3, vec_ref, bup_ref, nvec_ref = refs[:8]
    outs = refs[8 + ranks :]
    h1_ref, u_ref, h_out = outs[:3]
    wout, wud, sems = outs[-3:]
    weights = Weights(sc, refs[8 : 8 + ranks], wout, wud, sems)
    weights.start((0, 1))
    total = h_ref[...] + vec_ref[0, 0:1, :]
    for s, o_ref in enumerate((o0, o1, o2, o3)):
        weights.wait(0, s)
        total = total + nt(o_ref[...], wout[s])
    h1_ref[...] = total
    centered, _ = stats(total)
    a2 = (centered * vec_ref[0, 2:3, :] + vec_ref[0, 3:4, :]).astype(BF16)
    h_out[...] = total + vec_ref[0, 1:2, :]
    for s in range(4):
        weights.wait(1, s)
        bias = bup_ref[0, pl.ds(sc[3] ^ s, 1), 0, :]
        up = nn(a2, wud[s, :, 0:768]) + bias
        u_ref[s] = up.astype(BF16)
        act = 0.5 * up * (1.0 + jnp.tanh(GELU_COEF * (up + 0.044715 * up * up * up)))
        h_out[...] += nt(act.astype(BF16), wud[s, :, 768:1536])
    if last:
        y_refs = outs[3:7]
        send_features(sc, h_out, y_refs)
    else:
        a_ref, ap_ref = outs[3:5]
        centered, _ = stats(h_out[...])
        nxt = (centered * nvec_ref[0, 4:5, :] + nvec_ref[0, 5:6, :]).astype(BF16)
        a_ref[...] = nxt
        ap_ref[...] = nxt[:prompt]


def send_features(sc, value, refs):
    width = refs[0].shape[1]
    for s, ref in enumerate(refs):
        for c in range(4):

            def put(ref=ref, c=c):
                ref[...] = value[:, c * width : (c + 1) * width].astype(BF16)

            pl.when((sc[3] ^ s) == c)(put)


def whole_spec(shape):
    return pl.BlockSpec(shape, lambda i, sc: (0,) * len(shape))


def vec_specs(layer):
    at = layer * 8
    return [
        pl.BlockSpec((1, 8, D), lambda i, sc: (sc[at], 0, 0)),
        pl.BlockSpec((1, 4, 1, D), lambda i, sc: (sc[at], 0, 0, 0)),
        pl.BlockSpec((1, 8, D), lambda i, sc: (sc[at + 2], 0, 0)),
    ]


WSCR = [
    pltpu.VMEM((4, D, 256), BF16),
    pltpu.VMEM((4, D, 1536), BF16),
    pltpu.SemaphoreType.DMA((2, 4)),
]
ANY = pl.BlockSpec(memory_space=pl.ANY)


def mlp_fwd(layer, sc, hidden, o_parts, vecs, bup, packs, prompt, last, width, deps=()):
    tok = hidden.shape[0]
    shapes = [
        jax.ShapeDtypeStruct((tok, D), F32),
        jax.ShapeDtypeStruct((4, tok, D), BF16),
        jax.ShapeDtypeStruct((tok, D), F32),
    ]
    if last:
        shapes += [jax.ShapeDtypeStruct((tok, width), BF16)] * 4
    else:
        shapes += [jax.ShapeDtypeStruct((tok, D), BF16), jax.ShapeDtypeStruct((prompt, D), BF16)]
    out_specs = [whole_spec(v.shape) for v in shapes]
    ins = [hidden, *o_parts, vecs, bup, vecs, *packs]
    kernel = functools.partial(mlp_fwd_kernel, len(packs), last, prompt)
    return pl.pallas_call(
        strip(kernel, layer, len(ins), len(deps)),
        grid_spec=pltpu.PrefetchScalarGridSpec(
            num_scalar_prefetch=1,
            grid=(1,),
            in_specs=[whole_spec((tok, D))]
            + [whole_spec((tok, 256))] * 4
            + vec_specs(layer)
            + [ANY] * (len(packs) + len(deps)),
            out_specs=out_specs,
            scratch_shapes=WSCR,
        ),
        out_shape=shapes,
        compiler_params=params(44),
        cost_estimate=cost(2 * tok * D * 6912, 16e6, tok * 3072),
        name="mlp_fwd",
    )(sc, *ins, *deps)


def mlp_bwd_kernel(ranks, others, first, prompt, sc, *refs):
    if first:
        g_ref, refs = refs[0], refs[1:]
    else:
        nin = 4 + 2 * others
        g_ref, hn_ref, p0_ref, rx_ref = refs[:4]
        rest = refs[4:nin]
        refs = refs[nin:]
    h1_ref, u_hbm, vec_ref, nvec_ref = refs[:4]
    outs = refs[4 + ranks :]
    tok_ref, mine_ref, theirs_ref, g1_ref, d0, d1, d2, d3, small_ref = outs[:9]
    wout, wud, sems, u_ref, usem = outs[9:]
    loads = [pltpu.make_async_copy(u_hbm.at[s], u_ref.at[s], usem.at[s]) for s in range(4)]
    weights = Weights(sc, refs[4 : 4 + ranks], wout, wud, sems)
    weights.start((1, 0))
    for copy in loads:
        copy.start()
    small_ref[...] = jnp.zeros_like(small_ref)
    if first:
        grad = g_ref[...]
    else:
        g1_ref[...] = p0_ref[...].astype(F32) + rx_ref[...].astype(F32)
        for ref in rest:
            g1_ref[0:prompt, :] += ref[...].astype(F32)
        da1 = g1_ref[...]
        centered, inverse = stats(hn_ref[...])
        small_ref[8:9, :] = colsum(da1 * centered)
        small_ref[9:10, :] = colsum(da1)
        grad = g_ref[...] + norm_back(da1, nvec_ref[0, 4:5, :], centered, inverse)
    gm = grad.astype(BF16)
    tok_ref[1] = gm
    small_ref[4:5, :] = colsum(gm.astype(F32))
    for s in range(4):
        weights.wait(1, s)
        dm = nn(gm, wud[s, :, 768:1536])
        loads[s].wait()
        up = u_ref[s].astype(F32)
        square = up * up
        tanh = jnp.tanh(GELU_COEF * up * (1.0 + 0.044715 * square))
        slope = 0.5 * (1.0 + tanh) + 0.5 * up * (1.0 - tanh * tanh) * (
            GELU_COEF * (1.0 + 3.0 * 0.044715 * square)
        )
        du = (dm * slope).astype(BF16)
        side = mine_ref if s % 2 == 0 else theirs_ref
        side[s // 2] = du
        side[2 + s // 2] = (0.5 * up * (1.0 + tanh)).astype(BF16)
        small_ref[s : s + 1, :] = colsum(du.astype(F32))
        term = nt(du, wud[s, :, 0:768])
        if s == 0:
            g1_ref[...] = term
        else:
            g1_ref[...] += term
    da2 = g1_ref[...]
    centered, inverse = stats(h1_ref[...])
    gain = vec_ref[0, 2:3, :]
    tok_ref[0] = (centered * gain + vec_ref[0, 3:4, :]).astype(BF16)
    small_ref[6:7, :] = colsum(da2 * centered)
    small_ref[7:8, :] = colsum(da2)
    grad = grad + norm_back(da2, gain, centered, inverse)
    g1_ref[...] = grad
    go = grad.astype(BF16)
    tok_ref[2] = go
    small_ref[5:6, :] = colsum(go.astype(F32))
    for s, ref in enumerate((d0, d1, d2, d3)):
        weights.wait(0, s)
        ref[...] = nn(go, wout[s]).astype(BF16)


def mlp_bwd(layer, sc, grad, back, h1, up, vecs, packs, prompt, deps=()):
    tok = grad.shape[0]
    first = back is None
    others = 0 if first else len(back[3])
    shapes = [
        jax.ShapeDtypeStruct((3, tok, D), BF16),
        jax.ShapeDtypeStruct((4, tok, D), BF16),
        jax.ShapeDtypeStruct((4, tok, D), BF16),
        jax.ShapeDtypeStruct((tok, D), F32),
    ]
    shapes += [jax.ShapeDtypeStruct((tok, 256), BF16)] * 4
    shapes += [jax.ShapeDtypeStruct((16, D), F32)]
    extra = [] if first else [back[0], back[1], back[2], *back[3]]
    specs = vec_specs(layer)
    ins = [grad, *extra, h1, up, vecs, vecs, *packs]
    kernel = functools.partial(mlp_bwd_kernel, len(packs), others // 2, first, prompt)
    return pl.pallas_call(
        strip(kernel, layer, len(ins), len(deps)),
        grid_spec=pltpu.PrefetchScalarGridSpec(
            num_scalar_prefetch=1,
            grid=(1,),
            in_specs=[whole_spec(v.shape) for v in [grad, *extra, h1]]
            + [ANY, specs[0], specs[2]]
            + [ANY] * (len(packs) + len(deps)),
            out_specs=[whole_spec(s.shape) for s in shapes],
            scratch_shapes=WSCR + [pltpu.VMEM((4, tok, D), BF16), pltpu.SemaphoreType.DMA((4,))],
        ),
        out_shape=shapes,
        compiler_params=params(48),
        cost_estimate=cost(2 * tok * D * 6912, 16e6, tok * 3072),
        name="mlp_bwd",
    )(sc, *ins, *deps)


def attn_fwd_kernel(dims, sc, *refs):
    rows, piece, cpiece, chunk, cont = dims
    npc = 4 * rows
    own, oth = refs[:4], refs[4:npc]
    w_ref, b_ref, prow, pcol, crow, ccol, srow, scol = refs[npc : npc + 8]
    outs = refs[npc + 8 :]
    o_refs = outs[:4]
    q_ref, kv_ref, lse_ref, lsec_ref, m_s, l_s, acc_s = outs[4:]
    head = pl.program_id(0)
    base_b = chunk * rows
    base_c = 2 * chunk * rows
    weight = w_ref[0]
    bias = b_ref[0]
    for s in range(4):
        mixed = nn(own[s][...], weight) + bias
        low_q = (mixed[:, 0:128].astype(BF16).astype(F32) * 0.125).astype(BF16)
        low_kv = mixed[:, 128:256].astype(BF16)
        q_ref[0, s * piece : (s + 1) * piece, :] = low_q[0:piece]
        q_ref[0, chunk + s * piece : chunk + (s + 1) * piece, :] = low_q[piece : 2 * piece]
        q_ref[0, 2 * chunk + s * cpiece : 2 * chunk + (s + 1) * cpiece, :] = low_q[2 * piece :]
        kv_ref[0, s * piece : (s + 1) * piece, :] = low_kv[0:piece]
        kv_ref[0, base_b + s * piece : base_b + (s + 1) * piece, :] = low_kv[piece : 2 * piece]
        kv_ref[0, base_c + s * cpiece : base_c + (s + 1) * cpiece, :] = low_kv[2 * piece :]
    for t in range(1, rows):
        for s in range(4):
            low_kv = (nn(oth[(t - 1) * 4 + s][...], weight[:, 128:256]) + bias[:, 128:256]).astype(BF16)
            at = t * chunk + s * piece
            kv_ref[0, at : at + piece, :] = low_kv[0:piece]
            kv_ref[0, base_b + at : base_b + at + piece, :] = low_kv[piece : 2 * piece]
    lanes = lax.broadcasted_iota(jnp.int32, (1, 128), 1)
    upper = lanes >= 64
    sub = min(256, chunk)

    def begin(query, keys, mask):
        scores = nt(query, keys)
        if mask is not None:
            size = mask.shape[1]
            tail = jnp.where(mask, scores[:, -size:], MASK_FILL)
            if size == scores.shape[1]:
                scores = tail
            else:
                scores = jnp.concatenate([scores[:, :-size], tail], axis=1)
        top = jnp.max(scores, axis=1, keepdims=True)
        prob = jnp.exp(scores - top)
        return top, jnp.sum(prob, axis=1, keepdims=True), nn(prob.astype(BF16), keys)

    def put(out, row, size):
        low = jnp.where(upper, out, 0.0)

        def first_head():
            value = pltpu.roll(low, 64, 1).astype(BF16)
            store(value, row, size, 0, False)

        def second_head():
            store(low.astype(BF16), row, size, 0, True)

        def third_head():
            store(pltpu.roll(low, 64, 1).astype(BF16), row, size, 1, False)

        pl.when(head == 0)(first_head)
        pl.when(head == 1)(second_head)
        pl.when(head == 2)(third_head)

    def store(value, row, size, half, add):
        s, at = row
        lo = half * 128
        if add:
            o_refs[s][at : at + size, lo : lo + 128] = (
                o_refs[s][at : at + size, lo : lo + 128] + value
            )
        else:
            o_refs[s][at : at + size, lo : lo + 128] = value

    for i in range(chunk // sub):
        at = i * sub
        mask = prow[0:1, :] <= pcol[at : at + sub, :]
        top, total, acc = begin(q_ref[0, at : at + sub, :], kv_ref[0, 0:chunk, :], mask)
        m_s[at : at + sub, :], l_s[at : at + sub, :], acc_s[at : at + sub, :] = top, total, acc
        at_b = chunk + at
        top, total, acc = begin(
            q_ref[0, at_b : at_b + sub, :], kv_ref[0, 0 : base_b + chunk, :], mask
        )
        m_s[at_b : at_b + sub, :], l_s[at_b : at_b + sub, :] = top, total
        acc_s[at_b : at_b + sub, :] = acc
    my_row = sc[5]
    for t in range(1, rows):
        before = lax.rem(my_row + t, rows) < my_row
        q_at = jnp.where(before, 0, chunk)
        k_at = jnp.where(before, t * chunk, base_b + t * chunk)
        keys = kv_ref[0, pl.ds(pl.multiple_of(k_at, 128), chunk), :]
        for i in range(chunk // sub):
            at = pl.ds(pl.multiple_of(q_at + i * sub, 128), sub)
            scores = nt(q_ref[0, at, :], keys)
            old = m_s[at, :]
            top = jnp.maximum(old, jnp.max(scores, axis=1, keepdims=True))
            scale = jnp.exp(old - top)
            prob = jnp.exp(scores - top)
            m_s[at, :] = top
            l_s[at, :] = l_s[at, :] * scale + jnp.sum(prob, axis=1, keepdims=True)
            acc_s[at, :] = acc_s[at, :] * scale + nn(prob.astype(BF16), keys)
    for half in range(2):
        for s in range(4):
            at = half * chunk + s * piece
            total = l_s[at : at + piece, :]
            put(acc_s[at : at + piece, :] / total, (s, half * piece), piece)
        for i in range(chunk // sub):
            at = half * chunk + i * sub
            column = m_s[at : at + sub, :] + jnp.log(l_s[at : at + sub, :])
            lse_ref[0, half, :, i * sub : (i + 1) * sub] = to_row(column)
    mask = (crow[0:1, :] <= ccol[...]) & (srow[0:1, :] == scol[...])
    query = q_ref[0, 2 * chunk : 2 * chunk + cont, :]
    top, total, acc = begin(query, kv_ref[0], mask)
    out = acc / total
    for s in range(4):
        put(out[s * cpiece : (s + 1) * cpiece], (s, 2 * piece), cpiece)
    lsec_ref[0] = to_row(top + jnp.log(total))


def attn_inputs(pos):
    return [pl.BlockSpec(v.shape, lambda i, sc: (0, 0)) for v in pos]


def attn_fwd(layer, sc, own, oth, w_all, b_all, pos, dims, deps=()):
    single = w_all.shape[0] == 1
    rows, piece, cpiece, chunk, cont = dims
    tok = own[0].shape[0]
    nq, nk = 2 * chunk + cont, 2 * chunk * rows + cont
    shapes = [jax.ShapeDtypeStruct((tok, 256), BF16)] * 4 + [
        jax.ShapeDtypeStruct((3, nq, 128), BF16),
        jax.ShapeDtypeStruct((3, nk, 128), BF16),
        jax.ShapeDtypeStruct((3, 2, 1, chunk), F32),
        jax.ShapeDtypeStruct((3, 1, cont), F32),
    ]
    out_specs = [whole_spec((tok, 256))] * 4 + [
        pl.BlockSpec((1, nq, 128), lambda i, sc: (i, 0, 0)),
        pl.BlockSpec((1, nk, 128), lambda i, sc: (i, 0, 0)),
        pl.BlockSpec((1, 2, 1, chunk), lambda i, sc: (i, 0, 0, 0)),
        pl.BlockSpec((1, 1, cont), lambda i, sc: (i, 0, 0)),
    ]
    at = layer * 8
    count = len(own) + len(oth) + 2 + len(pos)
    return pl.pallas_call(
        strip(functools.partial(attn_fwd_kernel, dims), layer, count, len(deps)),
        grid_spec=pltpu.PrefetchScalarGridSpec(
            num_scalar_prefetch=1,
            grid=(3,),
            in_specs=[whole_spec(v.shape) for v in [*own, *oth]]
            + [
                pl.BlockSpec((1, D, 256), lambda i, sc: (0 if single else sc[at + 1], 0, i)),
                pl.BlockSpec((1, 1, 256), lambda i, sc: (sc[at], 0, i)),
            ]
            + attn_inputs(pos)
            + [ANY] * len(deps),
            out_specs=out_specs,
            scratch_shapes=[
                pltpu.VMEM((2 * chunk, 1), F32),
                pltpu.VMEM((2 * chunk, 1), F32),
                pltpu.VMEM((2 * chunk, 128), F32),
            ],
        ),
        out_shape=shapes,
        compiler_params=params(52),
        cost_estimate=cost(2 * nq * D * 768 * 2 + 8 * 3 * nq * nk * 64, 12e6, 3 * nq * nk),
        name="attn_fwd",
    )(sc, *own, *oth, w_all, b_all, *pos, *deps)


def attn_bwd_kernel(dims, sc, *refs):
    rows, piece, cpiece, chunk, cont = dims
    do_refs, o_refs = refs[:4], refs[4:8]
    q_ref, kv_ref, lse_ref, lsec_ref, w_ref = refs[8:13]
    prow, pcol, crow, ccol, srow, scol = refs[13:19]
    outs = refs[19:]
    npc = 4 * rows
    mine_out, theirs_out = outs[:2]
    dq_out, dkv_out, bias_out = outs[2:5]
    do_s, drow, drowc, dq_s, dkv_s, da_s = outs[5:]
    head = pl.program_id(0)
    base_b = chunk * rows
    base_c = 2 * chunk * rows
    tok = 2 * piece + cpiece
    upper = lax.broadcasted_iota(jnp.int32, (1, 128), 1) >= 64

    def take(ref):
        value = ref[...].astype(F32)
        left, right = value[:, 0:128], value[:, 128:256]
        pick = jnp.where(head == 2, pltpu.roll(right, 64, 1), left)
        pick = jnp.where(head == 0, pltpu.roll(left, 64, 1), pick)
        return jnp.where(upper, pick, 0.0)

    for s in range(4):
        dout = take(do_refs[s])
        low = dout.astype(BF16)
        do_s[s * piece : (s + 1) * piece, :] = low[0:piece]
        do_s[chunk + s * piece : chunk + (s + 1) * piece, :] = low[piece : 2 * piece]
        do_s[2 * chunk + s * cpiece : 2 * chunk + (s + 1) * cpiece, :] = low[2 * piece :]
        dot = dout * take(o_refs[s])
        dq_s[s * piece : (s + 1) * piece, :] = dot[0:piece]
        dq_s[chunk + s * piece : chunk + (s + 1) * piece, :] = dot[piece : 2 * piece]
        dq_s[2 * chunk + s * cpiece : 2 * chunk + (s + 1) * cpiece, :] = dot[2 * piece :]
    sub = min(128, chunk)
    for half in range(2):
        for i in range(chunk // sub):
            at = half * chunk + i * sub
            column = jnp.sum(dq_s[at : at + sub, :], axis=1, keepdims=True)
            drow[half, :, i * sub : (i + 1) * sub] = to_row(column)
    column = jnp.sum(dq_s[2 * chunk :, :], axis=1, keepdims=True)
    drowc[...] = to_row(column)
    dq_s[...] = jnp.zeros_like(dq_s)
    dkv_s[...] = jnp.zeros_like(dkv_s)

    def pair(q_at, k_at, lse, dot, mask):
        query = q_ref[0, q_at, :]
        keys = kv_ref[0, k_at, :]
        dout = do_s[q_at, :]
        prob = jnp.exp(nt(keys, query) - lse)
        if mask is not None:
            prob = jnp.where(mask, prob, 0.0)
        dprob = nt(keys, dout)
        dscore = (prob * (dprob - dot)).astype(BF16)
        dkv_s[k_at, :] += nn(prob.astype(BF16), dout) + nn(dscore, query)
        dq_s[q_at, :] += tn(dscore, keys)

    kb = min(512, chunk)
    at_a, at_b = pl.ds(0, chunk), pl.ds(chunk, chunk)
    lse_a, lse_b, dot_a, dot_b = lse_ref[0, 0], lse_ref[0, 1], drow[0], drow[1]
    for j in range(chunk // kb):
        mask = pcol[j * kb : (j + 1) * kb, :] <= prow[0:1, :]
        pair(at_a, pl.ds(j * kb, kb), lse_a, dot_a, mask)
        pair(at_b, pl.ds(base_b + j * kb, kb), lse_b, dot_b, mask)
    for j in range(base_b // kb):
        pair(at_b, pl.ds(j * kb, kb), lse_b, dot_b, None)
    my_row = sc[5]
    for t in range(1, rows):
        before = lax.rem(my_row + t, rows) < my_row
        which = jnp.where(before, 0, 1)
        q_at = pl.ds(pl.multiple_of(which * chunk, 128), chunk)
        k_base = jnp.where(before, t * chunk, base_b + t * chunk)
        for j in range(chunk // kb):
            k_at = pl.ds(pl.multiple_of(k_base + j * kb, 128), kb)
            pair(q_at, k_at, lse_ref[0, which], drow[which], None)
    at_c = pl.ds(2 * chunk, cont)
    for j in range(base_c // 512):
        pair(at_c, pl.ds(j * 512, 512), lsec_ref[0], drowc[...], None)
    mask = (ccol[...] <= crow[0:1, :]) & (scol[...] == srow[0:1, :])
    pair(at_c, pl.ds(base_c, cont), lsec_ref[0], drowc[...], mask)

    weight = w_ref[0]
    lower = jnp.logical_not(upper)
    dq_all = jnp.where(lower, dq_s[...] * 0.125, 0.0).astype(BF16)
    q_sum = colsum(dq_all.astype(F32))
    kv_sum = jnp.zeros((1, 128), F32)

    def gather3(value, where):
        return jnp.concatenate([value[a : a + n] for a, n in where], axis=0)

    def emit(slot, count, ref, row, term):
        at = pl.ds(slot, count)

        def set_first():
            da_s[at, :] = term

        def add_next():
            da_s[at, :] += term

        def finish():
            ref[row : row + count, :] = (da_s[at, :] + term).astype(BF16)

        pl.when(head == 0)(set_first)
        pl.when(head == 1)(add_next)
        pl.when(head == 2)(finish)

    for s in range(4):
        dq = gather3(
            dq_all,
            [(s * piece, piece), (chunk + s * piece, piece), (2 * chunk + s * cpiece, cpiece)],
        )
        dkv = jnp.concatenate(
            [
                dkv_s[s * piece : (s + 1) * piece, :],
                dkv_s[base_b + s * piece : base_b + (s + 1) * piece, :],
                dkv_s[base_c + s * cpiece : base_c + (s + 1) * cpiece, :],
            ],
            axis=0,
        ).astype(BF16)
        kv_sum = kv_sum + colsum(dkv.astype(F32))
        both = jnp.concatenate([dq, dkv], axis=1)
        dq_out[s, 0] = both
        side = mine_out if s % 2 == 0 else theirs_out
        emit(s * tok, tok, side, (s // 2) * tok, nt(both, weight))
    for t in range(1, rows):
        for s in range(4):
            at = t * chunk + s * piece
            dkv = jnp.concatenate(
                [dkv_s[at : at + piece, :], dkv_s[base_b + at : base_b + at + piece, :]], axis=0
            ).astype(BF16)
            kv_sum = kv_sum + colsum(dkv.astype(F32))
            k = (t - 1) * 4 + s
            dkv_out[k, 0] = dkv
            side = mine_out if s % 2 == 0 else theirs_out
            row = 2 * tok + (k // 2) * 2 * piece
            emit(4 * tok + k * 2 * piece, 2 * piece, side, row, nt(dkv, weight[:, 128:256]))
    bias_out[0] = jnp.broadcast_to(jnp.concatenate([q_sum, kv_sum], axis=1), (8, 256))


def attn_bwd(layer, sc, do_parts, o_parts, q, kv, lse, lsec, w_all, pos, dims, deps=()):
    rows, piece, cpiece, chunk, cont = dims
    tok = 2 * piece + cpiece
    nq, nk = 2 * chunk + cont, 2 * chunk * rows + cont
    noth = 4 * (rows - 1)
    shapes = (
        [jax.ShapeDtypeStruct((2 * tok + noth * piece, D), BF16)] * 2
        + [
            jax.ShapeDtypeStruct((4, 3, tok, 256), BF16),
            jax.ShapeDtypeStruct((noth, 3, 2 * piece, 128), BF16),
            jax.ShapeDtypeStruct((3, 8, 256), F32),
        ]
    )
    out_specs = [whole_spec(s.shape) for s in shapes[:2]] + [
        pl.BlockSpec((4, 1, tok, 256), lambda i, sc: (0, i, 0, 0)),
        pl.BlockSpec((noth, 1, 2 * piece, 128), lambda i, sc: (0, i, 0, 0)),
        pl.BlockSpec((1, 8, 256), lambda i, sc: (i, 0, 0)),
    ]
    at = layer * 8
    return pl.pallas_call(
        strip(functools.partial(attn_bwd_kernel, dims), layer, 13 + len(pos), len(deps)),
        grid_spec=pltpu.PrefetchScalarGridSpec(
            num_scalar_prefetch=1,
            grid=(3,),
            in_specs=[whole_spec((tok, 256))] * 8
            + [
                pl.BlockSpec((1, nq, 128), lambda i, sc: (i, 0, 0)),
                pl.BlockSpec((1, nk, 128), lambda i, sc: (i, 0, 0)),
                pl.BlockSpec((1, 2, 1, chunk), lambda i, sc: (i, 0, 0, 0)),
                pl.BlockSpec((1, 1, cont), lambda i, sc: (i, 0, 0)),
                pl.BlockSpec((1, D, 256), lambda i, sc: (sc[at + 1], 0, i)),
            ]
            + attn_inputs(pos)
            + [ANY] * len(deps),
            out_specs=out_specs,
            scratch_shapes=[
                pltpu.VMEM((nq, 128), BF16),
                pltpu.VMEM((2, 1, chunk), F32),
                pltpu.VMEM((1, cont), F32),
                pltpu.VMEM((nq, 128), F32),
                pltpu.VMEM((nk, 128), F32),
                pltpu.VMEM((4 * tok + noth * 2 * piece, D), F32),
            ],
        ),
        out_shape=shapes,
        compiler_params=params(56),
        cost_estimate=cost(2 * nq * D * 768 * 2 + 20 * 3 * nq * nk * 64, 14e6, 3 * nq * nk),
        name="attn_bwd",
    )(sc, *do_parts, *o_parts, q, kv, lse, lsec, w_all, *pos, *deps)


def dw_qkv_kernel(rows, sc, *refs):
    npc = 4 * rows
    noth = npc - 4
    srcs, (dq_hbm, dkv_hbm) = refs[:npc], refs[npc : npc + 2]
    new_ref, token = refs[npc + 2 : npc + 4]
    own, oth, dq_s, dkv_s, asem, dsem = refs[npc + 4 :]
    token[...] = jnp.zeros_like(token)
    head = pl.program_id(0)

    def rows_of(k):
        dst = own.at[k] if k < 4 else oth.at[k - 4]
        return pltpu.make_async_copy(srcs[k], dst, asem.at[k])

    def grads_of(h):
        return [
            pltpu.make_async_copy(dq_hbm.at[:, h], dq_s.at[:, h], dsem.at[0, h]),
            pltpu.make_async_copy(dkv_hbm.at[:, h], dkv_s.at[:, h], dsem.at[1, h]),
        ]

    def begin():
        for copy in grads_of(0):
            copy.start()
        for k in range(npc):
            rows_of(k).start()
        for h in (1, 2):
            for copy in grads_of(h):
                copy.start()
        for k in range(npc):
            rows_of(k).wait()

    pl.when(head == 0)(begin)
    for copy in grads_of(head):
        copy.wait()
    total = tn(own[0], dq_s[0, head])
    for s in range(1, 4):
        total = total + tn(own[s], dq_s[s, head])
    right = tn(oth[0], dkv_s[0, head])
    for k in range(1, noth):
        right = right + tn(oth[k], dkv_s[k, head])
    new_ref[:, 0:128] = total[:, 0:128].astype(BF16)
    new_ref[:, 128:256] = (total[:, 128:256] + right).astype(BF16)


def dw_qkv(layer, sc, own, oth, dq, dkv, deps=()):
    rows = (4 + len(oth)) // 4
    tok, two = own[0].shape[0], oth[0].shape[0]
    noth = len(oth)
    ins = [*own, *oth, dq, dkv]
    return pl.pallas_call(
        strip(functools.partial(dw_qkv_kernel, rows), layer, len(ins), len(deps)),
        grid_spec=pltpu.PrefetchScalarGridSpec(
            num_scalar_prefetch=1,
            grid=(3,),
            in_specs=[ANY] * len(ins) + [ANY] * len(deps),
            out_specs=[pl.BlockSpec((D, 256), lambda i, sc: (0, i)), whole_spec((8, 128))],
            scratch_shapes=[
                pltpu.VMEM((4, tok, D), BF16),
                pltpu.VMEM((noth, two, D), BF16),
                pltpu.VMEM((4, 3, tok, 256), BF16),
                pltpu.VMEM((noth, 3, two, 128), BF16),
                pltpu.SemaphoreType.DMA((4 * rows,)),
                pltpu.SemaphoreType.DMA((2, 3)),
            ],
        ),
        out_shape=[
            jax.ShapeDtypeStruct((D, D), BF16),
            jax.ShapeDtypeStruct((8, 128), F32),
        ],
        compiler_params=params(56),
        cost_estimate=cost(2 * 3 * D * (4 * tok * 256 + noth * two * 128), 10e6),
        name="dw_qkv",
    )(sc, *ins, *deps)


def dw_loads(refs, tok, side, outp, sems):
    tok_m, tok_r, mine, got, o0, o2, r1, r3 = refs
    size = tok_m.shape[1]
    low, high = pl.ds(0, size), pl.ds(size, size)
    pairs = [(tok_m, tok.at[:, low]), (tok_r, tok.at[:, high])]
    pairs += [(mine, side.at[:, low]), (got, side.at[:, high])]
    pairs += [(o0, outp.at[0, low]), (r1, outp.at[0, high])]
    pairs += [(o2, outp.at[1, low]), (r3, outp.at[1, high])]
    return [pltpu.make_async_copy(a, b, sems.at[k]) for k, (a, b) in enumerate(pairs)]


def dw_products(tile, tok, side, outp, put):
    for j in range(3):
        cols = slice(j * 256, (j + 1) * 256)
        put(j * 256, tn(tok[0], side[tile, :, cols]))
        put(768 + j * 256, tn(tok[1], side[2 + tile, :, cols]))
    put(1536, tn(tok[2], outp[tile]))


def dw_mlp_kernel(sc, *refs):
    old_ref, new_ref, token = refs[8:11]
    tok, side, outp, sems = refs[11:]
    token[...] = jnp.zeros_like(token)
    tile = pl.program_id(0)
    keep = sc[6] == 0

    def begin():
        loads = dw_loads(refs[:8], tok, side, outp, sems)
        for copy in loads:
            copy.start()
        for copy in loads:
            copy.wait()

    pl.when(tile == 0)(begin)

    def put(lo, value):
        size = value.shape[1]
        old = old_ref[0, 0, :, lo : lo + size].astype(F32)
        new_ref[0, 0, :, lo : lo + size] = (value + jnp.where(keep, old, 0.0)).astype(BF16)

    dw_products(tile, tok, side, outp, put)


def dw_scratch(tok):
    return [
        pltpu.VMEM((3, 2 * tok, D), BF16),
        pltpu.VMEM((4, 2 * tok, D), BF16),
        pltpu.VMEM((2, 2 * tok, 256), BF16),
        pltpu.SemaphoreType.DMA((8,)),
    ]


def dw_mlp(layer, sc, ins, acc, deps=()):
    tok = ins[0].shape[1]
    at = layer * 8
    acc_spec = pl.BlockSpec((1, 1, D, PACK), lambda i, sc: (sc[at + 1], i, 0, 0))
    return pl.pallas_call(
        strip(dw_mlp_kernel, layer, 9, len(deps)),
        grid_spec=pltpu.PrefetchScalarGridSpec(
            num_scalar_prefetch=1,
            grid=(2,),
            in_specs=[ANY] * 8 + [acc_spec] + [ANY] * len(deps),
            out_specs=[acc_spec, whole_spec((8, 128))],
            scratch_shapes=dw_scratch(tok),
        ),
        out_shape=[jax.ShapeDtypeStruct(acc.shape, acc.dtype), jax.ShapeDtypeStruct((8, 128), F32)],
        input_output_aliases={9: 0},
        compiler_params=params(56),
        cost_estimate=cost(2 * tok * D * 4 * PACK, 20e6),
        name="dw_mlp",
    )(sc, *ins, acc, *deps)


def dw_last_kernel(rank, groups, slot, sc, *refs):
    keep_a, give_a, keep_b, give_b, acc, token = refs[9:15]
    tok, side, outp, sems, done, other, dsem, osem, out_ref = refs[15:]
    token[...] = jnp.zeros_like(token)
    tile = pl.program_id(0)
    same = sc[1] == rank
    keep = sc[6] == 0
    used = jnp.logical_or(jnp.logical_not(same), keep)

    def load(t):
        return pltpu.make_async_copy(acc.at[rank, t], done.at[t], dsem.at[t])

    def begin():
        loads = dw_loads(refs[:8], tok, side, outp, sems)
        for copy in [*loads, load(0), load(1)]:
            copy.start()
        for copy in loads:
            copy.wait()

    pl.when(tile == 0)(begin)
    load(tile).wait()

    def fetch_other():
        copy = pltpu.make_async_copy(acc.at[sc[1], tile], other, osem)
        copy.start()
        copy.wait()

    pl.when(jnp.logical_not(same))(fetch_other)

    def put(lo, value):
        size = value.shape[1]
        cols = slice(lo, lo + size)
        old = jnp.where(used, done[tile, :, cols].astype(F32), 0.0)
        out_ref[:, cols] = (old + jnp.where(same, value, 0.0)).astype(BF16)

        def add_other():
            before = jnp.where(keep, other[:, cols].astype(F32), 0.0)
            other[:, cols] = (value + before).astype(BF16)

        pl.when(jnp.logical_not(same))(add_other)

    dw_products(tile, tok, side, outp, put)

    def store_other():
        copy = pltpu.make_async_copy(other, acc.at[sc[1], tile], osem)
        copy.start()
        copy.wait()

    pl.when(jnp.logical_not(same))(store_other)
    half = PACK // 2

    def first_half(ref):
        ref[...] = out_ref[:, 0:half]

    pl.when(tile == 0)(functools.partial(first_half, keep_a))
    pl.when(tile == 1)(functools.partial(first_half, give_a))
    size = D // (2 * groups)
    bit = sc[slot]
    for g in range(groups):
        for ref, part in ((keep_b, bit), (give_b, 1 - bit)):
            src = pl.ds(pl.multiple_of((2 * g + part) * size, size), size)
            dst = pl.ds(pl.multiple_of((tile * groups + g) * size, size), size)
            ref[dst, :] = out_ref[src, half:]


def dw_last(layer, sc, ins, acc, groups, deps=()):
    tok = ins[0].shape[1]
    slot = LAYERS * 8 + 1 + len(bits_of("dp")) - layer * 8
    half = jax.ShapeDtypeStruct((D, PACK // 2), BF16)
    return pl.pallas_call(
        strip(functools.partial(dw_last_kernel, layer, groups, slot), layer, 9, len(deps)),
        grid_spec=pltpu.PrefetchScalarGridSpec(
            num_scalar_prefetch=1,
            grid=(2,),
            in_specs=[ANY] * 9 + [ANY] * len(deps),
            out_specs=[whole_spec(half.shape)] * 4 + [ANY, whole_spec((8, 128))],
            scratch_shapes=dw_scratch(tok)
            + [
                pltpu.VMEM((2, D, PACK), BF16),
                pltpu.VMEM((D, PACK), BF16),
                pltpu.SemaphoreType.DMA((2,)),
                pltpu.SemaphoreType.DMA(()),
                pltpu.VMEM((D, PACK), BF16),
            ],
        ),
        out_shape=[half] * 4
        + [
            jax.ShapeDtypeStruct(acc.shape, acc.dtype),
            jax.ShapeDtypeStruct((8, 128), F32),
        ],
        input_output_aliases={9: 4},
        compiler_params=params(56),
        cost_estimate=cost(2 * tok * D * 4 * PACK, 20e6),
        name="dw_last",
    )(sc, *ins, acc, *deps)


def qkv_total(sc, rank, parts, groups, deps):
    size = D // (2 * groups)
    slot = LAYERS * 8 + 1 + len(bits_of("dp"))

    def add(sc, *refs):
        keep, give = refs[-2:]
        bit = sc[slot]
        for g in range(groups):
            for out, side in ((keep, bit), (give, 1 - bit)):
                at = pl.ds(pl.multiple_of((2 * g + side) * size, size), size)
                total = jnp.zeros((size, D), F32)
                for k, ref in enumerate(refs[:-2]):
                    used = sc[(rank + k) * 8 + 1] == rank
                    total = total + jnp.where(used, ref[at, :].astype(F32), 0.0)
                out[g * size : (g + 1) * size, :] = total.astype(BF16)

    shape = jax.ShapeDtypeStruct((D // 2, D), BF16)
    return simple_call(add, sc, parts, [shape] * 2, name="qkv_total", deps=deps)


def blank(shape, dtype):
    def body(out):
        del out

    return pl.pallas_call(
        body,
        out_shape=jax.ShapeDtypeStruct(shape, dtype),
        out_specs=pl.BlockSpec(memory_space=pl.ANY),
        name="blank",
    )()


SWAP = [(0, 1), (1, 0)]


def swap_core(value):
    return lax.ppermute(value, "core", SWAP)


def swap_x(value):
    return lax.ppermute(value, "x", SWAP)


def shift_row(value, t):
    rows = lax.axis_size("row")
    return lax.ppermute(value, "row", [(i, (i - t) % rows) for i in range(rows)])


def shift_row_x(value, t):
    rows = lax.axis_size("row")
    pairs = [(i * 2 + j, ((i - t) % rows) * 2 + (1 - j)) for i in range(rows) for j in range(2)]
    return lax.ppermute(value, ("row", "x"), pairs)


def spread(low, low_prompt):
    rows = lax.axis_size("row")
    from_x = swap_x(low)
    far = []
    for t in range(1, rows):
        far += [shift_row(low_prompt, t), shift_row_x(low_prompt, t)]
    own = [low, swap_core(low), from_x, swap_core(from_x)]
    oth = []
    for t in range(1, rows):
        near, diag = far[2 * t - 2], far[2 * t - 1]
        oth += [near, swap_core(near), diag, swap_core(diag)]
    return own, oth


def exchange_heads(parts):
    flip = {1: [1, 0, 3, 2], 2: [2, 3, 0, 1], 3: [3, 2, 1, 0]}
    out = [parts[0]]
    for s in (1, 2, 3):
        pairs = [(c, flip[s][c]) for c in range(4)]
        out.append(lax.ppermute(parts[s], ("x", "core"), pairs))
    return out


def add_low(a, b):
    return (a.astype(F32) + b.astype(F32)).astype(BF16)


def sum_kernel(sizes, a, b, *outs):
    at = 0
    for size, out in zip(sizes, outs):
        out[...] = add_low(a[at : at + size, :], b[at : at + size, :])
        at += size


def collect(mine, theirs, tok, prompt, deps=()):
    rows = lax.axis_size("row")
    sizes = [tok, tok] + [prompt] * (2 * (rows - 1))
    vmem = pl.BlockSpec(memory_space=pltpu.VMEM)
    count = len(deps)
    sums = pl.pallas_call(
        lambda a, b, *refs: sum_kernel(sizes, a, b, *refs[count:]),
        in_specs=[vmem] * 2 + [ANY] * count,
        out_specs=[vmem] * len(sizes),
        out_shape=[jax.ShapeDtypeStruct((n, D), BF16) for n in sizes],
        compiler_params=params(24),
        cost_estimate=cost(1e6, 4e6),
        name="sum_cores",
    )(mine, swap_core(theirs), *deps)
    got = swap_x(sums[1])
    rest = []
    for t in range(1, rows):
        rest += [shift_row(sums[2 * t], -t), shift_row_x(sums[2 * t + 1], -t)]
    return sums[0], got, rest


def behind(values, deps):
    if not deps:
        return list(values)
    count = len(values)

    def body(*refs):
        del refs

    return pl.pallas_call(
        body,
        in_specs=[ANY] * (count + len(deps)),
        out_specs=[ANY] * count,
        out_shape=[jax.ShapeDtypeStruct(v.shape, v.dtype) for v in values],
        input_output_aliases={k: k for k in range(count)},
        name="behind",
    )(*values, *deps)


def held(value, deps):
    def body(src, *rest):
        rest[-1][...] = src[...]

    vmem = pl.BlockSpec(memory_space=pltpu.VMEM)
    return pl.pallas_call(
        body,
        in_specs=[vmem] + [ANY] * len(deps),
        out_specs=vmem,
        out_shape=jax.ShapeDtypeStruct(value.shape, value.dtype),
        name="held",
    )(value, *deps)


def gather_begin(value, names):
    total = 1
    for a in names:
        total *= lax.axis_size(a)
    return [lax.ppermute(value, names, [(i, i ^ t) for i in range(total)]) for t in range(1, total)]


def gather_end(sc, pieces, index, ahead=(), deps=()):
    lead, n, width = pieces[0].shape
    count = len(pieces)

    def place(sc, *refs):
        out = refs[-1]
        for block in refs[count:-1]:
            out[0:1] = block[...]
        base = len(ahead)
        for t in range(count):
            at = pl.ds(pl.multiple_of((sc[index] ^ t) * n, n), n)
            out[base : base + lead, at, :] = refs[t][...]

    shape = jax.ShapeDtypeStruct((lead + len(ahead), count * n, width), BF16)
    return simple_call(place, sc, [*pieces, *ahead], [shape], name="place", deps=deps)[0]


def zig(j, rows):
    return j if j < rows else 2 * rows - 1 - j


def split_kernel(piece, cpiece, sc, even, odd, cont, *outs):
    for s, out in enumerate(outs):
        place = sc[3] ^ s
        at = pl.ds(pl.multiple_of(place * piece, piece), piece)

        def fill(first, second, out=out, at=at):
            out[0:piece, :] = first[at, :]
            out[piece : 2 * piece, :] = second[at, :]

        pl.when(sc[7] == 0)(functools.partial(fill, even, odd))
        pl.when(sc[7] == 1)(functools.partial(fill, odd, even))
        out[2 * piece :, :] = cont[pl.ds(pl.multiple_of(place * cpiece, cpiece), cpiece), :]


def merge_kernel(piece, cpiece, sc, p0, p1, p2, p3, even, odd, cont):
    for s, part in enumerate((p0, p1, p2, p3)):
        place = sc[3] ^ s
        at = pl.ds(pl.multiple_of(place * piece, piece), piece)

        def fill(first, second, part=part, at=at):
            first[at, :] = part[0:piece, :]
            second[at, :] = part[piece : 2 * piece, :]

        pl.when(sc[7] == 0)(functools.partial(fill, even, odd))
        pl.when(sc[7] == 1)(functools.partial(fill, odd, even))
        cont[pl.ds(pl.multiple_of(place * cpiece, cpiece), cpiece), :] = part[2 * piece :, :]


def join_kernel(prompt, normed, sc, p0, p1, p2, p3, vec_ref, h_ref, *outs):
    width = p0.shape[1]
    for s, part in enumerate((p0, p1, p2, p3)):
        value = part[...].astype(F32)
        for c in range(4):

            def put(value=value, c=c):
                h_ref[:, c * width : (c + 1) * width] = value

            pl.when((sc[3] ^ s) == c)(put)
    if normed:
        a_ref, ap_ref = outs
        centered, _ = stats(h_ref[...])
        low = (centered * vec_ref[0, 4:5, :] + vec_ref[0, 5:6, :]).astype(BF16)
        a_ref[...] = low
        ap_ref[...] = low[:prompt]


def simple_call(kernel, sc, ins, shapes, specs=None, name="small", deps=()):
    return pl.pallas_call(
        strip(kernel, 0, len(ins), len(deps)),
        grid_spec=pltpu.PrefetchScalarGridSpec(
            num_scalar_prefetch=1,
            grid=(1,),
            in_specs=(specs or [whole_spec(v.shape) for v in ins]) + [ANY] * len(deps),
            out_specs=[whole_spec(v.shape) for v in shapes],
        ),
        out_shape=shapes,
        compiler_params=params(24),
        cost_estimate=cost(1e6, 3e6),
        name=name,
    )(sc, *ins, *deps)


def enter(prompt, cont, sc, vecs, normed):
    parts = enter_begin(prompt, cont, sc)
    return parts, enter_end(exchange_heads(parts), sc, vecs, normed, prompt.shape[0] // 4)


def enter_begin(prompt, cont, sc, deps=()):
    rows = lax.axis_size("row")
    half, width = prompt.shape[0] // 2, prompt.shape[1]
    piece, cpiece = half // 4, cont.shape[0] // 4
    tok = 2 * piece + cpiece
    even = prompt[:half]
    odd = prompt[half:]
    if rows > 2:
        even = lax.ppermute(even, "row", [(i, zig(2 * i, rows)) for i in range(rows)])
    odd = lax.ppermute(odd, "row", [(i, zig(2 * i + 1, rows)) for i in range(rows)])
    part = jax.ShapeDtypeStruct((tok, width), BF16)
    parts = simple_call(
        functools.partial(split_kernel, piece, cpiece), sc, [even, odd, cont], [part] * 4, name="split", deps=deps
    )
    return parts


def enter_end(parts, sc, vecs, normed, prompt, deps=()):
    tok, width = parts[0].shape
    shapes = [jax.ShapeDtypeStruct((tok, D), F32)]
    if normed:
        shapes += [jax.ShapeDtypeStruct((tok, D), BF16), jax.ShapeDtypeStruct((prompt, D), BF16)]
    specs = [whole_spec((tok, width))] * 4 + [pl.BlockSpec((1, 8, D), lambda i, sc: (sc[0], 0, 0))]
    return simple_call(
        functools.partial(join_kernel, prompt, normed), sc, [*parts, vecs], shapes, specs, "join", deps
    )


def leave(parts, sc, prompt_rows):
    return leave_end(sc, *leave_begin(exchange_heads(parts), sc, prompt_rows))


def leave_begin(parts, sc, prompt_rows, deps=()):
    width = parts[0].shape[1]
    half = prompt_rows // 2
    piece = half // 4
    cpiece = parts[0].shape[0] - 2 * piece
    shapes = [jax.ShapeDtypeStruct((n, width), BF16) for n in (half, half, 4 * cpiece)]
    even, odd, cont = simple_call(
        functools.partial(merge_kernel, piece, cpiece), sc, parts, shapes, name="merge", deps=deps
    )
    return even, odd, cont


def leave_end(sc, even, odd, cont, deps=()):
    rows = lax.axis_size("row")
    if rows > 2:
        even = lax.ppermute(even, "row", [(zig(2 * i, rows), i) for i in range(rows)])
    odd = lax.ppermute(odd, "row", [(zig(2 * i + 1, rows), i) for i in range(rows)])
    half, width = even.shape

    def stack(sc, first, second, out):
        out[0, 0:half, :] = first[...]
        out[0, half:, :] = second[...]

    shape = jax.ShapeDtypeStruct((1, 2 * half, width), BF16)
    return simple_call(stack, sc, [even, odd], [shape], name="rows", deps=deps)[0], cont[None]


def final_kernel(prompt, others, sc, *refs):
    g_ref, h_ref, p0_ref, rx_ref = refs[:4]
    rest = refs[4 : 4 + others]
    vec_ref = refs[4 + others]
    outs, small, da_ref, out_ref = refs[5 + others : 9 + others], refs[9 + others], refs[10 + others], refs[11 + others]
    da_ref[...] = p0_ref[...].astype(F32) + rx_ref[...].astype(F32)
    for ref in rest:
        da_ref[0:prompt, :] += ref[...].astype(F32)
    da1 = da_ref[...]
    centered, inverse = stats(h_ref[...])
    small[0:1, :] = colsum(da1 * centered)
    small[1:2, :] = colsum(da1)
    out_ref[...] = g_ref[...] + norm_back(da1, vec_ref[0, 4:5, :], centered, inverse)
    send_features(sc, out_ref, outs)


def final_norm(sc, grad, back, vecs, prompt, width, deps):
    tok = grad.shape[0]
    h_in, base, got, rest = back
    ins = [grad, h_in, base, got, *rest, vecs]
    shapes = [jax.ShapeDtypeStruct((tok, width), BF16)] * 4 + [
        jax.ShapeDtypeStruct((8, D), F32),
        jax.ShapeDtypeStruct((tok, D), F32),
        jax.ShapeDtypeStruct((tok, D), F32),
    ]
    specs = [whole_spec(v.shape) for v in ins[:-1]] + [
        pl.BlockSpec((1, 8, D), lambda i, sc: (sc[0], 0, 0))
    ]
    return simple_call(
        functools.partial(final_kernel, prompt, len(rest)), sc, ins, shapes, specs, "final_norm", deps
    )


class Reduce:

    def __init__(self, sc, keep, give, name, names, plan):
        self.sc, self.keep, self.give = sc, keep, give
        self.names, self.plan = list(names), list(plan)
        self.ready, self.waiting = 0, None
        self.send(name)

    def send(self, name):
        axis, bit = name
        count = lax.axis_size(axis)
        self.got = lax.ppermute(self.give, axis, [(i, i ^ bit) for i in range(count)])

    def step(self, deps=(), hold=False):
        rows, width = self.keep.shape
        if not self.plan:
            return []
        name = self.plan.pop(0)
        where = self.names.index(name)
        self.names.pop(where)
        before, size = 2**where, rows // 2 ** (where + 1)
        if name[0] == "x":
            slot = None
        else:
            slot = LAYERS * 8 + 1 + (bits_of("dp") + bits_of("row")).index(name)

        def add(sc, keep, got, new_keep, new_give):
            bit = 0 if slot is None else sc[slot]
            for a in range(before):
                for out, side in ((new_keep, bit), (new_give, 1 - bit)):
                    lo = (2 * a + side) * size
                    at = pl.ds(lo if slot is None else pl.multiple_of(lo, size), size)
                    out[a * size : (a + 1) * size, :] = add_low(keep[at, :], got[at, :])

        if size % 16:
            total = add_low(self.keep, self.got).reshape(before, 2, size, width)
            bit = 0 if slot is None else self.sc[slot]
            self.keep, self.give = (
                lax.dynamic_index_in_dim(total, side, 1, keepdims=False).reshape(rows // 2, width)
                for side in (bit, 1 - bit)
            )
        else:
            shape = jax.ShapeDtypeStruct((rows // 2, width), BF16)
            self.keep, self.give = simple_call(
                add, self.sc, [self.keep, self.got], [shape] * 2, name="add", deps=deps
            )
        if hold and name[0] != "dp":
            self.waiting = name
        else:
            self.send(name)
        return [self.give]

    def release(self, deps):
        if self.waiting is not None:
            self.give = behind([self.give], deps)[0]
            self.send(self.waiting)
            self.waiting = None

    def finish(self):
        while self.plan:
            self.step()
        return [self.keep, self.got]


def bits_of(axis):
    bits, bit = [], lax.axis_size(axis) // 2
    while bit:
        bits.append((axis, bit))
        bit //= 2
    return bits


def reorder(value):
    shape = value.shape
    value = value.reshape((2, 2) + shape[1:])
    value = jnp.where(lax.axis_index("core") == 1, value[:, ::-1], value)
    value = jnp.where(lax.axis_index("x") == 1, value[::-1], value)
    return value.reshape(shape)


def narrow_kernel(width, sc, *refs):
    smalls, qkvs, last_ref, out = refs[:LAYERS], refs[LAYERS : 2 * LAYERS], refs[2 * LAYERS], refs[-1]
    out[...] = jnp.zeros_like(out)
    for b in range(NB):
        total = jnp.zeros((16, D), F32)
        qkv = jnp.zeros((HEADS_COL, 256), F32)
        for i in range(LAYERS):
            mine = sc[i * 8] == b
            total = total + jnp.where(mine, smalls[i][...], 0.0)
            qkv = qkv + jnp.where(mine, qkvs[i][:, 0, :], 0.0)
        gain = jnp.where(sc[0] == b, last_ref[0:2, :], 0.0)
        for i in range(1, LAYERS):
            gain = gain + jnp.where(sc[i * 8] == b, smalls[i - 1][8:10, :], 0.0)
        rows = jnp.concatenate([total[5:6], total[4:5], total[6:8], gain], axis=0)
        for s in range(4):
            out[s, b, 0:1, :] = total[s : s + 1]
            for c in range(4):

                def put(s=s, b=b, c=c, rows=rows):
                    out[s, b, 1:7, 0:width] = rows[:, c * width : (c + 1) * width]

                pl.when((sc[3] ^ s) == c)(put)
        for h in range(HEADS_COL):
            out[0, b, 7:8, h * 256 : (h + 1) * 256] = qkv[h : h + 1]


def end_slot():
    return LAYERS * 8 + 1 + len(bits_of("dp")) + len(bits_of("row"))


def pack_end(sc, parts, width):
    slot = end_slot()
    share = parts[0].shape[0]

    def end(sc, *refs):
        up, down, out = refs[-3:]
        for k in range(NB):
            ka, ga, kb, gb = refs[4 * k : 4 * k + 4]
            left = ka[...].astype(F32) + ga[...].astype(F32)
            right = kb[...].astype(F32) + gb[...].astype(F32)
            for b in range(NB):

                def put(b=b, left=left, right=right):
                    up[b] = left[:, 0:D]
                    down[b, :, 0 : 896 - D] = left[:, D:]
                    down[b, :, 896 - D :] = right[:, 0 : 2 * D - 896]
                    out[b] = right[:, 2 * D - 896 : 2 * D - 896 + width]

                pl.when(sc[slot + b] == k)(put)

    shapes = [jax.ShapeDtypeStruct((NB, share, n), F32) for n in (D, D, width)]
    return simple_call(end, sc, parts, shapes, name="pack_end")


def qkv_end(sc, parts, width):
    slot = end_slot()
    share = parts[0].shape[0]

    def end(sc, *refs):
        out = refs[-1]
        for k in range(NB):
            total = refs[2 * k][...].astype(F32) + refs[2 * k + 1][...].astype(F32)
            for b in range(NB):

                def put(b=b, total=total):
                    for h in range(HEADS_COL):
                        for j, lane in enumerate((0, 128, 192)):
                            at = h * 256 + lane
                            out[b, j, :, h * HD : (h + 1) * HD] = total[:, at : at + HD]

                pl.when(sc[slot + b] == k)(put)

    shape = jax.ShapeDtypeStruct((NB, 3, share, width), F32)
    return simple_call(end, sc, parts, [shape], name="qkv_end")[0].transpose(0, 2, 1, 3)


def narrow_end(sc, value, got, width):
    def end(sc, value, got, bup, qv, *vecs):
        for b in range(NB):
            total = value[b] + got[b]
            bup[b : b + 1, :] = total[0:1]
            for k, out in enumerate(vecs):
                out[b : b + 1, :] = total[1 + k : 2 + k, 0:width]
            for h in range(HEADS_COL):
                for j, lane in enumerate((0, 192)):
                    at = h * 256 + lane
                    qv[b, j : j + 1, h * HD : (h + 1) * HD] = total[7:8, at : at + HD]

    shapes = [jax.ShapeDtypeStruct((NB, D), F32), jax.ShapeDtypeStruct((NB, 2, width), F32)]
    shapes += [jax.ShapeDtypeStruct((NB, width), F32)] * 6
    return simple_call(end, sc, [value, got], shapes, name="narrow_end")


def sum_small(value):
    got = swap_core(jnp.stack([value[1], value[3]]))
    near, far = value[0] + got[0], value[2] + got[1]
    value = near + swap_x(far)
    steps = bits_of("row") + bits_of("dp")
    for k, (axis, bit) in enumerate(steps):
        got = lax.ppermute(value, axis, [(i, i ^ bit) for i in range(lax.axis_size(axis))])
        if k + 1 < len(steps):
            value = value + got
    return value, got


def per_device(
    x_prompt,
    x_cont,
    seg_ids,
    layer_map,
    w_qkv,
    bias_qv,
    w_out,
    b_out,
    w_up,
    b_up,
    w_down,
    b_down,
    ln1_gain,
    ln1_bias,
    ln2_gain,
    ln2_bias,
    cot_prompt,
    cot_cont,
):
    rows, dps = lax.axis_size("row"), lax.axis_size("dp")
    prompt_row, cont = x_prompt.shape[1], x_cont.shape[1]
    width = x_prompt.shape[2]
    chunk = prompt_row // 2
    piece, cpiece = chunk // 4, cont // 4
    prompt = 2 * piece
    dims = (rows, piece, cpiece, chunk, cont)
    my_row, my_x = lax.axis_index("row"), lax.axis_index("x")
    my_col = my_x * 2 + lax.axis_index("core")

    layer_map = layer_map.astype(jnp.int32)
    places = jnp.arange(LAYERS, dtype=jnp.int32)
    blocks = jnp.arange(NB, dtype=jnp.int32)
    first_use = jnp.min(jnp.where(layer_map[None] == blocks[:, None], places[None], 99), axis=1)
    rank_of = jnp.sum((first_use[None] < first_use[:, None]).astype(jnp.int32), axis=1)
    rank_layer = jnp.sum(jnp.where(layer_map[:, None] == blocks[None], rank_of[None], 0), axis=1)
    later = (rank_layer[None] == rank_layer[:, None]) & (places[None] > places[:, None])
    fresh = 1 - jnp.max(later.astype(jnp.int32), axis=1)
    after = jnp.concatenate([layer_map[1:], layer_map[-1:]])

    def fill(value):
        return jnp.broadcast_to(value, (LAYERS,)).astype(jnp.int32)

    sc = jnp.stack(
        [layer_map, rank_layer, after, fill(my_col), fill(my_x), fill(my_row), fresh, fill(my_row % 2)],
        axis=1,
    ).reshape(-1)
    my_dp = lax.axis_index("dp")
    extra = [my_dp * rows + my_row]
    ends = [rank_of[b] for b in range(NB)]
    extra += [(lax.axis_index(a) // b) % 2 for a, b in bits_of("dp") + bits_of("row")]
    sc = jnp.concatenate([sc, jnp.stack(extra + ends).astype(jnp.int32)])

    heads = w_qkv.reshape(NB, -1, 3, HEADS_COL, HD)
    zero = jnp.zeros_like(heads[:, :, 0])
    packed = jnp.stack([heads[:, :, 0], zero, heads[:, :, 1], heads[:, :, 2]], axis=3)
    packed = packed.reshape(NB, -1, D)

    def by_block(stacked):
        nothing = jnp.zeros((), stacked.dtype)
        return [
            sum(jnp.where(rank_of[b] == k, stacked[b], nothing) for b in range(NB)) for k in range(NB)
        ]

    packed = by_block(packed)
    pair = bias_qv.astype(F32).reshape(NB, 2, HEADS_COL, HD)
    none = jnp.zeros((NB, HEADS_COL, 2, HD), F32)
    bqkv = jnp.concatenate([pair[:, 0][:, :, None], none, pair[:, 1][:, :, None]], axis=2).reshape(NB, 1, D)

    def flat(value):
        return value.reshape(NB, -1)

    narrow = jnp.concatenate(
        [flat(v) for v in (b_out, b_down, ln2_gain, ln2_bias, ln1_gain, ln1_bias, b_up)], axis=1
    )
    narrow = jnp.stack(exchange_heads([narrow] * 4))
    narrow = reorder(narrow.astype(F32))
    vecs = narrow[:, :, : 6 * width].reshape(4, NB, 6, width).transpose(1, 2, 0, 3).reshape(NB, 6, D)
    vecs = jnp.concatenate([vecs, jnp.zeros((NB, 2, D), F32)], axis=1)
    bup = narrow[:, :, 6 * width :].transpose(1, 0, 2).reshape(NB, 4, 1, D)

    pack_local = jnp.concatenate(
        [w_up, w_down, w_out, jnp.zeros(w_out.shape[:2] + (64,), BF16)], axis=2
    )
    share = D // (dps * rows)
    packs = []
    for local in by_block(pack_local):
        pack = lax.all_gather(local, ("x", "core", "dp", "row"), axis=0)
        if share % 16:
            packs.append(pack.reshape(4, 1, D, PACK))
        else:
            packs.append(pack.reshape(4, dps * rows, share, PACK))

    def places_of(size):
        index = jnp.arange(4 * size, dtype=jnp.int32)
        return size * ((index // size) ^ my_col) + index % size

    ppos, cpos = places_of(piece), places_of(cpiece)
    seg = reorder(seg_ids[0].astype(jnp.int32).reshape(4, cpiece)).reshape(cont)
    pos = [ppos[None], ppos[:, None], cpos[None], cpos[:, None], seg[None], seg[:, None]]

    tok = prompt + cpiece
    direct = dps * rows <= 8
    parts, (hidden, low, low_prompt) = enter(x_prompt[0], x_cont[0], sc, vecs, True)
    if direct:
        first = held(packed[0][None], [parts[0]])
        first = [first] + gather_begin(first, ("dp", "row"))
        wqkv_first = gather_end(sc, first, LAYERS * 8, deps=[low])
    else:
        wqkv_all = lax.all_gather(jnp.stack(packed), ("dp", "row"), axis=1, tiled=True)
        wqkv_first = wqkv_all
    saved = []
    for i in range(LAYERS):
        last = i == LAYERS - 1
        own, oth = spread(low, low_prompt)
        if i == 1 and direct:
            wqkv_all = gather_end(sc, rest, LAYERS * 8, [wqkv_first], deps=[low])
        weight = wqkv_first if i == 0 else wqkv_all
        res = attn_fwd(i, sc, own, oth, weight, bqkv, pos, dims)
        o_send, (q, kv, lse, lsec) = res[:4], res[4:]
        if i == 0 and direct:
            rest = held(jnp.stack(packed[1:]), [lsec])
            rest = [rest] + gather_begin(rest, ("dp", "row"))
        deps = []
        if i == 2:
            cot_parts = enter_begin(cot_prompt[0], cot_cont[0], sc, [lsec])
            deps = [cot_parts[0]]
        if i == 3:
            grad = enter_end(cot_got, sc, vecs, False, prompt, [lsec])[0]
            deps = [grad]
        o_got = exchange_heads(o_send)
        avail = packs[: min(i, NB - 1) + 1]
        res = mlp_fwd(i, sc, hidden, o_got, vecs, bup, avail, prompt, last, width, deps)
        if i == 2:
            cot_got = exchange_heads(cot_parts)
        saved.append((hidden, own, oth, o_send, q, kv, lse, lsec, o_got, res[0], res[1]))
        hidden = res[2]
        if not last:
            low, low_prompt = res[3], res[4]
    y_send = exchange_heads(res[3:7])

    acc_pack = blank((NB, 2, D, PACK), BF16)
    back = None
    small = [None] * LAYERS
    small_qkv = [None] * LAYERS
    sums = []
    done_pack = [None] * NB
    done_qkv = [None] * NB
    dws = [None] * LAYERS
    dp_bits, row_bits = bits_of("dp"), bits_of("row")
    bits = dp_bits + row_bits
    top, x_bit = row_bits[0], ("x", 1)
    fence = []
    for i in reversed(range(LAYERS)):
        h_in, own, oth, o_send, q, kv, lse, lsec, o_got, h1, up = saved[i]
        res = mlp_bwd(i, sc, grad, back, h1, up, vecs, packs, prompt, fence)
        tokens, mine, theirs, grad = res[:4]
        do_send, small[i] = res[4:8], res[8]
        fence = []
        for part in sums:
            if part.ready <= 2 * (LAYERS - i):
                fence += part.step([small[i]])
        if i == LAYERS - 1:
            y_parts = leave_begin(y_send, sc, prompt_row, [small[i]])
            fence.append(y_parts[0])
        *do_send, tokens, theirs = behind([*do_send, tokens, theirs], fence)
        do_got = exchange_heads(do_send)
        ins = [tokens, swap_core(tokens), mine, swap_core(theirs)]
        ins += [o_got[0], o_got[2], swap_core(o_got[1]), swap_core(o_got[3])]
        if i < NB:
            res = dw_last(i, sc, ins, acc_pack, dps, do_got[1:])
            keep_a, give_a, keep_b, give_b, acc_pack, token = res
            left = [n for n in bits if n != top]
            done_pack[i] = [
                Reduce(sc, keep_a, give_a, x_bit, bits, row_bits + dp_bits[::-1]),
                Reduce(sc, keep_b, give_b, top, [x_bit] + left, [x_bit] + row_bits[1:] + dp_bits[::-1]),
            ]
            sums += done_pack[i]
            fence = [token]
            if i + 1 < NB:
                fence += done_qkv[i + 1].step([token])
        else:
            fence = []
        fence += [part.give for part in sums]
        res = attn_bwd(i, sc, do_got, o_send, q, kv, lse, lsec, wqkv_all, pos, dims, fence)
        da_mine, da_theirs, dq, dkv, small_qkv[i] = res
        fence = []
        for part in sums:
            if part.ready <= 2 * (LAYERS - i) + 1:
                fence += part.step([small_qkv[i]], i > 0)
        if i == LAYERS - 1:
            y_prompt, y_cont = leave_end(sc, *y_parts, deps=[small_qkv[i]])
            fence.append(y_prompt)
        if i > 0:
            base, got, rest = collect(da_mine, behind([da_theirs], fence)[0], tok, prompt)
            dws[i], token = dw_qkv(i, sc, own, oth, dq, dkv)
        else:
            dws[i], token = dw_qkv(i, sc, own, oth, dq, dkv, fence)
            fence = []
            for part in done_pack[0]:
                fence += part.step([token])
            base, got, rest = collect(da_mine, behind([da_theirs], fence)[0], tok, prompt)
        fence = [token]
        if i >= NB:
            acc_pack, token = dw_mlp(i, sc, ins, acc_pack, [base])
            fence.append(token)
        for part in sums:
            part.release([got, *rest])
        if i < NB:
            keep, give = qkv_total(sc, i, dws[i:], dps, [got])
            done_qkv[i] = Reduce(sc, keep, give, top, left, row_bits[1:] + dp_bits[::-1])
            done_qkv[i].ready = 2 * (LAYERS - i) + 3
            sums.append(done_qkv[i])
            fence.append(give)
        back = (h_in, base, got, rest)
        sums = [part for part in sums if part.plan]

    for part in sums:
        if part.ready <= 2 * LAYERS + 2:
            fence += part.step([got])
    res = final_norm(sc, grad, back, vecs, prompt, width, fence)
    dx_parts = leave_begin(exchange_heads(res[:4]), sc, prompt_row)
    for part in sums:
        part.step([dx_parts[0]])
    dx_prompt, dx_cont = leave_end(sc, *dx_parts)
    for part in sums:
        part.step([dx_prompt])
    for part in sums:
        part.step()
    g_up, g_down, g_out = pack_end(sc, [v for parts in done_pack for p in parts for v in p.finish()], width)
    g_qkv = qkv_end(sc, [v for part in done_qkv for v in part.finish()], width)

    shape = jax.ShapeDtypeStruct((4, NB, 8, D), F32)
    narrow = simple_call(
        functools.partial(narrow_kernel, width), sc, [*small, *small_qkv, res[4]], [shape], name="narrow"
    )[0]
    g_bup, g_qv, *g_vec = narrow_end(sc, *sum_small(narrow), width)
    return (
        y_prompt,
        y_cont,
        dx_prompt,
        dx_cont,
        g_qkv,
        g_qv,
        g_out,
        g_vec[0],
        g_up,
        g_bup,
        g_down,
        g_vec[1],
        g_vec[4],
        g_vec[5],
        g_vec[2],
        g_vec[3],
    )


def solution(mesh):
    dps, rows = mesh.shape["dp"], mesh.shape["row"]
    fine = Mesh(mesh.devices.reshape(dps, rows, 2, 2), ("dp", "row", "x", "core"))
    col = ("x", "core")
    both = ("dp", "row")
    tokens = P("dp", "row", col)
    narrow = P(None, col)
    wide = P(None, both, col)
    in_specs = (
        tokens,
        tokens,
        P("dp", "row"),
        P(),
        P(None, both, None, col),
        P(None, None, col),
        wide,
        narrow,
        wide,
        narrow,
        wide,
        narrow,
        narrow,
        narrow,
        narrow,
        narrow,
        tokens,
        tokens,
    )
    out_specs = (
        tokens,
        tokens,
        tokens,
        tokens,
        P(None, both, None, col),
        P(None, None, col),
        wide,
        narrow,
        wide,
        narrow,
        wide,
        narrow,
        narrow,
        narrow,
        narrow,
        narrow,
    )
    return jax.shard_map(
        per_device, mesh=fine, in_specs=in_specs, out_specs=out_specs, check_vma=False
    )
```

```python
import functools

import jax
import jax.numpy as jnp
from jax import lax
from jax.experimental import pallas as pl
from jax.experimental.pallas import tpu as pltpu
from jax.sharding import Mesh
from jax.sharding import PartitionSpec as P

D = 768
HD = 64
LAYERS = 6
NB = 3
HEADS_COL = 3
PACK = 1792
NORM_EPS = 1e-05
MASK_FILL = -1000000000.0
GELU_COEF = 0.7978845608028654
F32 = jnp.float32
BF16 = jnp.bfloat16
MIB = 1024 * 1024


def nn(a, b):
    return lax.dot_general(a, b, (((1,), (0,)), ((), ())), preferred_element_type=F32)


def nt(a, b):
    return lax.dot_general(a, b, (((1,), (1,)), ((), ())), preferred_element_type=F32)


def tn(a, b):
    return lax.dot_general(a, b, (((0,), (0,)), ((), ())), preferred_element_type=F32)


def stats(hidden):
    mean = jnp.sum(hidden, axis=1, keepdims=True) * (1.0 / D)
    square = jnp.sum(hidden * hidden, axis=1, keepdims=True) * (1.0 / D)
    inverse = lax.rsqrt(square - mean * mean + NORM_EPS)
    return (hidden - mean) * inverse, inverse


def norm_back(grad, gain, centered, inverse):
    scaled = grad * gain
    first = jnp.sum(scaled, axis=1, keepdims=True) * (1.0 / D)
    second = jnp.sum(scaled * centered, axis=1, keepdims=True) * (1.0 / D)
    return inverse * (scaled - first - centered * second)


def colsum(value):
    return jnp.sum(value, axis=0, keepdims=True)


def to_row(column):
    rows = column.shape[0]
    return jnp.transpose(jnp.broadcast_to(column, (rows, 128)))[0:1, :]


class Row:
    def __init__(self, ref, layer):
        self.ref, self.base = ref, layer * 8

    def __getitem__(self, j):
        return self.ref[self.base + j]


def strip(kernel, layer, count, deps):
    def run(sc, *refs):
        kernel(Row(sc, layer), *refs[:count], *refs[count + deps :])

    return run


def params(limit, **more):
    return pltpu.CompilerParams(vmem_limit_bytes=limit * MIB, **more)


def cost(flops, nbytes, trans=0):
    return pl.CostEstimate(flops=int(flops), bytes_accessed=int(nbytes), transcendentals=int(trans))


class Weights:

    def __init__(self, sc, packs, wout, wud, sems):
        self.sc, self.packs, self.sems = sc, packs, sems
        self.dst = ((wout, 1536, 256), (wud, 0, 1536))
        self.parts, self.size = packs[0].shape[1], packs[0].shape[2]

    def start(self, order):
        if len(self.packs) == 1:
            self.start_from(self.packs[0], order)
        else:
            for k, src in enumerate(self.packs):
                pl.when(self.sc[1] == k)(functools.partial(self.start_from, src, order))

    def start_from(self, src, order):
        for kind in order:
            dst, lo, size = self.dst[kind]
            for s in range(4):
                for j in range(self.parts):
                    rows = pl.ds(j * self.size, self.size)
                    pltpu.make_async_copy(
                        src.at[self.sc[3] ^ s, j, :, pl.ds(lo, size)],
                        dst.at[s, rows],
                        self.sems.at[kind, s],
                    ).start()

    def wait(self, kind, s):
        dst = self.dst[kind][0].at[s]
        pltpu.make_async_copy(dst, dst, self.sems.at[kind, s]).wait()


def mlp_fwd_kernel(ranks, last, prompt, sc, *refs):
    h_ref, o0, o1, o2, o3, vec_ref, bup_ref, nvec_ref = refs[:8]
    outs = refs[8 + ranks :]
    h1_ref, u_ref, h_out = outs[:3]
    wout, wud, sems = outs[-3:]
    weights = Weights(sc, refs[8 : 8 + ranks], wout, wud, sems)
    weights.start((0, 1))
    total = h_ref[...] + vec_ref[0, 0:1, :]
    for s, o_ref in enumerate((o0, o1, o2, o3)):
        weights.wait(0, s)
        total = total + nt(o_ref[...], wout[s])
    h1_ref[...] = total
    centered, _ = stats(total)
    a2 = (centered * vec_ref[0, 2:3, :] + vec_ref[0, 3:4, :]).astype(BF16)
    h_out[...] = total + vec_ref[0, 1:2, :]
    for s in range(4):
        weights.wait(1, s)
        bias = bup_ref[0, pl.ds(sc[3] ^ s, 1), 0, :]
        up = nn(a2, wud[s, :, 0:768]) + bias
        u_ref[s] = up.astype(BF16)
        act = 0.5 * up * (1.0 + jnp.tanh(GELU_COEF * (up + 0.044715 * up * up * up)))
        h_out[...] += nt(act.astype(BF16), wud[s, :, 768:1536])
    if last:
        y_refs = outs[3:7]
        send_features(sc, h_out, y_refs)
    else:
        a_ref, ap_ref = outs[3:5]
        centered, _ = stats(h_out[...])
        nxt = (centered * nvec_ref[0, 4:5, :] + nvec_ref[0, 5:6, :]).astype(BF16)
        a_ref[...] = nxt
        ap_ref[...] = nxt[:prompt]


def send_features(sc, value, refs):
    width = refs[0].shape[1]
    for s, ref in enumerate(refs):
        for c in range(4):

            def put(ref=ref, c=c):
                ref[...] = value[:, c * width : (c + 1) * width].astype(BF16)

            pl.when((sc[3] ^ s) == c)(put)


def whole_spec(shape):
    return pl.BlockSpec(shape, lambda i, sc: (0,) * len(shape))


def vec_specs(layer):
    at = layer * 8
    return [
        pl.BlockSpec((1, 8, D), lambda i, sc: (sc[at], 0, 0)),
        pl.BlockSpec((1, 4, 1, D), lambda i, sc: (sc[at], 0, 0, 0)),
        pl.BlockSpec((1, 8, D), lambda i, sc: (sc[at + 2], 0, 0)),
    ]


WSCR = [
    pltpu.VMEM((4, D, 256), BF16),
    pltpu.VMEM((4, D, 1536), BF16),
    pltpu.SemaphoreType.DMA((2, 4)),
]
ANY = pl.BlockSpec(memory_space=pl.ANY)


def mlp_fwd(layer, sc, hidden, o_parts, vecs, bup, packs, prompt, last, width, deps=()):
    tok = hidden.shape[0]
    shapes = [
        jax.ShapeDtypeStruct((tok, D), F32),
        jax.ShapeDtypeStruct((4, tok, D), BF16),
        jax.ShapeDtypeStruct((tok, D), F32),
    ]
    if last:
        shapes += [jax.ShapeDtypeStruct((tok, width), BF16)] * 4
    else:
        shapes += [jax.ShapeDtypeStruct((tok, D), BF16), jax.ShapeDtypeStruct((prompt, D), BF16)]
    out_specs = [whole_spec(v.shape) for v in shapes]
    ins = [hidden, *o_parts, vecs, bup, vecs, *packs]
    kernel = functools.partial(mlp_fwd_kernel, len(packs), last, prompt)
    return pl.pallas_call(
        strip(kernel, layer, len(ins), len(deps)),
        grid_spec=pltpu.PrefetchScalarGridSpec(
            num_scalar_prefetch=1,
            grid=(1,),
            in_specs=[whole_spec((tok, D))]
            + [whole_spec((tok, 256))] * 4
            + vec_specs(layer)
            + [ANY] * (len(packs) + len(deps)),
            out_specs=out_specs,
            scratch_shapes=WSCR,
        ),
        out_shape=shapes,
        compiler_params=params(44),
        cost_estimate=cost(2 * tok * D * 6912, 16e6, tok * 3072),
        name="mlp_fwd",
    )(sc, *ins, *deps)


def mlp_bwd_kernel(ranks, others, first, prompt, sc, *refs):
    if first:
        g_ref, refs = refs[0], refs[1:]
    else:
        nin = 4 + 2 * others
        g_ref, hn_ref, p0_ref, rx_ref = refs[:4]
        rest = refs[4:nin]
        refs = refs[nin:]
    h1_ref, u_hbm, vec_ref, nvec_ref = refs[:4]
    outs = refs[4 + ranks :]
    tok_ref, mine_ref, theirs_ref, g1_ref, d0, d1, d2, d3, small_ref = outs[:9]
    wout, wud, sems, u_ref, usem = outs[9:]
    loads = [pltpu.make_async_copy(u_hbm.at[s], u_ref.at[s], usem.at[s]) for s in range(4)]
    for copy in loads:
        copy.start()
    weights = Weights(sc, refs[4 : 4 + ranks], wout, wud, sems)
    weights.start((1, 0))
    small_ref[...] = jnp.zeros_like(small_ref)
    if first:
        grad = g_ref[...]
    else:
        g1_ref[...] = p0_ref[...].astype(F32) + rx_ref[...].astype(F32)
        for ref in rest:
            g1_ref[0:prompt, :] += ref[...].astype(F32)
        da1 = g1_ref[...]
        centered, inverse = stats(hn_ref[...])
        small_ref[8:9, :] = colsum(da1 * centered)
        small_ref[9:10, :] = colsum(da1)
        grad = g_ref[...] + norm_back(da1, nvec_ref[0, 4:5, :], centered, inverse)
    gm = grad.astype(BF16)
    tok_ref[1] = gm
    small_ref[4:5, :] = colsum(gm.astype(F32))
    for s in range(4):
        weights.wait(1, s)
        dm = nn(gm, wud[s, :, 768:1536])
        loads[s].wait()
        up = u_ref[s].astype(F32)
        square = up * up
        tanh = jnp.tanh(GELU_COEF * up * (1.0 + 0.044715 * square))
        slope = 0.5 * (1.0 + tanh) + 0.5 * up * (1.0 - tanh * tanh) * (
            GELU_COEF * (1.0 + 3.0 * 0.044715 * square)
        )
        du = (dm * slope).astype(BF16)
        side = mine_ref if s % 2 == 0 else theirs_ref
        side[s // 2] = du
        side[2 + s // 2] = (0.5 * up * (1.0 + tanh)).astype(BF16)
        small_ref[s : s + 1, :] = colsum(du.astype(F32))
        term = nt(du, wud[s, :, 0:768])
        if s == 0:
            g1_ref[...] = term
        else:
            g1_ref[...] += term
    da2 = g1_ref[...]
    centered, inverse = stats(h1_ref[...])
    gain = vec_ref[0, 2:3, :]
    tok_ref[0] = (centered * gain + vec_ref[0, 3:4, :]).astype(BF16)
    small_ref[6:7, :] = colsum(da2 * centered)
    small_ref[7:8, :] = colsum(da2)
    grad = grad + norm_back(da2, gain, centered, inverse)
    g1_ref[...] = grad
    go = grad.astype(BF16)
    tok_ref[2] = go
    small_ref[5:6, :] = colsum(go.astype(F32))
    for s, ref in enumerate((d0, d1, d2, d3)):
        weights.wait(0, s)
        ref[...] = nn(go, wout[s]).astype(BF16)


def mlp_bwd(layer, sc, grad, back, h1, up, vecs, packs, prompt, deps=()):
    tok = grad.shape[0]
    first = back is None
    others = 0 if first else len(back[3])
    shapes = [
        jax.ShapeDtypeStruct((3, tok, D), BF16),
        jax.ShapeDtypeStruct((4, tok, D), BF16),
        jax.ShapeDtypeStruct((4, tok, D), BF16),
        jax.ShapeDtypeStruct((tok, D), F32),
    ]
    shapes += [jax.ShapeDtypeStruct((tok, 256), BF16)] * 4
    shapes += [jax.ShapeDtypeStruct((16, D), F32)]
    extra = [] if first else [back[0], back[1], back[2], *back[3]]
    specs = vec_specs(layer)
    ins = [grad, *extra, h1, up, vecs, vecs, *packs]
    kernel = functools.partial(mlp_bwd_kernel, len(packs), others // 2, first, prompt)
    return pl.pallas_call(
        strip(kernel, layer, len(ins), len(deps)),
        grid_spec=pltpu.PrefetchScalarGridSpec(
            num_scalar_prefetch=1,
            grid=(1,),
            in_specs=[whole_spec(v.shape) for v in [grad, *extra, h1]]
            + [ANY, specs[0], specs[2]]
            + [ANY] * (len(packs) + len(deps)),
            out_specs=[whole_spec(s.shape) for s in shapes],
            scratch_shapes=WSCR + [pltpu.VMEM((4, tok, D), BF16), pltpu.SemaphoreType.DMA((4,))],
        ),
        out_shape=shapes,
        compiler_params=params(48),
        cost_estimate=cost(2 * tok * D * 6912, 16e6, tok * 3072),
        name="mlp_bwd",
    )(sc, *ins, *deps)


def attn_fwd_kernel(dims, sc, *refs):
    rows, piece, cpiece, chunk, cont = dims
    npc = 4 * rows
    own, oth = refs[:4], refs[4:npc]
    w_ref, b_ref, prow, pcol, crow, ccol, srow, scol = refs[npc : npc + 8]
    outs = refs[npc + 8 :]
    o_refs = outs[:4]
    q_ref, kv_ref, lse_ref, lsec_ref, m_s, l_s, acc_s = outs[4:]
    head = pl.program_id(0)
    base_b = chunk * rows
    base_c = 2 * chunk * rows
    weight = w_ref[0]
    bias = b_ref[0]
    for s in range(4):
        mixed = nn(own[s][...], weight) + bias
        low_q = (mixed[:, 0:128].astype(BF16).astype(F32) * 0.125).astype(BF16)
        low_kv = mixed[:, 128:256].astype(BF16)
        q_ref[0, s * piece : (s + 1) * piece, :] = low_q[0:piece]
        q_ref[0, chunk + s * piece : chunk + (s + 1) * piece, :] = low_q[piece : 2 * piece]
        q_ref[0, 2 * chunk + s * cpiece : 2 * chunk + (s + 1) * cpiece, :] = low_q[2 * piece :]
        kv_ref[0, s * piece : (s + 1) * piece, :] = low_kv[0:piece]
        kv_ref[0, base_b + s * piece : base_b + (s + 1) * piece, :] = low_kv[piece : 2 * piece]
        kv_ref[0, base_c + s * cpiece : base_c + (s + 1) * cpiece, :] = low_kv[2 * piece :]
    for t in range(1, rows):
        for s in range(4):
            low_kv = (nn(oth[(t - 1) * 4 + s][...], weight[:, 128:256]) + bias[:, 128:256]).astype(BF16)
            at = t * chunk + s * piece
            kv_ref[0, at : at + piece, :] = low_kv[0:piece]
            kv_ref[0, base_b + at : base_b + at + piece, :] = low_kv[piece : 2 * piece]
    lanes = lax.broadcasted_iota(jnp.int32, (1, 128), 1)
    upper = lanes >= 64
    sub = min(256, chunk)

    def begin(query, keys, mask):
        scores = nt(query, keys)
        if mask is not None:
            size = mask.shape[1]
            tail = jnp.where(mask, scores[:, -size:], MASK_FILL)
            if size == scores.shape[1]:
                scores = tail
            else:
                scores = jnp.concatenate([scores[:, :-size], tail], axis=1)
        top = jnp.max(scores, axis=1, keepdims=True)
        prob = jnp.exp(scores - top)
        return top, jnp.sum(prob, axis=1, keepdims=True), nn(prob.astype(BF16), keys)

    def put(out, row, size):
        low = jnp.where(upper, out, 0.0)

        def first_head():
            value = pltpu.roll(low, 64, 1).astype(BF16)
            store(value, row, size, 0, False)

        def second_head():
            store(low.astype(BF16), row, size, 0, True)

        def third_head():
            store(pltpu.roll(low, 64, 1).astype(BF16), row, size, 1, False)

        pl.when(head == 0)(first_head)
        pl.when(head == 1)(second_head)
        pl.when(head == 2)(third_head)

    def store(value, row, size, half, add):
        s, at = row
        lo = half * 128
        if add:
            o_refs[s][at : at + size, lo : lo + 128] = (
                o_refs[s][at : at + size, lo : lo + 128] + value
            )
        else:
            o_refs[s][at : at + size, lo : lo + 128] = value

    for i in range(chunk // sub):
        at = i * sub
        mask = prow[0:1, :] <= pcol[at : at + sub, :]
        top, total, acc = begin(q_ref[0, at : at + sub, :], kv_ref[0, 0:chunk, :], mask)
        m_s[at : at + sub, :], l_s[at : at + sub, :], acc_s[at : at + sub, :] = top, total, acc
        at_b = chunk + at
        top, total, acc = begin(
            q_ref[0, at_b : at_b + sub, :], kv_ref[0, 0 : base_b + chunk, :], mask
        )
        m_s[at_b : at_b + sub, :], l_s[at_b : at_b + sub, :] = top, total
        acc_s[at_b : at_b + sub, :] = acc
    my_row = sc[5]
    for t in range(1, rows):
        before = lax.rem(my_row + t, rows) < my_row
        q_at = jnp.where(before, 0, chunk)
        k_at = jnp.where(before, t * chunk, base_b + t * chunk)
        keys = kv_ref[0, pl.ds(pl.multiple_of(k_at, 128), chunk), :]
        for i in range(chunk // sub):
            at = pl.ds(pl.multiple_of(q_at + i * sub, 128), sub)
            scores = nt(q_ref[0, at, :], keys)
            old = m_s[at, :]
            top = jnp.maximum(old, jnp.max(scores, axis=1, keepdims=True))
            scale = jnp.exp(old - top)
            prob = jnp.exp(scores - top)
            m_s[at, :] = top
            l_s[at, :] = l_s[at, :] * scale + jnp.sum(prob, axis=1, keepdims=True)
            acc_s[at, :] = acc_s[at, :] * scale + nn(prob.astype(BF16), keys)
    for half in range(2):
        for s in range(4):
            at = half * chunk + s * piece
            total = l_s[at : at + piece, :]
            put(acc_s[at : at + piece, :] / total, (s, half * piece), piece)
        for i in range(chunk // sub):
            at = half * chunk + i * sub
            column = m_s[at : at + sub, :] + jnp.log(l_s[at : at + sub, :])
            lse_ref[0, half, :, i * sub : (i + 1) * sub] = to_row(column)
    mask = (crow[0:1, :] <= ccol[...]) & (srow[0:1, :] == scol[...])
    query = q_ref[0, 2 * chunk : 2 * chunk + cont, :]
    top, total, acc = begin(query, kv_ref[0], mask)
    out = acc / total
    for s in range(4):
        put(out[s * cpiece : (s + 1) * cpiece], (s, 2 * piece), cpiece)
    lsec_ref[0] = to_row(top + jnp.log(total))


def attn_inputs(pos):
    return [pl.BlockSpec(v.shape, lambda i, sc: (0, 0)) for v in pos]


def attn_fwd(layer, sc, own, oth, w_all, b_all, pos, dims, deps=()):
    single = w_all.shape[0] == 1
    rows, piece, cpiece, chunk, cont = dims
    tok = own[0].shape[0]
    nq, nk = 2 * chunk + cont, 2 * chunk * rows + cont
    shapes = [jax.ShapeDtypeStruct((tok, 256), BF16)] * 4 + [
        jax.ShapeDtypeStruct((3, nq, 128), BF16),
        jax.ShapeDtypeStruct((3, nk, 128), BF16),
        jax.ShapeDtypeStruct((3, 2, 1, chunk), F32),
        jax.ShapeDtypeStruct((3, 1, cont), F32),
    ]
    out_specs = [whole_spec((tok, 256))] * 4 + [
        pl.BlockSpec((1, nq, 128), lambda i, sc: (i, 0, 0)),
        pl.BlockSpec((1, nk, 128), lambda i, sc: (i, 0, 0)),
        pl.BlockSpec((1, 2, 1, chunk), lambda i, sc: (i, 0, 0, 0)),
        pl.BlockSpec((1, 1, cont), lambda i, sc: (i, 0, 0)),
    ]
    at = layer * 8
    count = len(own) + len(oth) + 2 + len(pos)
    return pl.pallas_call(
        strip(functools.partial(attn_fwd_kernel, dims), layer, count, len(deps)),
        grid_spec=pltpu.PrefetchScalarGridSpec(
            num_scalar_prefetch=1,
            grid=(3,),
            in_specs=[whole_spec(v.shape) for v in [*own, *oth]]
            + [
                pl.BlockSpec((1, D, 256), lambda i, sc: (0 if single else sc[at + 1], 0, i)),
                pl.BlockSpec((1, 1, 256), lambda i, sc: (sc[at], 0, i)),
            ]
            + attn_inputs(pos)
            + [ANY] * len(deps),
            out_specs=out_specs,
            scratch_shapes=[
                pltpu.VMEM((2 * chunk, 1), F32),
                pltpu.VMEM((2 * chunk, 1), F32),
                pltpu.VMEM((2 * chunk, 128), F32),
            ],
        ),
        out_shape=shapes,
        compiler_params=params(52),
        cost_estimate=cost(2 * nq * D * 768 * 2 + 8 * 3 * nq * nk * 64, 12e6, 3 * nq * nk),
        name="attn_fwd",
    )(sc, *own, *oth, w_all, b_all, *pos, *deps)


def attn_bwd_kernel(dims, sc, *refs):
    rows, piece, cpiece, chunk, cont = dims
    do_refs, o_refs = refs[:4], refs[4:8]
    q_ref, kv_ref, lse_ref, lsec_ref, w_ref = refs[8:13]
    prow, pcol, crow, ccol, srow, scol = refs[13:19]
    outs = refs[19:]
    npc = 4 * rows
    mine_out, theirs_out = outs[:2]
    dq_out, dkv_out, bias_out = outs[2:5]
    do_s, drow, drowc, dq_s, dkv_s, da_s = outs[5:]
    head = pl.program_id(0)
    base_b = chunk * rows
    base_c = 2 * chunk * rows
    tok = 2 * piece + cpiece
    upper = lax.broadcasted_iota(jnp.int32, (1, 128), 1) >= 64

    def take(ref):
        value = ref[...].astype(F32)
        left, right = value[:, 0:128], value[:, 128:256]
        pick = jnp.where(head == 2, pltpu.roll(right, 64, 1), left)
        pick = jnp.where(head == 0, pltpu.roll(left, 64, 1), pick)
        return jnp.where(upper, pick, 0.0)

    for s in range(4):
        dout = take(do_refs[s])
        low = dout.astype(BF16)
        do_s[s * piece : (s + 1) * piece, :] = low[0:piece]
        do_s[chunk + s * piece : chunk + (s + 1) * piece, :] = low[piece : 2 * piece]
        do_s[2 * chunk + s * cpiece : 2 * chunk + (s + 1) * cpiece, :] = low[2 * piece :]
        dot = dout * take(o_refs[s])
        dq_s[s * piece : (s + 1) * piece, :] = dot[0:piece]
        dq_s[chunk + s * piece : chunk + (s + 1) * piece, :] = dot[piece : 2 * piece]
        dq_s[2 * chunk + s * cpiece : 2 * chunk + (s + 1) * cpiece, :] = dot[2 * piece :]
    sub = min(128, chunk)
    for half in range(2):
        for i in range(chunk // sub):
            at = half * chunk + i * sub
            column = jnp.sum(dq_s[at : at + sub, :], axis=1, keepdims=True)
            drow[half, :, i * sub : (i + 1) * sub] = to_row(column)
    column = jnp.sum(dq_s[2 * chunk :, :], axis=1, keepdims=True)
    drowc[...] = to_row(column)
    dq_s[...] = jnp.zeros_like(dq_s)
    dkv_s[...] = jnp.zeros_like(dkv_s)

    def pair(q_at, k_at, lse, dot, mask):
        query = q_ref[0, q_at, :]
        keys = kv_ref[0, k_at, :]
        dout = do_s[q_at, :]
        prob = jnp.exp(nt(keys, query) - lse)
        if mask is not None:
            prob = jnp.where(mask, prob, 0.0)
        dprob = nt(keys, dout)
        dscore = (prob * (dprob - dot)).astype(BF16)
        dkv_s[k_at, :] += nn(prob.astype(BF16), dout) + nn(dscore, query)
        dq_s[q_at, :] += tn(dscore, keys)

    kb = min(512, chunk)
    at_a, at_b = pl.ds(0, chunk), pl.ds(chunk, chunk)
    lse_a, lse_b, dot_a, dot_b = lse_ref[0, 0], lse_ref[0, 1], drow[0], drow[1]
    for j in range(chunk // kb):
        mask = pcol[j * kb : (j + 1) * kb, :] <= prow[0:1, :]
        pair(at_a, pl.ds(j * kb, kb), lse_a, dot_a, mask)
        pair(at_b, pl.ds(base_b + j * kb, kb), lse_b, dot_b, mask)
    for j in range(base_b // kb):
        pair(at_b, pl.ds(j * kb, kb), lse_b, dot_b, None)
    my_row = sc[5]
    for t in range(1, rows):
        before = lax.rem(my_row + t, rows) < my_row
        which = jnp.where(before, 0, 1)
        q_at = pl.ds(pl.multiple_of(which * chunk, 128), chunk)
        k_base = jnp.where(before, t * chunk, base_b + t * chunk)
        for j in range(chunk // kb):
            k_at = pl.ds(pl.multiple_of(k_base + j * kb, 128), kb)
            pair(q_at, k_at, lse_ref[0, which], drow[which], None)
    at_c = pl.ds(2 * chunk, cont)
    for j in range(base_c // 512):
        pair(at_c, pl.ds(j * 512, 512), lsec_ref[0], drowc[...], None)
    mask = (ccol[...] <= crow[0:1, :]) & (scol[...] == srow[0:1, :])
    pair(at_c, pl.ds(base_c, cont), lsec_ref[0], drowc[...], mask)

    weight = w_ref[0]
    lower = jnp.logical_not(upper)
    dq_all = jnp.where(lower, dq_s[...] * 0.125, 0.0).astype(BF16)
    q_sum = colsum(dq_all.astype(F32))
    kv_sum = jnp.zeros((1, 128), F32)

    def gather3(value, where):
        return jnp.concatenate([value[a : a + n] for a, n in where], axis=0)

    def emit(slot, count, ref, row, term):
        at = pl.ds(slot, count)

        def set_first():
            da_s[at, :] = term

        def add_next():
            da_s[at, :] += term

        def finish():
            ref[row : row + count, :] = (da_s[at, :] + term).astype(BF16)

        pl.when(head == 0)(set_first)
        pl.when(head == 1)(add_next)
        pl.when(head == 2)(finish)

    for s in range(4):
        dq = gather3(
            dq_all,
            [(s * piece, piece), (chunk + s * piece, piece), (2 * chunk + s * cpiece, cpiece)],
        )
        dkv = jnp.concatenate(
            [
                dkv_s[s * piece : (s + 1) * piece, :],
                dkv_s[base_b + s * piece : base_b + (s + 1) * piece, :],
                dkv_s[base_c + s * cpiece : base_c + (s + 1) * cpiece, :],
            ],
            axis=0,
        ).astype(BF16)
        kv_sum = kv_sum + colsum(dkv.astype(F32))
        both = jnp.concatenate([dq, dkv], axis=1)
        dq_out[s, 0] = both
        side = mine_out if s % 2 == 0 else theirs_out
        emit(s * tok, tok, side, (s // 2) * tok, nt(both, weight))
    for t in range(1, rows):
        for s in range(4):
            at = t * chunk + s * piece
            dkv = jnp.concatenate(
                [dkv_s[at : at + piece, :], dkv_s[base_b + at : base_b + at + piece, :]], axis=0
            ).astype(BF16)
            kv_sum = kv_sum + colsum(dkv.astype(F32))
            k = (t - 1) * 4 + s
            dkv_out[k, 0] = dkv
            side = mine_out if s % 2 == 0 else theirs_out
            row = 2 * tok + (k // 2) * 2 * piece
            emit(4 * tok + k * 2 * piece, 2 * piece, side, row, nt(dkv, weight[:, 128:256]))
    bias_out[0] = jnp.broadcast_to(jnp.concatenate([q_sum, kv_sum], axis=1), (8, 256))


def attn_bwd(layer, sc, do_parts, o_parts, q, kv, lse, lsec, w_all, pos, dims, deps=()):
    rows, piece, cpiece, chunk, cont = dims
    tok = 2 * piece + cpiece
    nq, nk = 2 * chunk + cont, 2 * chunk * rows + cont
    noth = 4 * (rows - 1)
    shapes = (
        [jax.ShapeDtypeStruct((2 * tok + noth * piece, D), BF16)] * 2
        + [
            jax.ShapeDtypeStruct((4, 3, tok, 256), BF16),
            jax.ShapeDtypeStruct((noth, 3, 2 * piece, 128), BF16),
            jax.ShapeDtypeStruct((3, 8, 256), F32),
        ]
    )
    out_specs = [whole_spec(s.shape) for s in shapes[:2]] + [
        pl.BlockSpec((4, 1, tok, 256), lambda i, sc: (0, i, 0, 0)),
        pl.BlockSpec((noth, 1, 2 * piece, 128), lambda i, sc: (0, i, 0, 0)),
        pl.BlockSpec((1, 8, 256), lambda i, sc: (i, 0, 0)),
    ]
    at = layer * 8
    return pl.pallas_call(
        strip(functools.partial(attn_bwd_kernel, dims), layer, 13 + len(pos), len(deps)),
        grid_spec=pltpu.PrefetchScalarGridSpec(
            num_scalar_prefetch=1,
            grid=(3,),
            in_specs=[whole_spec((tok, 256))] * 8
            + [
                pl.BlockSpec((1, nq, 128), lambda i, sc: (i, 0, 0)),
                pl.BlockSpec((1, nk, 128), lambda i, sc: (i, 0, 0)),
                pl.BlockSpec((1, 2, 1, chunk), lambda i, sc: (i, 0, 0, 0)),
                pl.BlockSpec((1, 1, cont), lambda i, sc: (i, 0, 0)),
                pl.BlockSpec((1, D, 256), lambda i, sc: (sc[at + 1], 0, i)),
            ]
            + attn_inputs(pos)
            + [ANY] * len(deps),
            out_specs=out_specs,
            scratch_shapes=[
                pltpu.VMEM((nq, 128), BF16),
                pltpu.VMEM((2, 1, chunk), F32),
                pltpu.VMEM((1, cont), F32),
                pltpu.VMEM((nq, 128), F32),
                pltpu.VMEM((nk, 128), F32),
                pltpu.VMEM((4 * tok + noth * 2 * piece, D), F32),
            ],
        ),
        out_shape=shapes,
        compiler_params=params(56),
        cost_estimate=cost(2 * nq * D * 768 * 2 + 20 * 3 * nq * nk * 64, 14e6, 3 * nq * nk),
        name="attn_bwd",
    )(sc, *do_parts, *o_parts, q, kv, lse, lsec, w_all, *pos, *deps)


def dw_qkv_kernel(rows, sc, *refs):
    npc = 4 * rows
    noth = npc - 4
    srcs, (dq_hbm, dkv_hbm) = refs[:npc], refs[npc : npc + 2]
    new_ref, token = refs[npc + 2 : npc + 4]
    own, oth, dq_s, dkv_s, asem, dsem = refs[npc + 4 :]
    token[...] = jnp.zeros_like(token)
    head = pl.program_id(0)

    def rows_of(k):
        dst = own.at[k] if k < 4 else oth.at[k - 4]
        return pltpu.make_async_copy(srcs[k], dst, asem.at[k])

    def grads_of(h):
        return [
            pltpu.make_async_copy(dq_hbm.at[:, h], dq_s.at[:, h], dsem.at[0, h]),
            pltpu.make_async_copy(dkv_hbm.at[:, h], dkv_s.at[:, h], dsem.at[1, h]),
        ]

    def begin():
        for copy in grads_of(0):
            copy.start()
        for k in range(npc):
            rows_of(k).start()
        for h in (1, 2):
            for copy in grads_of(h):
                copy.start()
        for k in range(npc):
            rows_of(k).wait()

    pl.when(head == 0)(begin)
    for copy in grads_of(head):
        copy.wait()
    total = tn(own[0], dq_s[0, head])
    for s in range(1, 4):
        total = total + tn(own[s], dq_s[s, head])
    right = tn(oth[0], dkv_s[0, head])
    for k in range(1, noth):
        right = right + tn(oth[k], dkv_s[k, head])
    new_ref[:, 0:128] = total[:, 0:128].astype(BF16)
    new_ref[:, 128:256] = (total[:, 128:256] + right).astype(BF16)


def dw_qkv(layer, sc, own, oth, dq, dkv, deps=()):
    rows = (4 + len(oth)) // 4
    tok, two = own[0].shape[0], oth[0].shape[0]
    noth = len(oth)
    ins = [*own, *oth, dq, dkv]
    return pl.pallas_call(
        strip(functools.partial(dw_qkv_kernel, rows), layer, len(ins), len(deps)),
        grid_spec=pltpu.PrefetchScalarGridSpec(
            num_scalar_prefetch=1,
            grid=(3,),
            in_specs=[ANY] * len(ins) + [ANY] * len(deps),
            out_specs=[pl.BlockSpec((D, 256), lambda i, sc: (0, i)), whole_spec((8, 128))],
            scratch_shapes=[
                pltpu.VMEM((4, tok, D), BF16),
                pltpu.VMEM((noth, two, D), BF16),
                pltpu.VMEM((4, 3, tok, 256), BF16),
                pltpu.VMEM((noth, 3, two, 128), BF16),
                pltpu.SemaphoreType.DMA((4 * rows,)),
                pltpu.SemaphoreType.DMA((2, 3)),
            ],
        ),
        out_shape=[
            jax.ShapeDtypeStruct((D, D), BF16),
            jax.ShapeDtypeStruct((8, 128), F32),
        ],
        compiler_params=params(56),
        cost_estimate=cost(2 * 3 * D * (4 * tok * 256 + noth * two * 128), 10e6),
        name="dw_qkv",
    )(sc, *ins, *deps)


class Loads:

    def __init__(self, refs, tok, side, outp, sems):
        tok_m, tok_r, mine, got, o0, o2, r1, r3 = refs
        size = tok_m.shape[1]
        low, high = pl.ds(0, size), pl.ds(size, size)
        pairs = {}
        for k in range(3):
            pairs["tok", k] = [(tok_m.at[k], tok.at[k, low]), (tok_r.at[k], tok.at[k, high])]
        for k in range(4):
            pairs["side", k] = [(mine.at[k], side.at[k, low]), (got.at[k], side.at[k, high])]
        pairs["outp", 0] = [(o0, outp.at[0, low]), (r1, outp.at[0, high])]
        pairs["outp", 1] = [(o2, outp.at[1, low]), (r3, outp.at[1, high])]
        self.copies, n = {}, 0
        for key, both in pairs.items():
            self.copies[key] = []
            for a, b in both:
                self.copies[key].append(pltpu.make_async_copy(a, b, sems.at[n]))
                n += 1

    def start(self):
        first = [("tok", 0), ("side", 0), ("tok", 1), ("side", 2), ("tok", 2), ("outp", 0)]
        for key in [*first, ("side", 1), ("side", 3), ("outp", 1)]:
            for copy in self.copies[key]:
                copy.start()

    def wait(self, *key):
        for copy in self.copies[key]:
            copy.wait()

    def wait_tile(self, tile, name, index):
        tokens = {"up": 0, "down": 1, "out": 2}[index]

        def first():
            self.wait("tok", tokens)
            self.wait(name, 2 if index == "down" else 0)

        pl.when(tile == 0)(first)
        pl.when(tile == 1)(lambda: self.wait(name, 3 if index == "down" else 1))


def dw_products(tile, loads, tok, side, outp, put):
    loads.wait_tile(tile, "side", "up")
    for j in range(3):
        put(j * 256, tn(tok[0], side[tile, :, j * 256 : (j + 1) * 256]))
    loads.wait_tile(tile, "side", "down")
    for j in range(3):
        put(768 + j * 256, tn(tok[1], side[2 + tile, :, j * 256 : (j + 1) * 256]))
    loads.wait_tile(tile, "outp", "out")
    put(1536, tn(tok[2], outp[tile]))


def dw_mlp_kernel(sc, *refs):
    old_ref, new_ref, token = refs[8:11]
    tok, side, outp, sems = refs[11:]
    token[...] = jnp.zeros_like(token)
    tile = pl.program_id(0)
    keep = sc[6] == 0

    loads = Loads(refs[:8], tok, side, outp, sems)
    pl.when(tile == 0)(loads.start)

    def put(lo, value):
        size = value.shape[1]
        old = old_ref[0, 0, :, lo : lo + size].astype(F32)
        new_ref[0, 0, :, lo : lo + size] = (value + jnp.where(keep, old, 0.0)).astype(BF16)

    dw_products(tile, loads, tok, side, outp, put)


def dw_scratch(tok):
    return [
        pltpu.VMEM((3, 2 * tok, D), BF16),
        pltpu.VMEM((4, 2 * tok, D), BF16),
        pltpu.VMEM((2, 2 * tok, 256), BF16),
        pltpu.SemaphoreType.DMA((18,)),
    ]


def dw_mlp(layer, sc, ins, acc, deps=()):
    tok = ins[0].shape[1]
    at = layer * 8
    acc_spec = pl.BlockSpec((1, 1, D, PACK), lambda i, sc: (sc[at + 1], i, 0, 0))
    return pl.pallas_call(
        strip(dw_mlp_kernel, layer, 9, len(deps)),
        grid_spec=pltpu.PrefetchScalarGridSpec(
            num_scalar_prefetch=1,
            grid=(2,),
            in_specs=[ANY] * 8 + [acc_spec] + [ANY] * len(deps),
            out_specs=[acc_spec, whole_spec((8, 128))],
            scratch_shapes=dw_scratch(tok),
        ),
        out_shape=[jax.ShapeDtypeStruct(acc.shape, acc.dtype), jax.ShapeDtypeStruct((8, 128), F32)],
        input_output_aliases={9: 0},
        compiler_params=params(56),
        cost_estimate=cost(2 * tok * D * 4 * PACK, 20e6),
        name="dw_mlp",
    )(sc, *ins, acc, *deps)


def dw_last_kernel(rank, groups, slot, sc, *refs):
    keep_a, give_a, keep_b, give_b, acc, token = refs[9:15]
    tok, side, outp, sems, done, other, dsem, osem, out_a, out_b, asem, bsem = refs[15:]
    token[...] = jnp.zeros_like(token)
    tile = pl.program_id(0)
    same = sc[1] == rank
    keep = sc[6] == 0
    used = jnp.logical_or(jnp.logical_not(same), keep)

    def load(t):
        return pltpu.make_async_copy(acc.at[rank, t], done.at[t], dsem.at[t])

    loads = Loads(refs[:8], tok, side, outp, sems)

    def begin():
        loads.start()
        load(0).start()
        load(1).start()

    pl.when(tile == 0)(begin)
    load(tile).wait()

    def fetch_other():
        copy = pltpu.make_async_copy(acc.at[sc[1], tile], other, osem)
        copy.start()
        copy.wait()

    pl.when(jnp.logical_not(same))(fetch_other)

    def put(lo, value):
        size = value.shape[1]
        cols = slice(lo, lo + size)
        old = jnp.where(used, done[tile, :, cols].astype(F32), 0.0)
        total = (old + jnp.where(same, value, 0.0)).astype(BF16)
        if lo < D:
            out_a[tile, :, cols] = total
        else:
            out_b[tile, :, lo - D : lo - D + size] = total

        def add_other():
            before = jnp.where(keep, other[:, cols].astype(F32), 0.0)
            other[:, cols] = (value + before).astype(BF16)

        pl.when(jnp.logical_not(same))(add_other)

    dw_products(tile, loads, tok, side, outp, put)

    def store_other():
        copy = pltpu.make_async_copy(other, acc.at[sc[1], tile], osem)
        copy.start()
        copy.wait()

    pl.when(jnp.logical_not(same))(store_other)
    size = D // (2 * groups)
    bit = sc[slot]

    def copies(t):
        both = [pltpu.make_async_copy(out_a.at[t], (keep_a, give_a)[t], asem.at[t])]
        for g in range(groups):
            for k, (ref, part) in enumerate(((keep_b, bit), (give_b, 1 - bit))):
                src = pl.ds(pl.multiple_of((2 * g + part) * size, size), size)
                dst = pl.ds((t * groups + g) * size, size)
                both.append(pltpu.make_async_copy(out_b.at[t, src], ref.at[dst], bsem.at[t, 2 * g + k]))
        return both

    def leave(t):
        for copy in copies(t):
            copy.start()

    pl.when(tile == 0)(functools.partial(leave, 0))

    def finish():
        leave(1)
        for t in range(2):
            for copy in copies(t):
                copy.wait()

    pl.when(tile == 1)(finish)


def dw_last(layer, sc, ins, acc, groups, deps=()):
    tok = ins[0].shape[1]
    slot = LAYERS * 8 + 1 + len(bits_of("dp")) - layer * 8
    halves = [jax.ShapeDtypeStruct((D, n), BF16) for n in (D, D, PACK - D, PACK - D)]
    return pl.pallas_call(
        strip(functools.partial(dw_last_kernel, layer, groups, slot), layer, 9, len(deps)),
        grid_spec=pltpu.PrefetchScalarGridSpec(
            num_scalar_prefetch=1,
            grid=(2,),
            in_specs=[ANY] * 9 + [ANY] * len(deps),
            out_specs=[ANY] * 4 + [ANY, whole_spec((8, 128))],
            scratch_shapes=dw_scratch(tok)
            + [
                pltpu.VMEM((2, D, PACK), BF16),
                pltpu.VMEM((D, PACK), BF16),
                pltpu.SemaphoreType.DMA((2,)),
                pltpu.SemaphoreType.DMA(()),
                pltpu.VMEM((2, D, D), BF16),
                pltpu.VMEM((2, D, PACK - D), BF16),
                pltpu.SemaphoreType.DMA((2,)),
                pltpu.SemaphoreType.DMA((2, 2 * groups)),
            ],
        ),
        out_shape=halves
        + [
            jax.ShapeDtypeStruct(acc.shape, acc.dtype),
            jax.ShapeDtypeStruct((8, 128), F32),
        ],
        input_output_aliases={9: 4},
        compiler_params=params(56),
        cost_estimate=cost(2 * tok * D * 4 * PACK, 20e6),
        name="dw_last",
    )(sc, *ins, acc, *deps)


def qkv_total(sc, rank, parts, groups, deps):
    size = D // (2 * groups)
    slot = LAYERS * 8 + 1 + len(bits_of("dp"))

    def add(sc, *refs):
        keep, give = refs[-2:]
        bit = sc[slot]
        for g in range(groups):
            for out, side in ((keep, bit), (give, 1 - bit)):
                at = pl.ds(pl.multiple_of((2 * g + side) * size, size), size)
                total = jnp.zeros((size, D), F32)
                for k, ref in enumerate(refs[:-2]):
                    used = sc[(rank + k) * 8 + 1] == rank
                    total = total + jnp.where(used, ref[at, :].astype(F32), 0.0)
                out[g * size : (g + 1) * size, :] = total.astype(BF16)

    shape = jax.ShapeDtypeStruct((D // 2, D), BF16)
    return simple_call(add, sc, parts, [shape] * 2, name="qkv_total", deps=deps)


def blank(shape, dtype):
    def body(out):
        del out

    return pl.pallas_call(
        body,
        out_shape=jax.ShapeDtypeStruct(shape, dtype),
        out_specs=pl.BlockSpec(memory_space=pl.ANY),
        name="blank",
    )()


SWAP = [(0, 1), (1, 0)]


def swap_core(value):
    return lax.ppermute(value, "core", SWAP)


def swap_x(value):
    return lax.ppermute(value, "x", SWAP)


def shift_row(value, t):
    rows = lax.axis_size("row")
    return lax.ppermute(value, "row", [(i, (i - t) % rows) for i in range(rows)])


def shift_row_x(value, t):
    rows = lax.axis_size("row")
    pairs = [(i * 2 + j, ((i - t) % rows) * 2 + (1 - j)) for i in range(rows) for j in range(2)]
    return lax.ppermute(value, ("row", "x"), pairs)


def spread(low, low_prompt):
    rows = lax.axis_size("row")
    from_x = swap_x(low)
    far = []
    for t in range(1, rows):
        far += [shift_row(low_prompt, t), shift_row_x(low_prompt, t)]
    own = [low, swap_core(low), from_x, swap_core(from_x)]
    oth = []
    for t in range(1, rows):
        near, diag = far[2 * t - 2], far[2 * t - 1]
        oth += [near, swap_core(near), diag, swap_core(diag)]
    return own, oth


def exchange_heads(parts):
    flip = {1: [1, 0, 3, 2], 2: [2, 3, 0, 1], 3: [3, 2, 1, 0]}
    out = [parts[0]]
    for s in (1, 2, 3):
        pairs = [(c, flip[s][c]) for c in range(4)]
        out.append(lax.ppermute(parts[s], ("x", "core"), pairs))
    return out


def add_low(a, b):
    return (a.astype(F32) + b.astype(F32)).astype(BF16)


def sum_kernel(sizes, a, b, *outs):
    at = 0
    for size, out in zip(sizes, outs):
        out[...] = add_low(a[at : at + size, :], b[at : at + size, :])
        at += size


def collect(mine, theirs, tok, prompt, deps=()):
    rows = lax.axis_size("row")
    sizes = [tok, tok] + [prompt] * (2 * (rows - 1))
    vmem = pl.BlockSpec(memory_space=pltpu.VMEM)
    count = len(deps)
    sums = pl.pallas_call(
        lambda a, b, *refs: sum_kernel(sizes, a, b, *refs[count:]),
        in_specs=[vmem] * 2 + [ANY] * count,
        out_specs=[vmem] * len(sizes),
        out_shape=[jax.ShapeDtypeStruct((n, D), BF16) for n in sizes],
        compiler_params=params(24),
        cost_estimate=cost(1e6, 4e6),
        name="sum_cores",
    )(mine, swap_core(theirs), *deps)
    got = swap_x(sums[1])
    rest = []
    for t in range(1, rows):
        rest += [shift_row(sums[2 * t], -t), shift_row_x(sums[2 * t + 1], -t)]
    return sums[0], got, rest


def behind(values, deps):
    if not deps:
        return list(values)
    count = len(values)

    def body(*refs):
        del refs

    return pl.pallas_call(
        body,
        in_specs=[ANY] * (count + len(deps)),
        out_specs=[ANY] * count,
        out_shape=[jax.ShapeDtypeStruct(v.shape, v.dtype) for v in values],
        input_output_aliases={k: k for k in range(count)},
        name="behind",
    )(*values, *deps)


def held(value, deps):
    def body(src, *rest):
        rest[-1][...] = src[...]

    vmem = pl.BlockSpec(memory_space=pltpu.VMEM)
    return pl.pallas_call(
        body,
        in_specs=[vmem] + [ANY] * len(deps),
        out_specs=vmem,
        out_shape=jax.ShapeDtypeStruct(value.shape, value.dtype),
        name="held",
    )(value, *deps)


def gather_begin(value, names):
    total = 1
    for a in names:
        total *= lax.axis_size(a)
    return [lax.ppermute(value, names, [(i, i ^ t) for i in range(total)]) for t in range(1, total)]


def gather_end(sc, pieces, index, ahead=(), deps=()):
    lead, n, width = pieces[0].shape
    count = len(pieces)

    def place(sc, *refs):
        out = refs[-1]
        for block in refs[count:-1]:
            out[0:1] = block[...]
        base = len(ahead)
        for t in range(count):
            at = pl.ds(pl.multiple_of((sc[index] ^ t) * n, n), n)
            out[base : base + lead, at, :] = refs[t][...]

    shape = jax.ShapeDtypeStruct((lead + len(ahead), count * n, width), BF16)
    return simple_call(place, sc, [*pieces, *ahead], [shape], name="place", deps=deps)[0]


def zig(j, rows):
    return j if j < rows else 2 * rows - 1 - j


def split_kernel(piece, cpiece, sc, even, odd, cont, *outs):
    for s, out in enumerate(outs):
        place = sc[3] ^ s
        at = pl.ds(pl.multiple_of(place * piece, piece), piece)

        def fill(first, second, out=out, at=at):
            out[0:piece, :] = first[at, :]
            out[piece : 2 * piece, :] = second[at, :]

        pl.when(sc[7] == 0)(functools.partial(fill, even, odd))
        pl.when(sc[7] == 1)(functools.partial(fill, odd, even))
        out[2 * piece :, :] = cont[pl.ds(pl.multiple_of(place * cpiece, cpiece), cpiece), :]


def merge_kernel(piece, cpiece, sc, p0, p1, p2, p3, even, odd, cont):
    for s, part in enumerate((p0, p1, p2, p3)):
        place = sc[3] ^ s
        at = pl.ds(pl.multiple_of(place * piece, piece), piece)

        def fill(first, second, part=part, at=at):
            first[at, :] = part[0:piece, :]
            second[at, :] = part[piece : 2 * piece, :]

        pl.when(sc[7] == 0)(functools.partial(fill, even, odd))
        pl.when(sc[7] == 1)(functools.partial(fill, odd, even))
        cont[pl.ds(pl.multiple_of(place * cpiece, cpiece), cpiece), :] = part[2 * piece :, :]


def join_kernel(prompt, normed, sc, p0, p1, p2, p3, vec_ref, h_ref, *outs):
    width = p0.shape[1]
    for s, part in enumerate((p0, p1, p2, p3)):
        value = part[...].astype(F32)
        for c in range(4):

            def put(value=value, c=c):
                h_ref[:, c * width : (c + 1) * width] = value

            pl.when((sc[3] ^ s) == c)(put)
    if normed:
        a_ref, ap_ref = outs
        centered, _ = stats(h_ref[...])
        low = (centered * vec_ref[0, 4:5, :] + vec_ref[0, 5:6, :]).astype(BF16)
        a_ref[...] = low
        ap_ref[...] = low[:prompt]


def simple_call(kernel, sc, ins, shapes, specs=None, name="small", deps=()):
    return pl.pallas_call(
        strip(kernel, 0, len(ins), len(deps)),
        grid_spec=pltpu.PrefetchScalarGridSpec(
            num_scalar_prefetch=1,
            grid=(1,),
            in_specs=(specs or [whole_spec(v.shape) for v in ins]) + [ANY] * len(deps),
            out_specs=[whole_spec(v.shape) for v in shapes],
        ),
        out_shape=shapes,
        compiler_params=params(24),
        cost_estimate=cost(1e6, 3e6),
        name=name,
    )(sc, *ins, *deps)


def enter(prompt, cont, sc, vecs, normed):
    parts = enter_begin(prompt, cont, sc)
    return parts, enter_end(exchange_heads(parts), sc, vecs, normed, prompt.shape[0] // 4)


def enter_begin(prompt, cont, sc, deps=()):
    rows = lax.axis_size("row")
    half, width = prompt.shape[0] // 2, prompt.shape[1]
    piece, cpiece = half // 4, cont.shape[0] // 4
    tok = 2 * piece + cpiece
    even = prompt[:half]
    odd = prompt[half:]
    if rows > 2:
        even = lax.ppermute(even, "row", [(i, zig(2 * i, rows)) for i in range(rows)])
    odd = lax.ppermute(odd, "row", [(i, zig(2 * i + 1, rows)) for i in range(rows)])
    part = jax.ShapeDtypeStruct((tok, width), BF16)
    parts = simple_call(
        functools.partial(split_kernel, piece, cpiece), sc, [even, odd, cont], [part] * 4, name="split", deps=deps
    )
    return parts


def enter_end(parts, sc, vecs, normed, prompt, deps=()):
    tok, width = parts[0].shape
    shapes = [jax.ShapeDtypeStruct((tok, D), F32)]
    if normed:
        shapes += [jax.ShapeDtypeStruct((tok, D), BF16), jax.ShapeDtypeStruct((prompt, D), BF16)]
    specs = [whole_spec((tok, width))] * 4 + [pl.BlockSpec((1, 8, D), lambda i, sc: (sc[0], 0, 0))]
    return simple_call(
        functools.partial(join_kernel, prompt, normed), sc, [*parts, vecs], shapes, specs, "join", deps
    )


def leave(parts, sc, prompt_rows):
    return leave_end(sc, *leave_begin(exchange_heads(parts), sc, prompt_rows))


def leave_begin(parts, sc, prompt_rows, deps=()):
    width = parts[0].shape[1]
    half = prompt_rows // 2
    piece = half // 4
    cpiece = parts[0].shape[0] - 2 * piece
    shapes = [jax.ShapeDtypeStruct((n, width), BF16) for n in (half, half, 4 * cpiece)]
    even, odd, cont = simple_call(
        functools.partial(merge_kernel, piece, cpiece), sc, parts, shapes, name="merge", deps=deps
    )
    return even, odd, cont


def leave_end(sc, even, odd, cont, deps=()):
    rows = lax.axis_size("row")
    if rows > 2:
        even = lax.ppermute(even, "row", [(zig(2 * i, rows), i) for i in range(rows)])
    odd = lax.ppermute(odd, "row", [(zig(2 * i + 1, rows), i) for i in range(rows)])
    half, width = even.shape

    def stack(sc, first, second, out):
        out[0, 0:half, :] = first[...]
        out[0, half:, :] = second[...]

    shape = jax.ShapeDtypeStruct((1, 2 * half, width), BF16)
    return simple_call(stack, sc, [even, odd], [shape], name="rows", deps=deps)[0], cont[None]


def final_kernel(prompt, others, sc, *refs):
    g_ref, h_ref, p0_ref, rx_ref = refs[:4]
    rest = refs[4 : 4 + others]
    vec_ref = refs[4 + others]
    outs, small, da_ref, out_ref = refs[5 + others : 9 + others], refs[9 + others], refs[10 + others], refs[11 + others]
    da_ref[...] = p0_ref[...].astype(F32) + rx_ref[...].astype(F32)
    for ref in rest:
        da_ref[0:prompt, :] += ref[...].astype(F32)
    da1 = da_ref[...]
    centered, inverse = stats(h_ref[...])
    small[0:1, :] = colsum(da1 * centered)
    small[1:2, :] = colsum(da1)
    out_ref[...] = g_ref[...] + norm_back(da1, vec_ref[0, 4:5, :], centered, inverse)
    send_features(sc, out_ref, outs)


def final_norm(sc, grad, back, vecs, prompt, width, deps):
    tok = grad.shape[0]
    h_in, base, got, rest = back
    ins = [grad, h_in, base, got, *rest, vecs]
    shapes = [jax.ShapeDtypeStruct((tok, width), BF16)] * 4 + [
        jax.ShapeDtypeStruct((8, D), F32),
        jax.ShapeDtypeStruct((tok, D), F32),
        jax.ShapeDtypeStruct((tok, D), F32),
    ]
    specs = [whole_spec(v.shape) for v in ins[:-1]] + [
        pl.BlockSpec((1, 8, D), lambda i, sc: (sc[0], 0, 0))
    ]
    return simple_call(
        functools.partial(final_kernel, prompt, len(rest)), sc, ins, shapes, specs, "final_norm", deps
    )


class Reduce:

    def __init__(self, sc, keep, give, name, names, plan):
        self.sc, self.keep, self.give = sc, keep, give
        self.names, self.plan = list(names), list(plan)
        self.ready, self.waiting = 0, None
        self.send(name)

    def send(self, name):
        axis, bit = name
        count = lax.axis_size(axis)
        self.got = lax.ppermute(self.give, axis, [(i, i ^ bit) for i in range(count)])

    def step(self, deps=(), hold=False):
        rows, width = self.keep.shape
        if not self.plan:
            return []
        name = self.plan.pop(0)
        where = self.names.index(name)
        self.names.pop(where)
        before, size = 2**where, rows // 2 ** (where + 1)
        if name[0] == "x":
            slot = None
        else:
            slot = LAYERS * 8 + 1 + (bits_of("dp") + bits_of("row")).index(name)

        def add(sc, keep, got, new_keep, new_give):
            bit = 0 if slot is None else sc[slot]
            for a in range(before):
                for out, side in ((new_keep, bit), (new_give, 1 - bit)):
                    lo = (2 * a + side) * size
                    at = pl.ds(lo if slot is None else pl.multiple_of(lo, size), size)
                    out[a * size : (a + 1) * size, :] = add_low(keep[at, :], got[at, :])

        if size % 16:
            total = add_low(self.keep, self.got).reshape(before, 2, size, width)
            bit = 0 if slot is None else self.sc[slot]
            self.keep, self.give = (
                lax.dynamic_index_in_dim(total, side, 1, keepdims=False).reshape(rows // 2, width)
                for side in (bit, 1 - bit)
            )
        else:
            shape = jax.ShapeDtypeStruct((rows // 2, width), BF16)
            self.keep, self.give = simple_call(
                add, self.sc, [self.keep, self.got], [shape] * 2, name="add", deps=deps
            )
        if hold and name[0] != "dp":
            self.waiting = name
        else:
            self.send(name)
        return [self.give]

    def release(self, deps):
        if self.waiting is not None:
            self.give = behind([self.give], deps)[0]
            self.send(self.waiting)
            self.waiting = None

    def finish(self):
        while self.plan:
            self.step()
        return [self.keep, self.got]


def bits_of(axis):
    bits, bit = [], lax.axis_size(axis) // 2
    while bit:
        bits.append((axis, bit))
        bit //= 2
    return bits


def reorder(value):
    shape = value.shape
    value = value.reshape((2, 2) + shape[1:])
    value = jnp.where(lax.axis_index("core") == 1, value[:, ::-1], value)
    value = jnp.where(lax.axis_index("x") == 1, value[::-1], value)
    return value.reshape(shape)


def narrow_kernel(width, sc, *refs):
    smalls, qkvs, last_ref, out = refs[:LAYERS], refs[LAYERS : 2 * LAYERS], refs[2 * LAYERS], refs[-1]
    out[...] = jnp.zeros_like(out)
    for b in range(NB):
        total = jnp.zeros((16, D), F32)
        qkv = jnp.zeros((HEADS_COL, 256), F32)
        for i in range(LAYERS):
            mine = sc[i * 8] == b
            total = total + jnp.where(mine, smalls[i][...], 0.0)
            qkv = qkv + jnp.where(mine, qkvs[i][:, 0, :], 0.0)
        gain = jnp.where(sc[0] == b, last_ref[0:2, :], 0.0)
        for i in range(1, LAYERS):
            gain = gain + jnp.where(sc[i * 8] == b, smalls[i - 1][8:10, :], 0.0)
        rows = jnp.concatenate([total[5:6], total[4:5], total[6:8], gain], axis=0)
        for s in range(4):
            out[s, b, 0:1, :] = total[s : s + 1]
            for c in range(4):

                def put(s=s, b=b, c=c, rows=rows):
                    out[s, b, 1:7, 0:width] = rows[:, c * width : (c + 1) * width]

                pl.when((sc[3] ^ s) == c)(put)
        for h in range(HEADS_COL):
            out[0, b, 7:8, h * 256 : (h + 1) * 256] = qkv[h : h + 1]


def end_slot():
    return LAYERS * 8 + 1 + len(bits_of("dp")) + len(bits_of("row"))


def pack_end(sc, parts, width):
    slot = end_slot()
    share = parts[0].shape[0]

    def end(sc, *refs):
        up, down, out = refs[-3:]
        for k in range(NB):
            ka, ga, kb, gb = refs[4 * k : 4 * k + 4]
            left = ka[...].astype(F32) + ga[...].astype(F32)
            right = kb[...].astype(F32) + gb[...].astype(F32)
            for b in range(NB):

                def put(b=b, left=left, right=right):
                    up[b] = left
                    down[b] = right[:, 0:D]
                    out[b] = right[:, D : D + width]

                pl.when(sc[slot + b] == k)(put)

    shapes = [jax.ShapeDtypeStruct((NB, share, n), F32) for n in (D, D, width)]
    return simple_call(end, sc, parts, shapes, name="pack_end")


def qkv_end(sc, parts, width):
    slot = end_slot()
    share = parts[0].shape[0]

    def end(sc, *refs):
        out = refs[-1]
        for k in range(NB):
            total = refs[2 * k][...].astype(F32) + refs[2 * k + 1][...].astype(F32)
            for b in range(NB):

                def put(b=b, total=total):
                    for h in range(HEADS_COL):
                        for j, lane in enumerate((0, 128, 192)):
                            at = h * 256 + lane
                            out[b, j, :, h * HD : (h + 1) * HD] = total[:, at : at + HD]

                pl.when(sc[slot + b] == k)(put)

    shape = jax.ShapeDtypeStruct((NB, 3, share, width), F32)
    return simple_call(end, sc, parts, [shape], name="qkv_end")[0].transpose(0, 2, 1, 3)


def narrow_end(sc, value, got, width):
    def end(sc, value, got, bup, qv, *vecs):
        for b in range(NB):
            total = value[b] + got[b]
            bup[b : b + 1, :] = total[0:1]
            for k, out in enumerate(vecs):
                out[b : b + 1, :] = total[1 + k : 2 + k, 0:width]
            for h in range(HEADS_COL):
                for j, lane in enumerate((0, 192)):
                    at = h * 256 + lane
                    qv[b, j : j + 1, h * HD : (h + 1) * HD] = total[7:8, at : at + HD]

    shapes = [jax.ShapeDtypeStruct((NB, D), F32), jax.ShapeDtypeStruct((NB, 2, width), F32)]
    shapes += [jax.ShapeDtypeStruct((NB, width), F32)] * 6
    return simple_call(end, sc, [value, got], shapes, name="narrow_end")


def sum_small(value):
    got = swap_core(jnp.stack([value[1], value[3]]))
    near, far = value[0] + got[0], value[2] + got[1]
    value = near + swap_x(far)
    steps = bits_of("row") + bits_of("dp")
    for k, (axis, bit) in enumerate(steps):
        got = lax.ppermute(value, axis, [(i, i ^ bit) for i in range(lax.axis_size(axis))])
        if k + 1 < len(steps):
            value = value + got
    return value, got


def per_device(
    x_prompt,
    x_cont,
    seg_ids,
    layer_map,
    w_qkv,
    bias_qv,
    w_out,
    b_out,
    w_up,
    b_up,
    w_down,
    b_down,
    ln1_gain,
    ln1_bias,
    ln2_gain,
    ln2_bias,
    cot_prompt,
    cot_cont,
):
    rows, dps = lax.axis_size("row"), lax.axis_size("dp")
    prompt_row, cont = x_prompt.shape[1], x_cont.shape[1]
    width = x_prompt.shape[2]
    chunk = prompt_row // 2
    piece, cpiece = chunk // 4, cont // 4
    prompt = 2 * piece
    dims = (rows, piece, cpiece, chunk, cont)
    my_row, my_x = lax.axis_index("row"), lax.axis_index("x")
    my_col = my_x * 2 + lax.axis_index("core")

    layer_map = layer_map.astype(jnp.int32)
    places = jnp.arange(LAYERS, dtype=jnp.int32)
    blocks = jnp.arange(NB, dtype=jnp.int32)
    first_use = jnp.min(jnp.where(layer_map[None] == blocks[:, None], places[None], 99), axis=1)
    rank_of = jnp.sum((first_use[None] < first_use[:, None]).astype(jnp.int32), axis=1)
    rank_layer = jnp.sum(jnp.where(layer_map[:, None] == blocks[None], rank_of[None], 0), axis=1)
    later = (rank_layer[None] == rank_layer[:, None]) & (places[None] > places[:, None])
    fresh = 1 - jnp.max(later.astype(jnp.int32), axis=1)
    after = jnp.concatenate([layer_map[1:], layer_map[-1:]])

    def fill(value):
        return jnp.broadcast_to(value, (LAYERS,)).astype(jnp.int32)

    sc = jnp.stack(
        [layer_map, rank_layer, after, fill(my_col), fill(my_x), fill(my_row), fresh, fill(my_row % 2)],
        axis=1,
    ).reshape(-1)
    my_dp = lax.axis_index("dp")
    extra = [my_dp * rows + my_row]
    ends = [rank_of[b] for b in range(NB)]
    extra += [(lax.axis_index(a) // b) % 2 for a, b in bits_of("dp") + bits_of("row")]
    sc = jnp.concatenate([sc, jnp.stack(extra + ends).astype(jnp.int32)])

    heads = w_qkv.reshape(NB, -1, 3, HEADS_COL, HD)
    zero = jnp.zeros_like(heads[:, :, 0])
    packed = jnp.stack([heads[:, :, 0], zero, heads[:, :, 1], heads[:, :, 2]], axis=3)
    packed = packed.reshape(NB, -1, D)

    def by_block(stacked):
        nothing = jnp.zeros((), stacked.dtype)
        return [
            sum(jnp.where(rank_of[b] == k, stacked[b], nothing) for b in range(NB)) for k in range(NB)
        ]

    packed = by_block(packed)
    pair = bias_qv.astype(F32).reshape(NB, 2, HEADS_COL, HD)
    none = jnp.zeros((NB, HEADS_COL, 2, HD), F32)
    bqkv = jnp.concatenate([pair[:, 0][:, :, None], none, pair[:, 1][:, :, None]], axis=2).reshape(NB, 1, D)

    def flat(value):
        return value.reshape(NB, -1)

    narrow = jnp.concatenate(
        [flat(v) for v in (b_out, b_down, ln2_gain, ln2_bias, ln1_gain, ln1_bias, b_up)], axis=1
    )
    narrow = jnp.stack(exchange_heads([narrow] * 4))
    narrow = reorder(narrow.astype(F32))
    vecs = narrow[:, :, : 6 * width].reshape(4, NB, 6, width).transpose(1, 2, 0, 3).reshape(NB, 6, D)
    vecs = jnp.concatenate([vecs, jnp.zeros((NB, 2, D), F32)], axis=1)
    bup = narrow[:, :, 6 * width :].transpose(1, 0, 2).reshape(NB, 4, 1, D)

    pack_local = jnp.concatenate(
        [w_up, w_down, w_out, jnp.zeros(w_out.shape[:2] + (64,), BF16)], axis=2
    )
    share = D // (dps * rows)
    packs = []
    for local in by_block(pack_local):
        pack = lax.all_gather(local, ("x", "core", "dp", "row"), axis=0)
        if share % 16:
            packs.append(pack.reshape(4, 1, D, PACK))
        else:
            packs.append(pack.reshape(4, dps * rows, share, PACK))

    def places_of(size):
        index = jnp.arange(4 * size, dtype=jnp.int32)
        return size * ((index // size) ^ my_col) + index % size

    ppos, cpos = places_of(piece), places_of(cpiece)
    seg = reorder(seg_ids[0].astype(jnp.int32).reshape(4, cpiece)).reshape(cont)
    pos = [ppos[None], ppos[:, None], cpos[None], cpos[:, None], seg[None], seg[:, None]]

    tok = prompt + cpiece
    direct = dps * rows <= 8
    parts, (hidden, low, low_prompt) = enter(x_prompt[0], x_cont[0], sc, vecs, True)
    if direct:
        first = held(packed[0][None], [parts[0]])
        first = [first] + gather_begin(first, ("dp", "row"))
        wqkv_first = gather_end(sc, first, LAYERS * 8, deps=[low])
    else:
        wqkv_all = lax.all_gather(jnp.stack(packed), ("dp", "row"), axis=1, tiled=True)
        wqkv_first = wqkv_all
    saved = []
    for i in range(LAYERS):
        last = i == LAYERS - 1
        own, oth = spread(low, low_prompt)
        if i == 1 and direct:
            wqkv_all = gather_end(sc, rest, LAYERS * 8, [wqkv_first], deps=[low])
        weight = wqkv_first if i == 0 else wqkv_all
        res = attn_fwd(i, sc, own, oth, weight, bqkv, pos, dims)
        o_send, (q, kv, lse, lsec) = res[:4], res[4:]
        if i == 0 and direct:
            rest = held(jnp.stack(packed[1:]), [lsec])
            rest = [rest] + gather_begin(rest, ("dp", "row"))
        deps = []
        if i == 2:
            cot_parts = enter_begin(cot_prompt[0], cot_cont[0], sc, [lsec])
            deps = [cot_parts[0]]
        if i == 3:
            grad = enter_end(cot_got, sc, vecs, False, prompt, [lsec])[0]
            deps = [grad]
        o_got = exchange_heads(o_send)
        avail = packs[: min(i, NB - 1) + 1]
        res = mlp_fwd(i, sc, hidden, o_got, vecs, bup, avail, prompt, last, width, deps)
        if i == 2:
            cot_got = exchange_heads(cot_parts)
        saved.append((hidden, own, oth, o_send, q, kv, lse, lsec, o_got, res[0], res[1]))
        hidden = res[2]
        if not last:
            low, low_prompt = res[3], res[4]
    y_send = exchange_heads(res[3:7])

    acc_pack = blank((NB, 2, D, PACK), BF16)
    back = None
    small = [None] * LAYERS
    small_qkv = [None] * LAYERS
    sums = []
    done_pack = [None] * NB
    done_qkv = [None] * NB
    dws = [None] * LAYERS
    dp_bits, row_bits = bits_of("dp"), bits_of("row")
    bits = dp_bits + row_bits
    top, x_bit = row_bits[0], ("x", 1)
    fence = []
    for i in reversed(range(LAYERS)):
        h_in, own, oth, o_send, q, kv, lse, lsec, o_got, h1, up = saved[i]
        res = mlp_bwd(i, sc, grad, back, h1, up, vecs, packs, prompt, fence)
        tokens, mine, theirs, grad = res[:4]
        do_send, small[i] = res[4:8], res[8]
        fence = []
        for part in sums:
            if part.ready <= 2 * (LAYERS - i):
                fence += part.step([small[i]])
        if i == LAYERS - 1:
            y_parts = leave_begin(y_send, sc, prompt_row, [small[i]])
            fence.append(y_parts[0])
        *do_send, tokens, theirs = behind([*do_send, tokens, theirs], fence)
        do_got = exchange_heads(do_send)
        ins = [tokens, swap_core(tokens), mine, swap_core(theirs)]
        ins += [o_got[0], o_got[2], swap_core(o_got[1]), swap_core(o_got[3])]
        if i < NB:
            res = dw_last(i, sc, ins, acc_pack, dps)
            keep_a, give_a, keep_b, give_b, acc_pack, token = res
            give_a, give_b = behind([give_a, give_b], do_got[1:])
            left = [n for n in bits if n != top]
            done_pack[i] = [
                Reduce(sc, keep_a, give_a, x_bit, bits, row_bits + dp_bits[::-1]),
                Reduce(sc, keep_b, give_b, top, [x_bit] + left, [x_bit] + row_bits[1:] + dp_bits[::-1]),
            ]
            sums += done_pack[i]
            fence = [token]
            if i + 1 < NB:
                fence += done_qkv[i + 1].step([token])
        else:
            fence = []
        fence += [part.give for part in sums]
        res = attn_bwd(i, sc, do_got, o_send, q, kv, lse, lsec, wqkv_all, pos, dims, fence)
        da_mine, da_theirs, dq, dkv, small_qkv[i] = res
        fence = []
        for part in sums if i > 0 else done_pack[0]:
            if part.ready <= 2 * (LAYERS - i) + 1:
                fence += part.step([small_qkv[i]], i > 0)
        if i == LAYERS - 1:
            y_prompt, y_cont = leave_end(sc, *y_parts, deps=[small_qkv[i]])
            fence.append(y_prompt)
        if i > 0:
            base, got, rest = collect(da_mine, behind([da_theirs], fence)[0], tok, prompt)
            dws[i], token = dw_qkv(i, sc, own, oth, dq, dkv)
        else:
            dws[i], token = dw_qkv(i, sc, own, oth, dq, dkv, fence)
            fence = []
            for part in done_pack[0]:
                fence += part.step([token])
            base, got, rest = collect(da_mine, behind([da_theirs], fence)[0], tok, prompt)
        fence = [token]
        if i >= NB:
            acc_pack, token = dw_mlp(i, sc, ins, acc_pack, [base])
            fence.append(token)
        for part in sums:
            part.release([got, *rest, token])
        if i < NB:
            keep, give = qkv_total(sc, i, dws[i:], dps, [got])
            done_qkv[i] = Reduce(sc, keep, give, top, left, row_bits[1:] + dp_bits[::-1])
            done_qkv[i].ready = 2 * (LAYERS - i) + 3
            sums.append(done_qkv[i])
            fence.append(give)
        back = (h_in, base, got, rest)
        sums = [part for part in sums if part.plan]

    for part in sums:
        if part.ready <= 2 * LAYERS + 2:
            step = part.step([got])
            if part not in done_pack[0]:
                continue
            fence += step
    res = final_norm(sc, grad, back, vecs, prompt, width, fence)
    dx_parts = leave_begin(exchange_heads(res[:4]), sc, prompt_row)
    for part in sums:
        part.step([dx_parts[0]])
    dx_prompt, dx_cont = leave_end(sc, *dx_parts)
    for part in sums:
        part.step([dx_prompt])
    for part in sums:
        part.step()
    g_up, g_down, g_out = pack_end(sc, [v for parts in done_pack for p in parts for v in p.finish()], width)
    g_qkv = qkv_end(sc, [v for part in done_qkv for v in part.finish()], width)

    shape = jax.ShapeDtypeStruct((4, NB, 8, D), F32)
    narrow = simple_call(
        functools.partial(narrow_kernel, width), sc, [*small, *small_qkv, res[4]], [shape], name="narrow"
    )[0]
    g_bup, g_qv, *g_vec = narrow_end(sc, *sum_small(narrow), width)
    return (
        y_prompt,
        y_cont,
        dx_prompt,
        dx_cont,
        g_qkv,
        g_qv,
        g_out,
        g_vec[0],
        g_up,
        g_bup,
        g_down,
        g_vec[1],
        g_vec[4],
        g_vec[5],
        g_vec[2],
        g_vec[3],
    )


def solution(mesh):
    dps, rows = mesh.shape["dp"], mesh.shape["row"]
    fine = Mesh(mesh.devices.reshape(dps, rows, 2, 2), ("dp", "row", "x", "core"))
    col = ("x", "core")
    both = ("dp", "row")
    tokens = P("dp", "row", col)
    narrow = P(None, col)
    wide = P(None, both, col)
    in_specs = (
        tokens,
        tokens,
        P("dp", "row"),
        P(),
        P(None, both, None, col),
        P(None, None, col),
        wide,
        narrow,
        wide,
        narrow,
        wide,
        narrow,
        narrow,
        narrow,
        narrow,
        narrow,
        tokens,
        tokens,
    )
    out_specs = (
        tokens,
        tokens,
        tokens,
        tokens,
        P(None, both, None, col),
        P(None, None, col),
        wide,
        narrow,
        wide,
        narrow,
        wide,
        narrow,
        narrow,
        narrow,
        narrow,
        narrow,
    )
    return jax.shard_map(
        per_device, mesh=fine, in_specs=in_specs, out_specs=out_specs, check_vma=False
    )
```

```python
import functools

import jax
import jax.numpy as jnp
from jax import lax
from jax.experimental import pallas as pl
from jax.experimental.pallas import tpu as pltpu
from jax.sharding import Mesh
from jax.sharding import PartitionSpec as P

D = 768
HD = 64
LAYERS = 6
NB = 3
HEADS_COL = 3
PACK = 1792
NORM_EPS = 1e-05
MASK_FILL = -1000000000.0
GELU_COEF = 0.7978845608028654
F32 = jnp.float32
BF16 = jnp.bfloat16
MIB = 1024 * 1024


def nn(a, b):
    return lax.dot_general(a, b, (((1,), (0,)), ((), ())), preferred_element_type=F32)


def nt(a, b):
    return lax.dot_general(a, b, (((1,), (1,)), ((), ())), preferred_element_type=F32)


def tn(a, b):
    return lax.dot_general(a, b, (((0,), (0,)), ((), ())), preferred_element_type=F32)


def stats(hidden):
    mean = jnp.sum(hidden, axis=1, keepdims=True) * (1.0 / D)
    square = jnp.sum(hidden * hidden, axis=1, keepdims=True) * (1.0 / D)
    inverse = lax.rsqrt(square - mean * mean + NORM_EPS)
    return (hidden - mean) * inverse, inverse


def norm_back(grad, gain, centered, inverse):
    scaled = grad * gain
    first = jnp.sum(scaled, axis=1, keepdims=True) * (1.0 / D)
    second = jnp.sum(scaled * centered, axis=1, keepdims=True) * (1.0 / D)
    return inverse * (scaled - first - centered * second)


def colsum(value):
    return jnp.sum(value, axis=0, keepdims=True)


def to_row(column):
    rows = column.shape[0]
    return jnp.transpose(jnp.broadcast_to(column, (rows, 128)))[0:1, :]


class Row:
    def __init__(self, ref, layer):
        self.ref, self.base = ref, layer * 8

    def __getitem__(self, j):
        return self.ref[self.base + j]


def strip(kernel, layer, count, deps):
    def run(sc, *refs):
        kernel(Row(sc, layer), *refs[:count], *refs[count + deps :])

    return run


def params(limit, **more):
    return pltpu.CompilerParams(vmem_limit_bytes=limit * MIB, **more)


def cost(flops, nbytes, trans=0):
    return pl.CostEstimate(flops=int(flops), bytes_accessed=int(nbytes), transcendentals=int(trans))


class Weights:

    def __init__(self, sc, packs, wout, wud, sems):
        self.sc, self.packs, self.sems = sc, packs, sems
        self.dst = ((wout, 1536, 256), (wud, 0, 1536))
        self.parts, self.size = packs[0].shape[1], packs[0].shape[2]

    def start(self, order):
        if len(self.packs) == 1:
            self.start_from(self.packs[0], order)
        else:
            for k, src in enumerate(self.packs):
                pl.when(self.sc[1] == k)(functools.partial(self.start_from, src, order))

    def start_from(self, src, order):
        for kind in order:
            dst, lo, size = self.dst[kind]
            for s in range(4):
                for j in range(self.parts):
                    rows = pl.ds(j * self.size, self.size)
                    pltpu.make_async_copy(
                        src.at[self.sc[3] ^ s, j, :, pl.ds(lo, size)],
                        dst.at[s, rows],
                        self.sems.at[kind, s],
                    ).start()

    def wait(self, kind, s):
        dst = self.dst[kind][0].at[s]
        pltpu.make_async_copy(dst, dst, self.sems.at[kind, s]).wait()


def mlp_fwd_kernel(ranks, last, prompt, sc, *refs):
    h_ref, o0, o1, o2, o3, vec_ref, bup_ref, nvec_ref = refs[:8]
    outs = refs[8 + ranks :]
    h1_ref, u_ref, h_out = outs[:3]
    wout, wud, sems = outs[-3:]
    weights = Weights(sc, refs[8 : 8 + ranks], wout, wud, sems)
    weights.start((0, 1))
    total = h_ref[...] + vec_ref[0, 0:1, :]
    for s, o_ref in enumerate((o0, o1, o2, o3)):
        weights.wait(0, s)
        total = total + nt(o_ref[...], wout[s])
    h1_ref[...] = total
    centered, _ = stats(total)
    a2 = (centered * vec_ref[0, 2:3, :] + vec_ref[0, 3:4, :]).astype(BF16)
    h_out[...] = total + vec_ref[0, 1:2, :]
    for s in range(4):
        weights.wait(1, s)
        bias = bup_ref[0, pl.ds(sc[3] ^ s, 1), 0, :]
        up = nn(a2, wud[s, :, 0:768]) + bias
        u_ref[s] = up.astype(BF16)
        act = 0.5 * up * (1.0 + jnp.tanh(GELU_COEF * (up + 0.044715 * up * up * up)))
        h_out[...] += nt(act.astype(BF16), wud[s, :, 768:1536])
    if last:
        y_refs = outs[3:7]
        send_features(sc, h_out, y_refs)
    else:
        a_ref, ap_ref = outs[3:5]
        centered, _ = stats(h_out[...])
        nxt = (centered * nvec_ref[0, 4:5, :] + nvec_ref[0, 5:6, :]).astype(BF16)
        a_ref[...] = nxt
        ap_ref[...] = nxt[:prompt]


def send_features(sc, value, refs):
    width = refs[0].shape[1]
    for s, ref in enumerate(refs):
        for c in range(4):

            def put(ref=ref, c=c):
                ref[...] = value[:, c * width : (c + 1) * width].astype(BF16)

            pl.when((sc[3] ^ s) == c)(put)


def whole_spec(shape):
    return pl.BlockSpec(shape, lambda i, sc: (0,) * len(shape))


def vec_specs(layer):
    at = layer * 8
    return [
        pl.BlockSpec((1, 8, D), lambda i, sc: (sc[at], 0, 0)),
        pl.BlockSpec((1, 4, 1, D), lambda i, sc: (sc[at], 0, 0, 0)),
        pl.BlockSpec((1, 8, D), lambda i, sc: (sc[at + 2], 0, 0)),
    ]


WSCR = [
    pltpu.VMEM((4, D, 256), BF16),
    pltpu.VMEM((4, D, 1536), BF16),
    pltpu.SemaphoreType.DMA((2, 4)),
]
ANY = pl.BlockSpec(memory_space=pl.ANY)


def mlp_fwd(layer, sc, hidden, o_parts, vecs, bup, packs, prompt, last, width, deps=()):
    tok = hidden.shape[0]
    shapes = [
        jax.ShapeDtypeStruct((tok, D), F32),
        jax.ShapeDtypeStruct((4, tok, D), BF16),
        jax.ShapeDtypeStruct((tok, D), F32),
    ]
    if last:
        shapes += [jax.ShapeDtypeStruct((tok, width), BF16)] * 4
    else:
        shapes += [jax.ShapeDtypeStruct((tok, D), BF16), jax.ShapeDtypeStruct((prompt, D), BF16)]
    out_specs = [whole_spec(v.shape) for v in shapes]
    ins = [hidden, *o_parts, vecs, bup, vecs, *packs]
    kernel = functools.partial(mlp_fwd_kernel, len(packs), last, prompt)
    return pl.pallas_call(
        strip(kernel, layer, len(ins), len(deps)),
        grid_spec=pltpu.PrefetchScalarGridSpec(
            num_scalar_prefetch=1,
            grid=(1,),
            in_specs=[whole_spec((tok, D))]
            + [whole_spec((tok, 256))] * 4
            + vec_specs(layer)
            + [ANY] * (len(packs) + len(deps)),
            out_specs=out_specs,
            scratch_shapes=WSCR,
        ),
        out_shape=shapes,
        compiler_params=params(44),
        cost_estimate=cost(2 * tok * D * 6912, 16e6, tok * 3072),
        name="mlp_fwd",
    )(sc, *ins, *deps)


def mlp_bwd_kernel(ranks, others, first, prompt, sc, *refs):
    if first:
        g_ref, refs = refs[0], refs[1:]
    else:
        nin = 4 + 2 * others
        g_ref, hn_ref, p0_ref, rx_ref = refs[:4]
        rest = refs[4:nin]
        refs = refs[nin:]
    h1_ref, u_hbm, vec_ref, nvec_ref = refs[:4]
    outs = refs[4 + ranks :]
    tok_ref, mine_ref, theirs_ref, g1_ref, d0, d1, d2, d3, small_ref = outs[:9]
    wout, wud, sems, u_ref, usem = outs[9:]
    loads = [pltpu.make_async_copy(u_hbm.at[s], u_ref.at[s], usem.at[s]) for s in range(4)]
    for copy in loads:
        copy.start()
    weights = Weights(sc, refs[4 : 4 + ranks], wout, wud, sems)
    weights.start((1, 0))
    small_ref[...] = jnp.zeros_like(small_ref)
    if first:
        grad = g_ref[...]
    else:
        g1_ref[...] = p0_ref[...].astype(F32) + rx_ref[...].astype(F32)
        for ref in rest:
            g1_ref[0:prompt, :] += ref[...].astype(F32)
        da1 = g1_ref[...]
        centered, inverse = stats(hn_ref[...])
        small_ref[8:9, :] = colsum(da1 * centered)
        small_ref[9:10, :] = colsum(da1)
        grad = g_ref[...] + norm_back(da1, nvec_ref[0, 4:5, :], centered, inverse)
    gm = grad.astype(BF16)
    tok_ref[1] = gm
    small_ref[4:5, :] = colsum(gm.astype(F32))
    for s in range(4):
        weights.wait(1, s)
        dm = nn(gm, wud[s, :, 768:1536])
        loads[s].wait()
        up = u_ref[s].astype(F32)
        square = up * up
        tanh = jnp.tanh(GELU_COEF * up * (1.0 + 0.044715 * square))
        slope = 0.5 * (1.0 + tanh) + 0.5 * up * (1.0 - tanh * tanh) * (
            GELU_COEF * (1.0 + 3.0 * 0.044715 * square)
        )
        du = (dm * slope).astype(BF16)
        side = mine_ref if s % 2 == 0 else theirs_ref
        side[s // 2] = du
        side[2 + s // 2] = (0.5 * up * (1.0 + tanh)).astype(BF16)
        small_ref[s : s + 1, :] = colsum(du.astype(F32))
        term = nt(du, wud[s, :, 0:768])
        if s == 0:
            g1_ref[...] = term
        else:
            g1_ref[...] += term
    da2 = g1_ref[...]
    centered, inverse = stats(h1_ref[...])
    gain = vec_ref[0, 2:3, :]
    tok_ref[0] = (centered * gain + vec_ref[0, 3:4, :]).astype(BF16)
    small_ref[6:7, :] = colsum(da2 * centered)
    small_ref[7:8, :] = colsum(da2)
    grad = grad + norm_back(da2, gain, centered, inverse)
    g1_ref[...] = grad
    go = grad.astype(BF16)
    tok_ref[2] = go
    small_ref[5:6, :] = colsum(go.astype(F32))
    for s, ref in enumerate((d0, d1, d2, d3)):
        weights.wait(0, s)
        ref[...] = nn(go, wout[s]).astype(BF16)


def mlp_bwd(layer, sc, grad, back, h1, up, vecs, packs, prompt, deps=()):
    tok = grad.shape[0]
    first = back is None
    others = 0 if first else len(back[3])
    shapes = [
        jax.ShapeDtypeStruct((3, tok, D), BF16),
        jax.ShapeDtypeStruct((4, tok, D), BF16),
        jax.ShapeDtypeStruct((4, tok, D), BF16),
        jax.ShapeDtypeStruct((tok, D), F32),
    ]
    shapes += [jax.ShapeDtypeStruct((tok, 256), BF16)] * 4
    shapes += [jax.ShapeDtypeStruct((16, D), F32)]
    extra = [] if first else [back[0], back[1], back[2], *back[3]]
    specs = vec_specs(layer)
    ins = [grad, *extra, h1, up, vecs, vecs, *packs]
    kernel = functools.partial(mlp_bwd_kernel, len(packs), others // 2, first, prompt)
    return pl.pallas_call(
        strip(kernel, layer, len(ins), len(deps)),
        grid_spec=pltpu.PrefetchScalarGridSpec(
            num_scalar_prefetch=1,
            grid=(1,),
            in_specs=[whole_spec(v.shape) for v in [grad, *extra, h1]]
            + [ANY, specs[0], specs[2]]
            + [ANY] * (len(packs) + len(deps)),
            out_specs=[whole_spec(s.shape) for s in shapes],
            scratch_shapes=WSCR + [pltpu.VMEM((4, tok, D), BF16), pltpu.SemaphoreType.DMA((4,))],
        ),
        out_shape=shapes,
        compiler_params=params(48),
        cost_estimate=cost(2 * tok * D * 6912, 16e6, tok * 3072),
        name="mlp_bwd",
    )(sc, *ins, *deps)


def attn_fwd_kernel(dims, sc, *refs):
    rows, piece, cpiece, chunk, cont = dims
    npc = 4 * rows
    own, oth = refs[:4], refs[4:npc]
    w_ref, b_ref, prow, pcol, crow, ccol, srow, scol = refs[npc : npc + 8]
    outs = refs[npc + 8 :]
    o_refs = outs[:4]
    q_ref, kv_ref, lse_ref, lsec_ref, m_s, l_s, acc_s = outs[4:]
    head = pl.program_id(0)
    base_b = chunk * rows
    base_c = 2 * chunk * rows
    weight = w_ref[0]
    bias = b_ref[0]
    for s in range(4):
        mixed = nn(own[s][...], weight) + bias
        low_q = (mixed[:, 0:128].astype(BF16).astype(F32) * 0.125).astype(BF16)
        low_kv = mixed[:, 128:256].astype(BF16)
        q_ref[0, s * piece : (s + 1) * piece, :] = low_q[0:piece]
        q_ref[0, chunk + s * piece : chunk + (s + 1) * piece, :] = low_q[piece : 2 * piece]
        q_ref[0, 2 * chunk + s * cpiece : 2 * chunk + (s + 1) * cpiece, :] = low_q[2 * piece :]
        kv_ref[0, s * piece : (s + 1) * piece, :] = low_kv[0:piece]
        kv_ref[0, base_b + s * piece : base_b + (s + 1) * piece, :] = low_kv[piece : 2 * piece]
        kv_ref[0, base_c + s * cpiece : base_c + (s + 1) * cpiece, :] = low_kv[2 * piece :]
    for t in range(1, rows):
        for s in range(4):
            low_kv = (nn(oth[(t - 1) * 4 + s][...], weight[:, 128:256]) + bias[:, 128:256]).astype(BF16)
            at = t * chunk + s * piece
            kv_ref[0, at : at + piece, :] = low_kv[0:piece]
            kv_ref[0, base_b + at : base_b + at + piece, :] = low_kv[piece : 2 * piece]
    lanes = lax.broadcasted_iota(jnp.int32, (1, 128), 1)
    upper = lanes >= 64
    sub = min(256, chunk)

    def begin(query, keys, mask):
        scores = nt(query, keys)
        if mask is not None:
            size = mask.shape[1]
            tail = jnp.where(mask, scores[:, -size:], MASK_FILL)
            if size == scores.shape[1]:
                scores = tail
            else:
                scores = jnp.concatenate([scores[:, :-size], tail], axis=1)
        top = jnp.max(scores, axis=1, keepdims=True)
        prob = jnp.exp(scores - top)
        return top, jnp.sum(prob, axis=1, keepdims=True), nn(prob.astype(BF16), keys)

    def put(out, row, size):
        low = jnp.where(upper, out, 0.0)

        def first_head():
            value = pltpu.roll(low, 64, 1).astype(BF16)
            store(value, row, size, 0, False)

        def second_head():
            store(low.astype(BF16), row, size, 0, True)

        def third_head():
            store(pltpu.roll(low, 64, 1).astype(BF16), row, size, 1, False)

        pl.when(head == 0)(first_head)
        pl.when(head == 1)(second_head)
        pl.when(head == 2)(third_head)

    def store(value, row, size, half, add):
        s, at = row
        lo = half * 128
        if add:
            o_refs[s][at : at + size, lo : lo + 128] = (
                o_refs[s][at : at + size, lo : lo + 128] + value
            )
        else:
            o_refs[s][at : at + size, lo : lo + 128] = value

    for i in range(chunk // sub):
        at = i * sub
        mask = prow[0:1, :] <= pcol[at : at + sub, :]
        top, total, acc = begin(q_ref[0, at : at + sub, :], kv_ref[0, 0:chunk, :], mask)
        m_s[at : at + sub, :], l_s[at : at + sub, :], acc_s[at : at + sub, :] = top, total, acc
        at_b = chunk + at
        top, total, acc = begin(
            q_ref[0, at_b : at_b + sub, :], kv_ref[0, 0 : base_b + chunk, :], mask
        )
        m_s[at_b : at_b + sub, :], l_s[at_b : at_b + sub, :] = top, total
        acc_s[at_b : at_b + sub, :] = acc
    my_row = sc[5]
    for t in range(1, rows):
        before = lax.rem(my_row + t, rows) < my_row
        q_at = jnp.where(before, 0, chunk)
        k_at = jnp.where(before, t * chunk, base_b + t * chunk)
        keys = kv_ref[0, pl.ds(pl.multiple_of(k_at, 128), chunk), :]
        for i in range(chunk // sub):
            at = pl.ds(pl.multiple_of(q_at + i * sub, 128), sub)
            scores = nt(q_ref[0, at, :], keys)
            old = m_s[at, :]
            top = jnp.maximum(old, jnp.max(scores, axis=1, keepdims=True))
            scale = jnp.exp(old - top)
            prob = jnp.exp(scores - top)
            m_s[at, :] = top
            l_s[at, :] = l_s[at, :] * scale + jnp.sum(prob, axis=1, keepdims=True)
            acc_s[at, :] = acc_s[at, :] * scale + nn(prob.astype(BF16), keys)
    for half in range(2):
        for s in range(4):
            at = half * chunk + s * piece
            total = l_s[at : at + piece, :]
            put(acc_s[at : at + piece, :] / total, (s, half * piece), piece)
        for i in range(chunk // sub):
            at = half * chunk + i * sub
            column = m_s[at : at + sub, :] + jnp.log(l_s[at : at + sub, :])
            lse_ref[0, half, :, i * sub : (i + 1) * sub] = to_row(column)
    mask = (crow[0:1, :] <= ccol[...]) & (srow[0:1, :] == scol[...])
    query = q_ref[0, 2 * chunk : 2 * chunk + cont, :]
    top, total, acc = begin(query, kv_ref[0], mask)
    out = acc / total
    for s in range(4):
        put(out[s * cpiece : (s + 1) * cpiece], (s, 2 * piece), cpiece)
    lsec_ref[0] = to_row(top + jnp.log(total))


def attn_inputs(pos):
    return [pl.BlockSpec(v.shape, lambda i, sc: (0, 0)) for v in pos]


def attn_fwd(layer, sc, own, oth, w_all, b_all, pos, dims, deps=()):
    single = w_all.shape[0] == 1
    rows, piece, cpiece, chunk, cont = dims
    tok = own[0].shape[0]
    nq, nk = 2 * chunk + cont, 2 * chunk * rows + cont
    shapes = [jax.ShapeDtypeStruct((tok, 256), BF16)] * 4 + [
        jax.ShapeDtypeStruct((3, nq, 128), BF16),
        jax.ShapeDtypeStruct((3, nk, 128), BF16),
        jax.ShapeDtypeStruct((3, 2, 1, chunk), F32),
        jax.ShapeDtypeStruct((3, 1, cont), F32),
    ]
    out_specs = [whole_spec((tok, 256))] * 4 + [
        pl.BlockSpec((1, nq, 128), lambda i, sc: (i, 0, 0)),
        pl.BlockSpec((1, nk, 128), lambda i, sc: (i, 0, 0)),
        pl.BlockSpec((1, 2, 1, chunk), lambda i, sc: (i, 0, 0, 0)),
        pl.BlockSpec((1, 1, cont), lambda i, sc: (i, 0, 0)),
    ]
    at = layer * 8
    count = len(own) + len(oth) + 2 + len(pos)
    return pl.pallas_call(
        strip(functools.partial(attn_fwd_kernel, dims), layer, count, len(deps)),
        grid_spec=pltpu.PrefetchScalarGridSpec(
            num_scalar_prefetch=1,
            grid=(3,),
            in_specs=[whole_spec(v.shape) for v in [*own, *oth]]
            + [
                pl.BlockSpec((1, D, 256), lambda i, sc: (0 if single else sc[at + 1], 0, i)),
                pl.BlockSpec((1, 1, 256), lambda i, sc: (sc[at], 0, i)),
            ]
            + attn_inputs(pos)
            + [ANY] * len(deps),
            out_specs=out_specs,
            scratch_shapes=[
                pltpu.VMEM((2 * chunk, 1), F32),
                pltpu.VMEM((2 * chunk, 1), F32),
                pltpu.VMEM((2 * chunk, 128), F32),
            ],
        ),
        out_shape=shapes,
        compiler_params=params(52),
        cost_estimate=cost(2 * nq * D * 768 * 2 + 8 * 3 * nq * nk * 64, 12e6, 3 * nq * nk),
        name="attn_fwd",
    )(sc, *own, *oth, w_all, b_all, *pos, *deps)


def attn_bwd_kernel(dims, sc, *refs):
    rows, piece, cpiece, chunk, cont = dims
    do_refs, o_refs = refs[:4], refs[4:8]
    q_ref, kv_ref, lse_ref, lsec_ref, w_ref = refs[8:13]
    prow, pcol, crow, ccol, srow, scol = refs[13:19]
    outs = refs[19:]
    npc = 4 * rows
    mine_out, theirs_out = outs[:2]
    dq_out, dkv_out, bias_out = outs[2:5]
    do_s, drow, drowc, dq_s, dkv_s = outs[5:]
    head = pl.program_id(0)
    base_b = chunk * rows
    base_c = 2 * chunk * rows
    tok = 2 * piece + cpiece
    upper = lax.broadcasted_iota(jnp.int32, (1, 128), 1) >= 64

    def take(ref):
        value = ref[...].astype(F32)
        left, right = value[:, 0:128], value[:, 128:256]
        pick = jnp.where(head == 2, pltpu.roll(right, 64, 1), left)
        pick = jnp.where(head == 0, pltpu.roll(left, 64, 1), pick)
        return jnp.where(upper, pick, 0.0)

    for s in range(4):
        dout = take(do_refs[s])
        low = dout.astype(BF16)
        do_s[s * piece : (s + 1) * piece, :] = low[0:piece]
        do_s[chunk + s * piece : chunk + (s + 1) * piece, :] = low[piece : 2 * piece]
        do_s[2 * chunk + s * cpiece : 2 * chunk + (s + 1) * cpiece, :] = low[2 * piece :]
        dot = dout * take(o_refs[s])
        dq_s[s * piece : (s + 1) * piece, :] = dot[0:piece]
        dq_s[chunk + s * piece : chunk + (s + 1) * piece, :] = dot[piece : 2 * piece]
        dq_s[2 * chunk + s * cpiece : 2 * chunk + (s + 1) * cpiece, :] = dot[2 * piece :]
    sub = min(128, chunk)
    for half in range(2):
        for i in range(chunk // sub):
            at = half * chunk + i * sub
            column = jnp.sum(dq_s[at : at + sub, :], axis=1, keepdims=True)
            drow[half, :, i * sub : (i + 1) * sub] = to_row(column)
    column = jnp.sum(dq_s[2 * chunk :, :], axis=1, keepdims=True)
    drowc[...] = to_row(column)
    dq_s[...] = jnp.zeros_like(dq_s)
    dkv_s[...] = jnp.zeros_like(dkv_s)

    def pair(q_at, k_at, lse, dot, mask):
        query = q_ref[0, q_at, :]
        keys = kv_ref[0, k_at, :]
        dout = do_s[q_at, :]
        prob = jnp.exp(nt(keys, query) - lse)
        if mask is not None:
            prob = jnp.where(mask, prob, 0.0)
        dprob = nt(keys, dout)
        dscore = (prob * (dprob - dot)).astype(BF16)
        dkv_s[k_at, :] += nn(prob.astype(BF16), dout) + nn(dscore, query)
        dq_s[q_at, :] += tn(dscore, keys)

    kb = min(512, chunk)
    at_a, at_b = pl.ds(0, chunk), pl.ds(chunk, chunk)
    lse_a, lse_b, dot_a, dot_b = lse_ref[0, 0], lse_ref[0, 1], drow[0], drow[1]
    for j in range(chunk // kb):
        mask = pcol[j * kb : (j + 1) * kb, :] <= prow[0:1, :]
        pair(at_a, pl.ds(j * kb, kb), lse_a, dot_a, mask)
        pair(at_b, pl.ds(base_b + j * kb, kb), lse_b, dot_b, mask)
    for j in range(base_b // kb):
        pair(at_b, pl.ds(j * kb, kb), lse_b, dot_b, None)
    my_row = sc[5]
    for t in range(1, rows):
        before = lax.rem(my_row + t, rows) < my_row
        which = jnp.where(before, 0, 1)
        q_at = pl.ds(pl.multiple_of(which * chunk, 128), chunk)
        k_base = jnp.where(before, t * chunk, base_b + t * chunk)
        for j in range(chunk // kb):
            k_at = pl.ds(pl.multiple_of(k_base + j * kb, 128), kb)
            pair(q_at, k_at, lse_ref[0, which], drow[which], None)
    at_c = pl.ds(2 * chunk, cont)
    for j in range(base_c // 512):
        pair(at_c, pl.ds(j * 512, 512), lsec_ref[0], drowc[...], None)
    mask = (ccol[...] <= crow[0:1, :]) & (scol[...] == srow[0:1, :])
    pair(at_c, pl.ds(base_c, cont), lsec_ref[0], drowc[...], mask)

    lower = jnp.logical_not(upper)
    dq_all = jnp.where(lower, dq_s[...] * 0.125, 0.0).astype(BF16)
    q_sum = colsum(dq_all.astype(F32))
    kv_sum = jnp.zeros((1, 128), F32)
    lanes_q = pl.ds(pl.multiple_of(head * 256, 128), 128)
    lanes_kv = pl.ds(pl.multiple_of(head * 256 + 128, 128), 128)
    lanes_oth = pl.ds(pl.multiple_of(head * 128, 128), 128)
    for s in range(4):
        spots = (
            (s * tok, piece, s * piece, s * piece),
            (s * tok + piece, piece, chunk + s * piece, base_b + s * piece),
            (s * tok + 2 * piece, cpiece, 2 * chunk + s * cpiece, base_c + s * cpiece),
        )
        for to, size, q_row, k_row in spots:
            dkv = dkv_s[k_row : k_row + size, :].astype(BF16)
            kv_sum = kv_sum + colsum(dkv.astype(F32))
            dq_out[to : to + size, lanes_q] = dq_all[q_row : q_row + size]
            dq_out[to : to + size, lanes_kv] = dkv
    for t in range(1, rows):
        for s in range(4):
            at = t * chunk + s * piece
            to = ((t - 1) * 4 + s) * 2 * piece
            for k_row in (at, base_b + at):
                dkv = dkv_s[k_row : k_row + piece, :].astype(BF16)
                kv_sum = kv_sum + colsum(dkv.astype(F32))
                dkv_out[to : to + piece, lanes_oth] = dkv
                to += piece

    def finish():
        weight = w_ref[0]
        for s in range(4):
            side = mine_out if s % 2 == 0 else theirs_out
            term = nt(dq_out[s * tok : (s + 1) * tok, :], weight)
            side[(s // 2) * tok : (s // 2 + 1) * tok, :] = term.astype(BF16)
        narrow = jnp.concatenate([weight[:, h * 256 + 128 : (h + 1) * 256] for h in range(3)], axis=1)
        for k in range(npc - 4):
            side = mine_out if k % 2 == 0 else theirs_out
            row = 2 * tok + (k // 2) * 2 * piece
            term = nt(dkv_out[k * 2 * piece : (k + 1) * 2 * piece, :], narrow)
            side[row : row + 2 * piece, :] = term.astype(BF16)

    pl.when(head == 2)(finish)
    bias_out[0] = jnp.broadcast_to(jnp.concatenate([q_sum, kv_sum], axis=1), (8, 256))


def attn_bwd(layer, sc, do_parts, o_parts, q, kv, lse, lsec, w_all, pos, dims, deps=()):
    rows, piece, cpiece, chunk, cont = dims
    tok = 2 * piece + cpiece
    nq, nk = 2 * chunk + cont, 2 * chunk * rows + cont
    noth = 4 * (rows - 1)
    shapes = (
        [jax.ShapeDtypeStruct((2 * tok + noth * piece, D), BF16)] * 2
        + [
            jax.ShapeDtypeStruct((4 * tok, D), BF16),
            jax.ShapeDtypeStruct((noth * 2 * piece, 384), BF16),
            jax.ShapeDtypeStruct((3, 8, 256), F32),
        ]
    )
    out_specs = [whole_spec(s.shape) for s in shapes[:4]] + [
        pl.BlockSpec((1, 8, 256), lambda i, sc: (i, 0, 0)),
    ]
    at = layer * 8
    return pl.pallas_call(
        strip(functools.partial(attn_bwd_kernel, dims), layer, 13 + len(pos), len(deps)),
        grid_spec=pltpu.PrefetchScalarGridSpec(
            num_scalar_prefetch=1,
            grid=(3,),
            in_specs=[whole_spec((tok, 256))] * 8
            + [
                pl.BlockSpec((1, nq, 128), lambda i, sc: (i, 0, 0)),
                pl.BlockSpec((1, nk, 128), lambda i, sc: (i, 0, 0)),
                pl.BlockSpec((1, 2, 1, chunk), lambda i, sc: (i, 0, 0, 0)),
                pl.BlockSpec((1, 1, cont), lambda i, sc: (i, 0, 0)),
                pl.BlockSpec((1, D, D), lambda i, sc: (sc[at + 1], 0, 0)),
            ]
            + attn_inputs(pos)
            + [ANY] * len(deps),
            out_specs=out_specs,
            scratch_shapes=[
                pltpu.VMEM((nq, 128), BF16),
                pltpu.VMEM((2, 1, chunk), F32),
                pltpu.VMEM((1, cont), F32),
                pltpu.VMEM((nq, 128), F32),
                pltpu.VMEM((nk, 128), F32),
            ],
        ),
        out_shape=shapes,
        compiler_params=params(56),
        cost_estimate=cost(2 * nq * D * 768 * 2 + 20 * 3 * nq * nk * 64, 14e6, 3 * nq * nk),
        name="attn_bwd",
    )(sc, *do_parts, *o_parts, q, kv, lse, lsec, w_all, *pos, *deps)


def dw_qkv_kernel(rows, sc, *refs):
    npc = 4 * rows
    srcs, (dq_hbm, dkv_hbm) = refs[:npc], refs[npc : npc + 2]
    new_ref, token = refs[npc + 2 : npc + 4]
    own, oth, dq_s, dkv_s, asem, dsem = refs[npc + 4 :]
    token[...] = jnp.zeros_like(token)
    tok, two = srcs[0].shape[0], srcs[4].shape[0]

    def rows_of(k):
        dst = own.at[pl.ds(k * tok, tok)] if k < 4 else oth.at[pl.ds((k - 4) * two, two)]
        return pltpu.make_async_copy(srcs[k], dst, asem.at[k])

    loads = [rows_of(k) for k in range(npc)]
    grads = [
        pltpu.make_async_copy(dq_hbm, dq_s, dsem.at[0]),
        pltpu.make_async_copy(dkv_hbm, dkv_s, dsem.at[1]),
    ]
    for copy in [grads[0], *loads[:4], grads[1], *loads[4:]]:
        copy.start()
    for copy in [grads[0], *loads[:4]]:
        copy.wait()
    total = tn(own[...], dq_s[...])
    for copy in [grads[1], *loads[4:]]:
        copy.wait()
    right = tn(oth[...], dkv_s[...])
    for h in range(HEADS_COL):
        lo = h * 256
        new_ref[:, lo : lo + 128] = total[:, lo : lo + 128].astype(BF16)
        both = total[:, lo + 128 : lo + 256] + right[:, h * 128 : (h + 1) * 128]
        new_ref[:, lo + 128 : lo + 256] = both.astype(BF16)


def dw_qkv(layer, sc, own, oth, dq, dkv, deps=()):
    rows = (4 + len(oth)) // 4
    tok, two = own[0].shape[0], oth[0].shape[0]
    noth = len(oth)
    ins = [*own, *oth, dq, dkv]
    return pl.pallas_call(
        strip(functools.partial(dw_qkv_kernel, rows), layer, len(ins), len(deps)),
        grid_spec=pltpu.PrefetchScalarGridSpec(
            num_scalar_prefetch=1,
            grid=(1,),
            in_specs=[ANY] * len(ins) + [ANY] * len(deps),
            out_specs=[whole_spec((D, D)), whole_spec((8, 128))],
            scratch_shapes=[
                pltpu.VMEM((4 * tok, D), BF16),
                pltpu.VMEM((noth * two, D), BF16),
                pltpu.VMEM(dq.shape, BF16),
                pltpu.VMEM(dkv.shape, BF16),
                pltpu.SemaphoreType.DMA((4 * rows,)),
                pltpu.SemaphoreType.DMA((2,)),
            ],
        ),
        out_shape=[
            jax.ShapeDtypeStruct((D, D), BF16),
            jax.ShapeDtypeStruct((8, 128), F32),
        ],
        compiler_params=params(56),
        cost_estimate=cost(2 * 3 * D * (4 * tok * 256 + noth * two * 128), 10e6),
        name="dw_qkv",
    )(sc, *ins, *deps)


class Loads:

    def __init__(self, refs, tok, side, outp, sems):
        tok_m, tok_r, mine, got, o0, o2, r1, r3 = refs
        size = tok_m.shape[1]
        low, high = pl.ds(0, size), pl.ds(size, size)
        pairs = {}
        for k in range(3):
            pairs["tok", k] = [(tok_m.at[k], tok.at[k, low]), (tok_r.at[k], tok.at[k, high])]
        for k in range(4):
            pairs["side", k] = [(mine.at[k], side.at[k, low]), (got.at[k], side.at[k, high])]
        pairs["outp", 0] = [(o0, outp.at[0, low]), (r1, outp.at[0, high])]
        pairs["outp", 1] = [(o2, outp.at[1, low]), (r3, outp.at[1, high])]
        self.copies, n = {}, 0
        for key, both in pairs.items():
            self.copies[key] = []
            for a, b in both:
                self.copies[key].append(pltpu.make_async_copy(a, b, sems.at[n]))
                n += 1

    def start(self):
        first = [("tok", 0), ("side", 0), ("tok", 1), ("side", 2), ("tok", 2), ("outp", 0)]
        for key in [*first, ("side", 1), ("side", 3), ("outp", 1)]:
            for copy in self.copies[key]:
                copy.start()

    def wait(self, *key):
        for copy in self.copies[key]:
            copy.wait()

    def wait_tile(self, tile, name, index):
        tokens = {"up": 0, "down": 1, "out": 2}[index]

        def first():
            self.wait("tok", tokens)
            self.wait(name, 2 if index == "down" else 0)

        pl.when(tile == 0)(first)
        pl.when(tile == 1)(lambda: self.wait(name, 3 if index == "down" else 1))


def dw_products(tile, loads, tok, side, outp, put):
    loads.wait_tile(tile, "side", "up")
    for j in range(3):
        put(j * 256, tn(tok[0], side[tile, :, j * 256 : (j + 1) * 256]))
    loads.wait_tile(tile, "side", "down")
    for j in range(3):
        put(768 + j * 256, tn(tok[1], side[2 + tile, :, j * 256 : (j + 1) * 256]))
    loads.wait_tile(tile, "outp", "out")
    put(1536, tn(tok[2], outp[tile]))


def dw_mlp_kernel(sc, *refs):
    old_ref, new_ref, token = refs[8:11]
    tok, side, outp, sems = refs[11:]
    token[...] = jnp.zeros_like(token)
    tile = pl.program_id(0)
    keep = sc[6] == 0

    loads = Loads(refs[:8], tok, side, outp, sems)
    pl.when(tile == 0)(loads.start)

    def put(lo, value):
        size = value.shape[1]
        old = old_ref[0, 0, :, lo : lo + size].astype(F32)
        new_ref[0, 0, :, lo : lo + size] = (value + jnp.where(keep, old, 0.0)).astype(BF16)

    dw_products(tile, loads, tok, side, outp, put)


def dw_scratch(tok):
    return [
        pltpu.VMEM((3, 2 * tok, D), BF16),
        pltpu.VMEM((4, 2 * tok, D), BF16),
        pltpu.VMEM((2, 2 * tok, 256), BF16),
        pltpu.SemaphoreType.DMA((18,)),
    ]


def dw_mlp(layer, sc, ins, acc, deps=()):
    tok = ins[0].shape[1]
    at = layer * 8
    acc_spec = pl.BlockSpec((1, 1, D, PACK), lambda i, sc: (sc[at + 1], i, 0, 0))
    return pl.pallas_call(
        strip(dw_mlp_kernel, layer, 9, len(deps)),
        grid_spec=pltpu.PrefetchScalarGridSpec(
            num_scalar_prefetch=1,
            grid=(2,),
            in_specs=[ANY] * 8 + [acc_spec] + [ANY] * len(deps),
            out_specs=[acc_spec, whole_spec((8, 128))],
            scratch_shapes=dw_scratch(tok),
        ),
        out_shape=[jax.ShapeDtypeStruct(acc.shape, acc.dtype), jax.ShapeDtypeStruct((8, 128), F32)],
        input_output_aliases={9: 0},
        compiler_params=params(56),
        cost_estimate=cost(2 * tok * D * 4 * PACK, 20e6),
        name="dw_mlp",
    )(sc, *ins, acc, *deps)


def dw_last_kernel(rank, groups, slot, sc, *refs):
    keep_a, give_a, keep_b, give_b, acc, token = refs[9:15]
    tok, side, outp, sems, done, other, dsem, osem, out_a, out_b, asem, bsem = refs[15:]
    token[...] = jnp.zeros_like(token)
    tile = pl.program_id(0)
    same = sc[1] == rank
    keep = sc[6] == 0
    used = jnp.logical_or(jnp.logical_not(same), keep)

    def load(t):
        return pltpu.make_async_copy(acc.at[rank, t], done.at[t], dsem.at[t])

    loads = Loads(refs[:8], tok, side, outp, sems)

    def begin():
        loads.start()
        load(0).start()
        load(1).start()

    pl.when(tile == 0)(begin)
    load(tile).wait()

    def fetch_other():
        copy = pltpu.make_async_copy(acc.at[sc[1], tile], other, osem)
        copy.start()
        copy.wait()

    pl.when(jnp.logical_not(same))(fetch_other)

    def put(lo, value):
        size = value.shape[1]
        cols = slice(lo, lo + size)
        old = jnp.where(used, done[tile, :, cols].astype(F32), 0.0)
        total = (old + jnp.where(same, value, 0.0)).astype(BF16)
        if lo < D:
            out_a[tile, :, cols] = total
        else:
            out_b[tile, :, lo - D : lo - D + size] = total

        def add_other():
            before = jnp.where(keep, other[:, cols].astype(F32), 0.0)
            other[:, cols] = (value + before).astype(BF16)

        pl.when(jnp.logical_not(same))(add_other)

    dw_products(tile, loads, tok, side, outp, put)

    def store_other():
        copy = pltpu.make_async_copy(other, acc.at[sc[1], tile], osem)
        copy.start()
        copy.wait()

    pl.when(jnp.logical_not(same))(store_other)
    size = D // (2 * groups)
    bit = sc[slot]

    def copies(t):
        both = [pltpu.make_async_copy(out_a.at[t], (keep_a, give_a)[t], asem.at[t])]
        for g in range(groups):
            for k, (ref, part) in enumerate(((keep_b, bit), (give_b, 1 - bit))):
                src = pl.ds(pl.multiple_of((2 * g + part) * size, size), size)
                dst = pl.ds((t * groups + g) * size, size)
                both.append(pltpu.make_async_copy(out_b.at[t, src], ref.at[dst], bsem.at[t, 2 * g + k]))
        return both

    def leave(t):
        for copy in copies(t):
            copy.start()

    pl.when(tile == 0)(functools.partial(leave, 0))

    def finish():
        leave(1)
        for t in range(2):
            for copy in copies(t):
                copy.wait()

    pl.when(tile == 1)(finish)


def dw_last(layer, sc, ins, acc, groups, deps=()):
    tok = ins[0].shape[1]
    slot = LAYERS * 8 + 1 + len(bits_of("dp")) - layer * 8
    halves = [jax.ShapeDtypeStruct((D, n), BF16) for n in (D, D, PACK - D, PACK - D)]
    return pl.pallas_call(
        strip(functools.partial(dw_last_kernel, layer, groups, slot), layer, 9, len(deps)),
        grid_spec=pltpu.PrefetchScalarGridSpec(
            num_scalar_prefetch=1,
            grid=(2,),
            in_specs=[ANY] * 9 + [ANY] * len(deps),
            out_specs=[ANY] * 4 + [ANY, whole_spec((8, 128))],
            scratch_shapes=dw_scratch(tok)
            + [
                pltpu.VMEM((2, D, PACK), BF16),
                pltpu.VMEM((D, PACK), BF16),
                pltpu.SemaphoreType.DMA((2,)),
                pltpu.SemaphoreType.DMA(()),
                pltpu.VMEM((2, D, D), BF16),
                pltpu.VMEM((2, D, PACK - D), BF16),
                pltpu.SemaphoreType.DMA((2,)),
                pltpu.SemaphoreType.DMA((2, 2 * groups)),
            ],
        ),
        out_shape=halves
        + [
            jax.ShapeDtypeStruct(acc.shape, acc.dtype),
            jax.ShapeDtypeStruct((8, 128), F32),
        ],
        input_output_aliases={9: 4},
        compiler_params=params(56),
        cost_estimate=cost(2 * tok * D * 4 * PACK, 20e6),
        name="dw_last",
    )(sc, *ins, acc, *deps)


def qkv_total(sc, rank, parts, groups, deps):
    size = D // (2 * groups)
    slot = LAYERS * 8 + 1 + len(bits_of("dp"))

    def add(sc, *refs):
        keep, give = refs[-2:]
        bit = sc[slot]
        for g in range(groups):
            for out, side in ((keep, bit), (give, 1 - bit)):
                at = pl.ds(pl.multiple_of((2 * g + side) * size, size), size)
                total = jnp.zeros((size, D), F32)
                for k, ref in enumerate(refs[:-2]):
                    used = sc[(rank + k) * 8 + 1] == rank
                    total = total + jnp.where(used, ref[at, :].astype(F32), 0.0)
                out[g * size : (g + 1) * size, :] = total.astype(BF16)

    shape = jax.ShapeDtypeStruct((D // 2, D), BF16)
    return simple_call(add, sc, parts, [shape] * 2, name="qkv_total", deps=deps)


def blank(shape, dtype):
    def body(out):
        del out

    return pl.pallas_call(
        body,
        out_shape=jax.ShapeDtypeStruct(shape, dtype),
        out_specs=pl.BlockSpec(memory_space=pl.ANY),
        name="blank",
    )()


SWAP = [(0, 1), (1, 0)]


def swap_core(value):
    return lax.ppermute(value, "core", SWAP)


def swap_x(value):
    return lax.ppermute(value, "x", SWAP)


def shift_row(value, t):
    rows = lax.axis_size("row")
    return lax.ppermute(value, "row", [(i, (i - t) % rows) for i in range(rows)])


def shift_row_x(value, t):
    rows = lax.axis_size("row")
    pairs = [(i * 2 + j, ((i - t) % rows) * 2 + (1 - j)) for i in range(rows) for j in range(2)]
    return lax.ppermute(value, ("row", "x"), pairs)


def spread(low, low_prompt):
    rows = lax.axis_size("row")
    from_x = swap_x(low)
    far = []
    for t in range(1, rows):
        far += [shift_row(low_prompt, t), shift_row_x(low_prompt, t)]
    own = [low, swap_core(low), from_x, swap_core(from_x)]
    oth = []
    for t in range(1, rows):
        near, diag = far[2 * t - 2], far[2 * t - 1]
        oth += [near, swap_core(near), diag, swap_core(diag)]
    return own, oth


def exchange_heads(parts):
    flip = {1: [1, 0, 3, 2], 2: [2, 3, 0, 1], 3: [3, 2, 1, 0]}
    out = [parts[0]]
    for s in (1, 2, 3):
        pairs = [(c, flip[s][c]) for c in range(4)]
        out.append(lax.ppermute(parts[s], ("x", "core"), pairs))
    return out


def add_low(a, b):
    return (a.astype(F32) + b.astype(F32)).astype(BF16)


def sum_kernel(sizes, a, b, *outs):
    at = 0
    for size, out in zip(sizes, outs):
        out[...] = add_low(a[at : at + size, :], b[at : at + size, :])
        at += size


def collect(mine, theirs, tok, prompt, deps=()):
    rows = lax.axis_size("row")
    sizes = [tok, tok] + [prompt] * (2 * (rows - 1))
    vmem = pl.BlockSpec(memory_space=pltpu.VMEM)
    count = len(deps)
    sums = pl.pallas_call(
        lambda a, b, *refs: sum_kernel(sizes, a, b, *refs[count:]),
        in_specs=[vmem] * 2 + [ANY] * count,
        out_specs=[vmem] * len(sizes),
        out_shape=[jax.ShapeDtypeStruct((n, D), BF16) for n in sizes],
        compiler_params=params(24),
        cost_estimate=cost(1e6, 4e6),
        name="sum_cores",
    )(mine, swap_core(theirs), *deps)
    got = swap_x(sums[1])
    rest = []
    for t in range(1, rows):
        rest += [shift_row(sums[2 * t], -t), shift_row_x(sums[2 * t + 1], -t)]
    return sums[0], got, rest


def behind(values, deps):
    if not deps:
        return list(values)
    count = len(values)

    def body(*refs):
        del refs

    return pl.pallas_call(
        body,
        in_specs=[ANY] * (count + len(deps)),
        out_specs=[ANY] * count,
        out_shape=[jax.ShapeDtypeStruct(v.shape, v.dtype) for v in values],
        input_output_aliases={k: k for k in range(count)},
        name="behind",
    )(*values, *deps)


def held(value, deps):
    def body(src, *rest):
        rest[-1][...] = src[...]

    vmem = pl.BlockSpec(memory_space=pltpu.VMEM)
    return pl.pallas_call(
        body,
        in_specs=[vmem] + [ANY] * len(deps),
        out_specs=vmem,
        out_shape=jax.ShapeDtypeStruct(value.shape, value.dtype),
        name="held",
    )(value, *deps)


def gather_begin(value, names):
    total = 1
    for a in names:
        total *= lax.axis_size(a)
    return [lax.ppermute(value, names, [(i, i ^ t) for i in range(total)]) for t in range(1, total)]


def gather_end(sc, pieces, index, ahead=(), deps=()):
    lead, n, width = pieces[0].shape
    count = len(pieces)

    def place(sc, *refs):
        out = refs[-1]
        for block in refs[count:-1]:
            out[0:1] = block[...]
        base = len(ahead)
        for t in range(count):
            at = pl.ds(pl.multiple_of((sc[index] ^ t) * n, n), n)
            out[base : base + lead, at, :] = refs[t][...]

    shape = jax.ShapeDtypeStruct((lead + len(ahead), count * n, width), BF16)
    return simple_call(place, sc, [*pieces, *ahead], [shape], name="place", deps=deps)[0]


def zig(j, rows):
    return j if j < rows else 2 * rows - 1 - j


def split_kernel(piece, cpiece, sc, even, odd, cont, *outs):
    for s, out in enumerate(outs):
        place = sc[3] ^ s
        at = pl.ds(pl.multiple_of(place * piece, piece), piece)

        def fill(first, second, out=out, at=at):
            out[0:piece, :] = first[at, :]
            out[piece : 2 * piece, :] = second[at, :]

        pl.when(sc[7] == 0)(functools.partial(fill, even, odd))
        pl.when(sc[7] == 1)(functools.partial(fill, odd, even))
        out[2 * piece :, :] = cont[pl.ds(pl.multiple_of(place * cpiece, cpiece), cpiece), :]


def merge_kernel(piece, cpiece, sc, p0, p1, p2, p3, even, odd, cont):
    for s, part in enumerate((p0, p1, p2, p3)):
        place = sc[3] ^ s
        at = pl.ds(pl.multiple_of(place * piece, piece), piece)

        def fill(first, second, part=part, at=at):
            first[at, :] = part[0:piece, :]
            second[at, :] = part[piece : 2 * piece, :]

        pl.when(sc[7] == 0)(functools.partial(fill, even, odd))
        pl.when(sc[7] == 1)(functools.partial(fill, odd, even))
        cont[pl.ds(pl.multiple_of(place * cpiece, cpiece), cpiece), :] = part[2 * piece :, :]


def join_kernel(prompt, normed, sc, p0, p1, p2, p3, vec_ref, h_ref, *outs):
    width = p0.shape[1]
    for s, part in enumerate((p0, p1, p2, p3)):
        value = part[...].astype(F32)
        for c in range(4):

            def put(value=value, c=c):
                h_ref[:, c * width : (c + 1) * width] = value

            pl.when((sc[3] ^ s) == c)(put)
    if normed:
        a_ref, ap_ref = outs
        centered, _ = stats(h_ref[...])
        low = (centered * vec_ref[0, 4:5, :] + vec_ref[0, 5:6, :]).astype(BF16)
        a_ref[...] = low
        ap_ref[...] = low[:prompt]


def simple_call(kernel, sc, ins, shapes, specs=None, name="small", deps=()):
    return pl.pallas_call(
        strip(kernel, 0, len(ins), len(deps)),
        grid_spec=pltpu.PrefetchScalarGridSpec(
            num_scalar_prefetch=1,
            grid=(1,),
            in_specs=(specs or [whole_spec(v.shape) for v in ins]) + [ANY] * len(deps),
            out_specs=[whole_spec(v.shape) for v in shapes],
        ),
        out_shape=shapes,
        compiler_params=params(24),
        cost_estimate=cost(1e6, 3e6),
        name=name,
    )(sc, *ins, *deps)


def enter(prompt, cont, sc, vecs, normed):
    parts = enter_begin(prompt, cont, sc)
    return parts, enter_end(exchange_heads(parts), sc, vecs, normed, prompt.shape[0] // 4)


def enter_begin(prompt, cont, sc, deps=()):
    rows = lax.axis_size("row")
    half, width = prompt.shape[0] // 2, prompt.shape[1]
    piece, cpiece = half // 4, cont.shape[0] // 4
    tok = 2 * piece + cpiece
    even = prompt[:half]
    odd = prompt[half:]
    if rows > 2:
        even = lax.ppermute(even, "row", [(i, zig(2 * i, rows)) for i in range(rows)])
    odd = lax.ppermute(odd, "row", [(i, zig(2 * i + 1, rows)) for i in range(rows)])
    part = jax.ShapeDtypeStruct((tok, width), BF16)
    parts = simple_call(
        functools.partial(split_kernel, piece, cpiece), sc, [even, odd, cont], [part] * 4, name="split", deps=deps
    )
    return parts


def enter_end(parts, sc, vecs, normed, prompt, deps=()):
    tok, width = parts[0].shape
    shapes = [jax.ShapeDtypeStruct((tok, D), F32)]
    if normed:
        shapes += [jax.ShapeDtypeStruct((tok, D), BF16), jax.ShapeDtypeStruct((prompt, D), BF16)]
    specs = [whole_spec((tok, width))] * 4 + [pl.BlockSpec((1, 8, D), lambda i, sc: (sc[0], 0, 0))]
    return simple_call(
        functools.partial(join_kernel, prompt, normed), sc, [*parts, vecs], shapes, specs, "join", deps
    )


def leave(parts, sc, prompt_rows):
    return leave_end(sc, *leave_begin(exchange_heads(parts), sc, prompt_rows))


def leave_begin(parts, sc, prompt_rows, deps=()):
    width = parts[0].shape[1]
    half = prompt_rows // 2
    piece = half // 4
    cpiece = parts[0].shape[0] - 2 * piece
    shapes = [jax.ShapeDtypeStruct((n, width), BF16) for n in (half, half, 4 * cpiece)]
    even, odd, cont = simple_call(
        functools.partial(merge_kernel, piece, cpiece), sc, parts, shapes, name="merge", deps=deps
    )
    return even, odd, cont


def leave_end(sc, even, odd, cont, deps=()):
    rows = lax.axis_size("row")
    if rows > 2:
        even = lax.ppermute(even, "row", [(zig(2 * i, rows), i) for i in range(rows)])
    odd = lax.ppermute(odd, "row", [(zig(2 * i + 1, rows), i) for i in range(rows)])
    half, width = even.shape

    def stack(sc, first, second, out):
        out[0, 0:half, :] = first[...]
        out[0, half:, :] = second[...]

    shape = jax.ShapeDtypeStruct((1, 2 * half, width), BF16)
    return simple_call(stack, sc, [even, odd], [shape], name="rows", deps=deps)[0], cont[None]


def final_kernel(prompt, others, sc, *refs):
    g_ref, h_ref, p0_ref, rx_ref = refs[:4]
    rest = refs[4 : 4 + others]
    vec_ref = refs[4 + others]
    outs, small, da_ref, out_ref = refs[5 + others : 9 + others], refs[9 + others], refs[10 + others], refs[11 + others]
    da_ref[...] = p0_ref[...].astype(F32) + rx_ref[...].astype(F32)
    for ref in rest:
        da_ref[0:prompt, :] += ref[...].astype(F32)
    da1 = da_ref[...]
    centered, inverse = stats(h_ref[...])
    small[0:1, :] = colsum(da1 * centered)
    small[1:2, :] = colsum(da1)
    out_ref[...] = g_ref[...] + norm_back(da1, vec_ref[0, 4:5, :], centered, inverse)
    send_features(sc, out_ref, outs)


def final_norm(sc, grad, back, vecs, prompt, width, deps):
    tok = grad.shape[0]
    h_in, base, got, rest = back
    ins = [grad, h_in, base, got, *rest, vecs]
    shapes = [jax.ShapeDtypeStruct((tok, width), BF16)] * 4 + [
        jax.ShapeDtypeStruct((8, D), F32),
        jax.ShapeDtypeStruct((tok, D), F32),
        jax.ShapeDtypeStruct((tok, D), F32),
    ]
    specs = [whole_spec(v.shape) for v in ins[:-1]] + [
        pl.BlockSpec((1, 8, D), lambda i, sc: (sc[0], 0, 0))
    ]
    return simple_call(
        functools.partial(final_kernel, prompt, len(rest)), sc, ins, shapes, specs, "final_norm", deps
    )


class Reduce:

    def __init__(self, sc, keep, give, name, names, plan):
        self.sc, self.keep, self.give = sc, keep, give
        self.names, self.plan = list(names), list(plan)
        self.ready, self.waiting = 0, None
        self.send(name)

    def send(self, name):
        axis, bit = name
        count = lax.axis_size(axis)
        self.got = lax.ppermute(self.give, axis, [(i, i ^ bit) for i in range(count)])

    def step(self, deps=(), hold=False):
        rows, width = self.keep.shape
        if not self.plan:
            return []
        name = self.plan.pop(0)
        where = self.names.index(name)
        self.names.pop(where)
        before, size = 2**where, rows // 2 ** (where + 1)
        if name[0] == "x":
            slot = None
        else:
            slot = LAYERS * 8 + 1 + (bits_of("dp") + bits_of("row")).index(name)

        def add(sc, keep, got, new_keep, new_give):
            bit = 0 if slot is None else sc[slot]
            for a in range(before):
                for out, side in ((new_keep, bit), (new_give, 1 - bit)):
                    lo = (2 * a + side) * size
                    at = pl.ds(lo if slot is None else pl.multiple_of(lo, size), size)
                    out[a * size : (a + 1) * size, :] = add_low(keep[at, :], got[at, :])

        if size % 16:
            total = add_low(self.keep, self.got).reshape(before, 2, size, width)
            bit = 0 if slot is None else self.sc[slot]
            self.keep, self.give = (
                lax.dynamic_index_in_dim(total, side, 1, keepdims=False).reshape(rows // 2, width)
                for side in (bit, 1 - bit)
            )
        else:
            shape = jax.ShapeDtypeStruct((rows // 2, width), BF16)
            self.keep, self.give = simple_call(
                add, self.sc, [self.keep, self.got], [shape] * 2, name="add", deps=deps
            )
        if hold and name[0] != "dp":
            self.waiting = name
        else:
            self.send(name)
        return [self.give]

    def release(self, deps):
        if self.waiting is not None:
            self.give = behind([self.give], deps)[0]
            self.send(self.waiting)
            self.waiting = None

    def finish(self):
        while self.plan:
            self.step()
        return [self.keep, self.got]


def bits_of(axis):
    bits, bit = [], lax.axis_size(axis) // 2
    while bit:
        bits.append((axis, bit))
        bit //= 2
    return bits


def reorder(value):
    shape = value.shape
    value = value.reshape((2, 2) + shape[1:])
    value = jnp.where(lax.axis_index("core") == 1, value[:, ::-1], value)
    value = jnp.where(lax.axis_index("x") == 1, value[::-1], value)
    return value.reshape(shape)


def narrow_kernel(width, sc, *refs):
    smalls, qkvs, last_ref, out = refs[:LAYERS], refs[LAYERS : 2 * LAYERS], refs[2 * LAYERS], refs[-1]
    out[...] = jnp.zeros_like(out)
    for b in range(NB):
        total = jnp.zeros((16, D), F32)
        qkv = jnp.zeros((HEADS_COL, 256), F32)
        for i in range(LAYERS):
            mine = sc[i * 8] == b
            total = total + jnp.where(mine, smalls[i][...], 0.0)
            qkv = qkv + jnp.where(mine, qkvs[i][:, 0, :], 0.0)
        gain = jnp.where(sc[0] == b, last_ref[0:2, :], 0.0)
        for i in range(1, LAYERS):
            gain = gain + jnp.where(sc[i * 8] == b, smalls[i - 1][8:10, :], 0.0)
        rows = jnp.concatenate([total[5:6], total[4:5], total[6:8], gain], axis=0)
        for s in range(4):
            out[s, b, 0:1, :] = total[s : s + 1]
            for c in range(4):

                def put(s=s, b=b, c=c, rows=rows):
                    out[s, b, 1:7, 0:width] = rows[:, c * width : (c + 1) * width]

                pl.when((sc[3] ^ s) == c)(put)
        for h in range(HEADS_COL):
            out[0, b, 7:8, h * 256 : (h + 1) * 256] = qkv[h : h + 1]


def end_slot():
    return LAYERS * 8 + 1 + len(bits_of("dp")) + len(bits_of("row"))


def pack_end(sc, parts, width):
    slot = end_slot()
    share = parts[0].shape[0]

    def end(sc, *refs):
        up, down, out = refs[-3:]
        for k in range(NB):
            ka, ga, kb, gb = refs[4 * k : 4 * k + 4]
            left = ka[...].astype(F32) + ga[...].astype(F32)
            right = kb[...].astype(F32) + gb[...].astype(F32)
            for b in range(NB):

                def put(b=b, left=left, right=right):
                    up[b] = left
                    down[b] = right[:, 0:D]
                    out[b] = right[:, D : D + width]

                pl.when(sc[slot + b] == k)(put)

    shapes = [jax.ShapeDtypeStruct((NB, share, n), F32) for n in (D, D, width)]
    return simple_call(end, sc, parts, shapes, name="pack_end")


def qkv_end(sc, parts, width):
    slot = end_slot()
    share = parts[0].shape[0]

    def end(sc, *refs):
        out = refs[-1]
        for k in range(NB):
            total = refs[2 * k][...].astype(F32) + refs[2 * k + 1][...].astype(F32)
            for b in range(NB):

                def put(b=b, total=total):
                    for h in range(HEADS_COL):
                        for j, lane in enumerate((0, 128, 192)):
                            at = h * 256 + lane
                            out[b, j, :, h * HD : (h + 1) * HD] = total[:, at : at + HD]

                pl.when(sc[slot + b] == k)(put)

    shape = jax.ShapeDtypeStruct((NB, 3, share, width), F32)
    return simple_call(end, sc, parts, [shape], name="qkv_end")[0].transpose(0, 2, 1, 3)


def narrow_end(sc, value, got, width):
    def end(sc, value, got, bup, qv, *vecs):
        for b in range(NB):
            total = value[b] + got[b]
            bup[b : b + 1, :] = total[0:1]
            for k, out in enumerate(vecs):
                out[b : b + 1, :] = total[1 + k : 2 + k, 0:width]
            for h in range(HEADS_COL):
                for j, lane in enumerate((0, 192)):
                    at = h * 256 + lane
                    qv[b, j : j + 1, h * HD : (h + 1) * HD] = total[7:8, at : at + HD]

    shapes = [jax.ShapeDtypeStruct((NB, D), F32), jax.ShapeDtypeStruct((NB, 2, width), F32)]
    shapes += [jax.ShapeDtypeStruct((NB, width), F32)] * 6
    return simple_call(end, sc, [value, got], shapes, name="narrow_end")


def sum_small(value):
    got = swap_core(jnp.stack([value[1], value[3]]))
    near, far = value[0] + got[0], value[2] + got[1]
    value = near + swap_x(far)
    steps = bits_of("row") + bits_of("dp")
    for k, (axis, bit) in enumerate(steps):
        got = lax.ppermute(value, axis, [(i, i ^ bit) for i in range(lax.axis_size(axis))])
        if k + 1 < len(steps):
            value = value + got
    return value, got


def per_device(
    x_prompt,
    x_cont,
    seg_ids,
    layer_map,
    w_qkv,
    bias_qv,
    w_out,
    b_out,
    w_up,
    b_up,
    w_down,
    b_down,
    ln1_gain,
    ln1_bias,
    ln2_gain,
    ln2_bias,
    cot_prompt,
    cot_cont,
):
    rows, dps = lax.axis_size("row"), lax.axis_size("dp")
    prompt_row, cont = x_prompt.shape[1], x_cont.shape[1]
    width = x_prompt.shape[2]
    chunk = prompt_row // 2
    piece, cpiece = chunk // 4, cont // 4
    prompt = 2 * piece
    dims = (rows, piece, cpiece, chunk, cont)
    my_row, my_x = lax.axis_index("row"), lax.axis_index("x")
    my_col = my_x * 2 + lax.axis_index("core")

    layer_map = layer_map.astype(jnp.int32)
    places = jnp.arange(LAYERS, dtype=jnp.int32)
    blocks = jnp.arange(NB, dtype=jnp.int32)
    first_use = jnp.min(jnp.where(layer_map[None] == blocks[:, None], places[None], 99), axis=1)
    rank_of = jnp.sum((first_use[None] < first_use[:, None]).astype(jnp.int32), axis=1)
    rank_layer = jnp.sum(jnp.where(layer_map[:, None] == blocks[None], rank_of[None], 0), axis=1)
    later = (rank_layer[None] == rank_layer[:, None]) & (places[None] > places[:, None])
    fresh = 1 - jnp.max(later.astype(jnp.int32), axis=1)
    after = jnp.concatenate([layer_map[1:], layer_map[-1:]])

    def fill(value):
        return jnp.broadcast_to(value, (LAYERS,)).astype(jnp.int32)

    sc = jnp.stack(
        [layer_map, rank_layer, after, fill(my_col), fill(my_x), fill(my_row), fresh, fill(my_row % 2)],
        axis=1,
    ).reshape(-1)
    my_dp = lax.axis_index("dp")
    extra = [my_dp * rows + my_row]
    ends = [rank_of[b] for b in range(NB)]
    extra += [(lax.axis_index(a) // b) % 2 for a, b in bits_of("dp") + bits_of("row")]
    sc = jnp.concatenate([sc, jnp.stack(extra + ends).astype(jnp.int32)])

    heads = w_qkv.reshape(NB, -1, 3, HEADS_COL, HD)
    zero = jnp.zeros_like(heads[:, :, 0])
    packed = jnp.stack([heads[:, :, 0], zero, heads[:, :, 1], heads[:, :, 2]], axis=3)
    packed = packed.reshape(NB, -1, D)

    def by_block(stacked):
        nothing = jnp.zeros((), stacked.dtype)
        return [
            sum(jnp.where(rank_of[b] == k, stacked[b], nothing) for b in range(NB)) for k in range(NB)
        ]

    packed = by_block(packed)
    pair = bias_qv.astype(F32).reshape(NB, 2, HEADS_COL, HD)
    none = jnp.zeros((NB, HEADS_COL, 2, HD), F32)
    bqkv = jnp.concatenate([pair[:, 0][:, :, None], none, pair[:, 1][:, :, None]], axis=2).reshape(NB, 1, D)

    def flat(value):
        return value.reshape(NB, -1)

    narrow = jnp.concatenate(
        [flat(v) for v in (b_out, b_down, ln2_gain, ln2_bias, ln1_gain, ln1_bias, b_up)], axis=1
    )
    narrow = jnp.stack(exchange_heads([narrow] * 4))
    narrow = reorder(narrow.astype(F32))
    vecs = narrow[:, :, : 6 * width].reshape(4, NB, 6, width).transpose(1, 2, 0, 3).reshape(NB, 6, D)
    vecs = jnp.concatenate([vecs, jnp.zeros((NB, 2, D), F32)], axis=1)
    bup = narrow[:, :, 6 * width :].transpose(1, 0, 2).reshape(NB, 4, 1, D)

    pack_local = jnp.concatenate(
        [w_up, w_down, w_out, jnp.zeros(w_out.shape[:2] + (64,), BF16)], axis=2
    )
    share = D // (dps * rows)
    packs = []
    for local in by_block(pack_local):
        pack = lax.all_gather(local, ("x", "core", "dp", "row"), axis=0)
        if share % 16:
            packs.append(pack.reshape(4, 1, D, PACK))
        else:
            packs.append(pack.reshape(4, dps * rows, share, PACK))

    def places_of(size):
        index = jnp.arange(4 * size, dtype=jnp.int32)
        return size * ((index // size) ^ my_col) + index % size

    ppos, cpos = places_of(piece), places_of(cpiece)
    seg = reorder(seg_ids[0].astype(jnp.int32).reshape(4, cpiece)).reshape(cont)
    pos = [ppos[None], ppos[:, None], cpos[None], cpos[:, None], seg[None], seg[:, None]]

    tok = prompt + cpiece
    direct = dps * rows <= 8
    parts, (hidden, low, low_prompt) = enter(x_prompt[0], x_cont[0], sc, vecs, True)
    if direct:
        first = held(packed[0][None], [parts[0]])
        first = [first] + gather_begin(first, ("dp", "row"))
        wqkv_first = gather_end(sc, first, LAYERS * 8, deps=[low])
    else:
        wqkv_all = lax.all_gather(jnp.stack(packed), ("dp", "row"), axis=1, tiled=True)
        wqkv_first = wqkv_all
    saved = []
    for i in range(LAYERS):
        last = i == LAYERS - 1
        own, oth = spread(low, low_prompt)
        if i == 1 and direct:
            wqkv_all = gather_end(sc, rest, LAYERS * 8, [wqkv_first], deps=[low])
        weight = wqkv_first if i == 0 else wqkv_all
        res = attn_fwd(i, sc, own, oth, weight, bqkv, pos, dims)
        o_send, (q, kv, lse, lsec) = res[:4], res[4:]
        if i == 0 and direct:
            rest = held(jnp.stack(packed[1:]), [lsec])
            rest = [rest] + gather_begin(rest, ("dp", "row"))
        deps = []
        if i == 2:
            cot_parts = enter_begin(cot_prompt[0], cot_cont[0], sc, [lsec])
            deps = [cot_parts[0]]
        if i == 3:
            grad = enter_end(cot_got, sc, vecs, False, prompt, [lsec])[0]
            deps = [grad]
        o_got = exchange_heads(o_send)
        avail = packs[: min(i, NB - 1) + 1]
        res = mlp_fwd(i, sc, hidden, o_got, vecs, bup, avail, prompt, last, width, deps)
        if i == 2:
            cot_got = exchange_heads(cot_parts)
        saved.append((hidden, own, oth, o_send, q, kv, lse, lsec, o_got, res[0], res[1]))
        hidden = res[2]
        if not last:
            low, low_prompt = res[3], res[4]
    y_send = exchange_heads(res[3:7])

    acc_pack = blank((NB, 2, D, PACK), BF16)
    back = None
    small = [None] * LAYERS
    small_qkv = [None] * LAYERS
    sums = []
    done_pack = [None] * NB
    done_qkv = [None] * NB
    dws = [None] * LAYERS
    dp_bits, row_bits = bits_of("dp"), bits_of("row")
    bits = dp_bits + row_bits
    top, x_bit = row_bits[0], ("x", 1)
    fence = []
    for i in reversed(range(LAYERS)):
        h_in, own, oth, o_send, q, kv, lse, lsec, o_got, h1, up = saved[i]
        res = mlp_bwd(i, sc, grad, back, h1, up, vecs, packs, prompt, fence)
        tokens, mine, theirs, grad = res[:4]
        do_send, small[i] = res[4:8], res[8]
        fence = []
        for part in sums:
            if part.ready <= 2 * (LAYERS - i):
                fence += part.step([small[i]])
        if i == LAYERS - 1:
            y_parts = leave_begin(y_send, sc, prompt_row, [small[i]])
            fence.append(y_parts[0])
        *do_send, tokens, theirs = behind([*do_send, tokens, theirs], fence)
        do_got = exchange_heads(do_send)
        ins = [tokens, swap_core(tokens), mine, swap_core(theirs)]
        ins += [o_got[0], o_got[2], swap_core(o_got[1]), swap_core(o_got[3])]
        if i < NB:
            res = dw_last(i, sc, ins, acc_pack, dps)
            keep_a, give_a, keep_b, give_b, acc_pack, token = res
            give_a, give_b = behind([give_a, give_b], do_got[1:])
            left = [n for n in bits if n != top]
            done_pack[i] = [
                Reduce(sc, keep_a, give_a, x_bit, bits, row_bits + dp_bits[::-1]),
                Reduce(sc, keep_b, give_b, top, [x_bit] + left, [x_bit] + row_bits[1:] + dp_bits[::-1]),
            ]
            sums += done_pack[i]
            fence = [token]
            if i + 1 < NB:
                fence += done_qkv[i + 1].step([token])
        else:
            fence = []
        fence += [part.give for part in sums]
        res = attn_bwd(i, sc, do_got, o_send, q, kv, lse, lsec, wqkv_all, pos, dims, fence)
        da_mine, da_theirs, dq, dkv, small_qkv[i] = res
        fence = []
        for part in sums if i > 0 else done_pack[0]:
            if part.ready <= 2 * (LAYERS - i) + 1:
                fence += part.step([small_qkv[i]], i > 0)
        if i == LAYERS - 1:
            y_prompt, y_cont = leave_end(sc, *y_parts, deps=[small_qkv[i]])
            fence.append(y_prompt)
        if i > 0:
            base, got, rest = collect(da_mine, behind([da_theirs], fence)[0], tok, prompt)
            dws[i], token = dw_qkv(i, sc, own, oth, dq, dkv)
        else:
            dws[i], token = dw_qkv(i, sc, own, oth, dq, dkv, fence)
            fence = []
            for part in done_pack[0]:
                fence += part.step([token])
            base, got, rest = collect(da_mine, behind([da_theirs], fence)[0], tok, prompt)
        fence = [token]
        if i >= NB:
            acc_pack, token = dw_mlp(i, sc, ins, acc_pack, [base])
            fence.append(token)
        for part in sums:
            part.release([got, *rest, token])
        if i < NB:
            keep, give = qkv_total(sc, i, dws[i:], dps, [got])
            done_qkv[i] = Reduce(sc, keep, give, top, left, row_bits[1:] + dp_bits[::-1])
            done_qkv[i].ready = 2 * (LAYERS - i) + 3
            sums.append(done_qkv[i])
            fence.append(give)
        back = (h_in, base, got, rest)
        sums = [part for part in sums if part.plan]

    for part in sums:
        if part.ready <= 2 * LAYERS + 2:
            step = part.step([got])
            if part not in done_pack[0]:
                continue
            fence += step
    res = final_norm(sc, grad, back, vecs, prompt, width, fence)
    dx_parts = leave_begin(exchange_heads(res[:4]), sc, prompt_row)
    for part in sums:
        part.step([dx_parts[0]])
    dx_prompt, dx_cont = leave_end(sc, *dx_parts)
    for part in sums:
        part.step([dx_prompt])
    for part in sums:
        part.step()
    g_up, g_down, g_out = pack_end(sc, [v for parts in done_pack for p in parts for v in p.finish()], width)
    g_qkv = qkv_end(sc, [v for part in done_qkv for v in part.finish()], width)

    shape = jax.ShapeDtypeStruct((4, NB, 8, D), F32)
    narrow = simple_call(
        functools.partial(narrow_kernel, width), sc, [*small, *small_qkv, res[4]], [shape], name="narrow"
    )[0]
    g_bup, g_qv, *g_vec = narrow_end(sc, *sum_small(narrow), width)
    return (
        y_prompt,
        y_cont,
        dx_prompt,
        dx_cont,
        g_qkv,
        g_qv,
        g_out,
        g_vec[0],
        g_up,
        g_bup,
        g_down,
        g_vec[1],
        g_vec[4],
        g_vec[5],
        g_vec[2],
        g_vec[3],
    )


def solution(mesh):
    dps, rows = mesh.shape["dp"], mesh.shape["row"]
    fine = Mesh(mesh.devices.reshape(dps, rows, 2, 2), ("dp", "row", "x", "core"))
    col = ("x", "core")
    both = ("dp", "row")
    tokens = P("dp", "row", col)
    narrow = P(None, col)
    wide = P(None, both, col)
    in_specs = (
        tokens,
        tokens,
        P("dp", "row"),
        P(),
        P(None, both, None, col),
        P(None, None, col),
        wide,
        narrow,
        wide,
        narrow,
        wide,
        narrow,
        narrow,
        narrow,
        narrow,
        narrow,
        tokens,
        tokens,
    )
    out_specs = (
        tokens,
        tokens,
        tokens,
        tokens,
        P(None, both, None, col),
        P(None, None, col),
        wide,
        narrow,
        wide,
        narrow,
        wide,
        narrow,
        narrow,
        narrow,
        narrow,
        narrow,
    )
    return jax.shard_map(
        per_device, mesh=fine, in_specs=in_specs, out_specs=out_specs, check_vma=False
    )
```

```python
import functools

import jax
import jax.numpy as jnp
from jax import lax
from jax.experimental import pallas as pl
from jax.experimental.pallas import tpu as pltpu
from jax.sharding import Mesh
from jax.sharding import PartitionSpec as P

D = 768
HD = 64
LAYERS = 6
NB = 3
HEADS_COL = 3
PACK = 1792
HALF = 896
NORM_EPS = 1e-05
MASK_FILL = -1000000000.0
GELU_COEF = 0.7978845608028654
F32 = jnp.float32
BF16 = jnp.bfloat16
MIB = 1024 * 1024


def nn(a, b):
    return lax.dot_general(a, b, (((1,), (0,)), ((), ())), preferred_element_type=F32)


def nt(a, b):
    return lax.dot_general(a, b, (((1,), (1,)), ((), ())), preferred_element_type=F32)


def tn(a, b):
    return lax.dot_general(a, b, (((0,), (0,)), ((), ())), preferred_element_type=F32)


def stats(hidden):
    mean = jnp.sum(hidden, axis=1, keepdims=True) * (1.0 / D)
    square = jnp.sum(hidden * hidden, axis=1, keepdims=True) * (1.0 / D)
    inverse = lax.rsqrt(square - mean * mean + NORM_EPS)
    return (hidden - mean) * inverse, inverse


def norm_back(grad, gain, centered, inverse):
    scaled = grad * gain
    first = jnp.sum(scaled, axis=1, keepdims=True) * (1.0 / D)
    second = jnp.sum(scaled * centered, axis=1, keepdims=True) * (1.0 / D)
    return inverse * (scaled - first - centered * second)


def colsum(value):
    return jnp.sum(value, axis=0, keepdims=True)


def to_row(column):
    rows = column.shape[0]
    return jnp.transpose(jnp.broadcast_to(column, (rows, 128)))[0:1, :]


class Row:
    def __init__(self, ref, layer):
        self.ref, self.base = ref, layer * 8

    def __getitem__(self, j):
        return self.ref[self.base + j]


def strip(kernel, layer, count, deps):
    def run(sc, *refs):
        kernel(Row(sc, layer), *refs[:count], *refs[count + deps :])

    return run


def params(limit, **more):
    return pltpu.CompilerParams(vmem_limit_bytes=limit * MIB, **more)


def cost(flops, nbytes, trans=0):
    return pl.CostEstimate(flops=int(flops), bytes_accessed=int(nbytes), transcendentals=int(trans))


class Weights:

    def __init__(self, sc, packs, wout, wud, sems):
        self.sc, self.packs, self.sems = sc, packs, sems
        self.dst = ((wout, 1536, 256), (wud, 0, 1536))
        self.parts, self.size = packs[0].shape[1], packs[0].shape[2]

    def start(self, order):
        if len(self.packs) == 1:
            self.start_from(self.packs[0], order)
        else:
            for k, src in enumerate(self.packs):
                pl.when(self.sc[1] == k)(functools.partial(self.start_from, src, order))

    def start_from(self, src, order):
        for kind in order:
            dst, lo, size = self.dst[kind]
            for s in range(4):
                for j in range(self.parts):
                    rows = pl.ds(j * self.size, self.size)
                    pltpu.make_async_copy(
                        src.at[self.sc[3] ^ s, j, :, pl.ds(lo, size)],
                        dst.at[s, rows],
                        self.sems.at[kind, s],
                    ).start()

    def wait(self, kind, s):
        dst = self.dst[kind][0].at[s]
        pltpu.make_async_copy(dst, dst, self.sems.at[kind, s]).wait()


def mlp_fwd_kernel(ranks, last, prompt, sc, *refs):
    h_ref, o0, o1, o2, o3, vec_ref, bup_ref, nvec_ref = refs[:8]
    outs = refs[8 + ranks :]
    h1_ref, u_ref, h_out = outs[:3]
    wout, wud, sems = outs[-3:]
    weights = Weights(sc, refs[8 : 8 + ranks], wout, wud, sems)
    weights.start((0, 1))
    total = h_ref[...] + vec_ref[0, 0:1, :]
    for s, o_ref in enumerate((o0, o1, o2, o3)):
        weights.wait(0, s)
        total = total + nt(o_ref[...], wout[s])
    h1_ref[...] = total
    centered, _ = stats(total)
    a2 = (centered * vec_ref[0, 2:3, :] + vec_ref[0, 3:4, :]).astype(BF16)
    h_out[...] = total + vec_ref[0, 1:2, :]
    for s in range(4):
        weights.wait(1, s)
        bias = bup_ref[0, pl.ds(sc[3] ^ s, 1), 0, :]
        up = nn(a2, wud[s, :, 0:768]) + bias
        u_ref[s] = up.astype(BF16)
        act = 0.5 * up * (1.0 + jnp.tanh(GELU_COEF * (up + 0.044715 * up * up * up)))
        h_out[...] += nt(act.astype(BF16), wud[s, :, 768:1536])
    if last:
        y_refs = outs[3:7]
        send_features(sc, h_out, y_refs)
    else:
        a_ref, ap_ref = outs[3:5]
        centered, _ = stats(h_out[...])
        nxt = (centered * nvec_ref[0, 4:5, :] + nvec_ref[0, 5:6, :]).astype(BF16)
        a_ref[...] = nxt
        ap_ref[...] = nxt[:prompt]


def send_features(sc, value, refs):
    width = refs[0].shape[1]
    for s, ref in enumerate(refs):
        for c in range(4):

            def put(ref=ref, c=c):
                ref[...] = value[:, c * width : (c + 1) * width].astype(BF16)

            pl.when((sc[3] ^ s) == c)(put)


def whole_spec(shape):
    return pl.BlockSpec(shape, lambda i, sc: (0,) * len(shape))


def vec_specs(layer):
    at = layer * 8
    return [
        pl.BlockSpec((1, 8, D), lambda i, sc: (sc[at], 0, 0)),
        pl.BlockSpec((1, 4, 1, D), lambda i, sc: (sc[at], 0, 0, 0)),
        pl.BlockSpec((1, 8, D), lambda i, sc: (sc[at + 2], 0, 0)),
    ]


WSCR = [
    pltpu.VMEM((4, D, 256), BF16),
    pltpu.VMEM((4, D, 1536), BF16),
    pltpu.SemaphoreType.DMA((2, 4)),
]
ANY = pl.BlockSpec(memory_space=pl.ANY)


def mlp_fwd(layer, sc, hidden, o_parts, vecs, bup, packs, prompt, last, width, deps=()):
    tok = hidden.shape[0]
    shapes = [
        jax.ShapeDtypeStruct((tok, D), F32),
        jax.ShapeDtypeStruct((4, tok, D), BF16),
        jax.ShapeDtypeStruct((tok, D), F32),
    ]
    if last:
        shapes += [jax.ShapeDtypeStruct((tok, width), BF16)] * 4
    else:
        shapes += [jax.ShapeDtypeStruct((tok, D), BF16), jax.ShapeDtypeStruct((prompt, D), BF16)]
    out_specs = [whole_spec(v.shape) for v in shapes]
    ins = [hidden, *o_parts, vecs, bup, vecs, *packs]
    kernel = functools.partial(mlp_fwd_kernel, len(packs), last, prompt)
    return pl.pallas_call(
        strip(kernel, layer, len(ins), len(deps)),
        grid_spec=pltpu.PrefetchScalarGridSpec(
            num_scalar_prefetch=1,
            grid=(1,),
            in_specs=[whole_spec((tok, D))]
            + [whole_spec((tok, 256))] * 4
            + vec_specs(layer)
            + [ANY] * (len(packs) + len(deps)),
            out_specs=out_specs,
            scratch_shapes=WSCR,
        ),
        out_shape=shapes,
        compiler_params=params(44),
        cost_estimate=cost(2 * tok * D * 6912, 16e6, tok * 3072),
        name="mlp_fwd",
    )(sc, *ins, *deps)


def mlp_bwd_kernel(ranks, others, first, prompt, sc, *refs):
    if first:
        g_ref, refs = refs[0], refs[1:]
    else:
        nin = 4 + 2 * others
        g_ref, hn_ref, p0_ref, rx_ref = refs[:4]
        rest = refs[4:nin]
        refs = refs[nin:]
    h1_ref, u_hbm, vec_ref, nvec_ref = refs[:4]
    outs = refs[4 + ranks :]
    tok_ref, mine_ref, theirs_ref, g1_ref, d0, d1, d2, d3, small_ref = outs[:9]
    wout, wud, sems, u_ref, usem = outs[9:]
    loads = [pltpu.make_async_copy(u_hbm.at[s], u_ref.at[s], usem.at[s]) for s in range(4)]
    for copy in loads:
        copy.start()
    weights = Weights(sc, refs[4 : 4 + ranks], wout, wud, sems)
    weights.start((1, 0))
    small_ref[...] = jnp.zeros_like(small_ref)
    if first:
        grad = g_ref[...]
    else:
        g1_ref[...] = p0_ref[...].astype(F32) + rx_ref[...].astype(F32)
        for ref in rest:
            g1_ref[0:prompt, :] += ref[...].astype(F32)
        da1 = g1_ref[...]
        centered, inverse = stats(hn_ref[...])
        small_ref[8:9, :] = colsum(da1 * centered)
        small_ref[9:10, :] = colsum(da1)
        grad = g_ref[...] + norm_back(da1, nvec_ref[0, 4:5, :], centered, inverse)
    gm = grad.astype(BF16)
    tok_ref[1] = gm
    small_ref[4:5, :] = colsum(gm.astype(F32))
    for s in range(4):
        weights.wait(1, s)
        dm = nn(gm, wud[s, :, 768:1536])
        loads[s].wait()
        up = u_ref[s].astype(F32)
        square = up * up
        tanh = jnp.tanh(GELU_COEF * up * (1.0 + 0.044715 * square))
        slope = 0.5 * (1.0 + tanh) + 0.5 * up * (1.0 - tanh * tanh) * (
            GELU_COEF * (1.0 + 3.0 * 0.044715 * square)
        )
        du = (dm * slope).astype(BF16)
        side = mine_ref if s % 2 == 0 else theirs_ref
        side[s // 2] = du
        side[2 + s // 2] = (0.5 * up * (1.0 + tanh)).astype(BF16)
        small_ref[s : s + 1, :] = colsum(du.astype(F32))
        term = nt(du, wud[s, :, 0:768])
        if s == 0:
            g1_ref[...] = term
        else:
            g1_ref[...] += term
    da2 = g1_ref[...]
    centered, inverse = stats(h1_ref[...])
    gain = vec_ref[0, 2:3, :]
    tok_ref[0] = (centered * gain + vec_ref[0, 3:4, :]).astype(BF16)
    small_ref[6:7, :] = colsum(da2 * centered)
    small_ref[7:8, :] = colsum(da2)
    grad = grad + norm_back(da2, gain, centered, inverse)
    g1_ref[...] = grad
    go = grad.astype(BF16)
    tok_ref[2] = go
    small_ref[5:6, :] = colsum(go.astype(F32))
    for s, ref in enumerate((d0, d1, d2, d3)):
        weights.wait(0, s)
        ref[...] = nn(go, wout[s]).astype(BF16)


def mlp_bwd(layer, sc, grad, back, h1, up, vecs, packs, prompt, deps=()):
    tok = grad.shape[0]
    first = back is None
    others = 0 if first else len(back[3])
    shapes = [
        jax.ShapeDtypeStruct((3, tok, D), BF16),
        jax.ShapeDtypeStruct((4, tok, D), BF16),
        jax.ShapeDtypeStruct((4, tok, D), BF16),
        jax.ShapeDtypeStruct((tok, D), F32),
    ]
    shapes += [jax.ShapeDtypeStruct((tok, 256), BF16)] * 4
    shapes += [jax.ShapeDtypeStruct((16, D), F32)]
    extra = [] if first else [back[0], back[1], back[2], *back[3]]
    specs = vec_specs(layer)
    ins = [grad, *extra, h1, up, vecs, vecs, *packs]
    kernel = functools.partial(mlp_bwd_kernel, len(packs), others // 2, first, prompt)
    return pl.pallas_call(
        strip(kernel, layer, len(ins), len(deps)),
        grid_spec=pltpu.PrefetchScalarGridSpec(
            num_scalar_prefetch=1,
            grid=(1,),
            in_specs=[whole_spec(v.shape) for v in [grad, *extra, h1]]
            + [ANY, specs[0], specs[2]]
            + [ANY] * (len(packs) + len(deps)),
            out_specs=[whole_spec(s.shape) for s in shapes],
            scratch_shapes=WSCR + [pltpu.VMEM((4, tok, D), BF16), pltpu.SemaphoreType.DMA((4,))],
        ),
        out_shape=shapes,
        compiler_params=params(48),
        cost_estimate=cost(2 * tok * D * 6912, 16e6, tok * 3072),
        name="mlp_bwd",
    )(sc, *ins, *deps)


def attn_fwd_kernel(dims, sc, *refs):
    rows, piece, cpiece, chunk, cont = dims
    npc = 4 * rows
    own, oth = refs[:4], refs[4:npc]
    w_ref, b_ref, prow, pcol, crow, ccol, srow, scol = refs[npc : npc + 8]
    outs = refs[npc + 8 :]
    o_refs = outs[:4]
    q_ref, kv_ref, lse_ref, lsec_ref, m_s, l_s, acc_s = outs[4:]
    head = pl.program_id(0)
    base_b = chunk * rows
    base_c = 2 * chunk * rows
    weight = w_ref[0]
    bias = b_ref[0]
    for s in range(4):
        mixed = nn(own[s][...], weight) + bias
        low_q = (mixed[:, 0:128].astype(BF16).astype(F32) * 0.125).astype(BF16)
        low_kv = mixed[:, 128:256].astype(BF16)
        q_ref[0, s * piece : (s + 1) * piece, :] = low_q[0:piece]
        q_ref[0, chunk + s * piece : chunk + (s + 1) * piece, :] = low_q[piece : 2 * piece]
        q_ref[0, 2 * chunk + s * cpiece : 2 * chunk + (s + 1) * cpiece, :] = low_q[2 * piece :]
        kv_ref[0, s * piece : (s + 1) * piece, :] = low_kv[0:piece]
        kv_ref[0, base_b + s * piece : base_b + (s + 1) * piece, :] = low_kv[piece : 2 * piece]
        kv_ref[0, base_c + s * cpiece : base_c + (s + 1) * cpiece, :] = low_kv[2 * piece :]
    for t in range(1, rows):
        for s in range(4):
            low_kv = (nn(oth[(t - 1) * 4 + s][...], weight[:, 128:256]) + bias[:, 128:256]).astype(BF16)
            at = t * chunk + s * piece
            kv_ref[0, at : at + piece, :] = low_kv[0:piece]
            kv_ref[0, base_b + at : base_b + at + piece, :] = low_kv[piece : 2 * piece]
    lanes = lax.broadcasted_iota(jnp.int32, (1, 128), 1)
    upper = lanes >= 64
    sub = min(256, chunk)

    def begin(query, keys, mask):
        scores = nt(query, keys)
        if mask is not None:
            size = mask.shape[1]
            tail = jnp.where(mask, scores[:, -size:], MASK_FILL)
            if size == scores.shape[1]:
                scores = tail
            else:
                scores = jnp.concatenate([scores[:, :-size], tail], axis=1)
        top = jnp.max(scores, axis=1, keepdims=True)
        prob = jnp.exp(scores - top)
        return top, jnp.sum(prob, axis=1, keepdims=True), nn(prob.astype(BF16), keys)

    def put(out, row, size):
        low = jnp.where(upper, out, 0.0)

        def first_head():
            value = pltpu.roll(low, 64, 1).astype(BF16)
            store(value, row, size, 0, False)

        def second_head():
            store(low.astype(BF16), row, size, 0, True)

        def third_head():
            store(pltpu.roll(low, 64, 1).astype(BF16), row, size, 1, False)

        pl.when(head == 0)(first_head)
        pl.when(head == 1)(second_head)
        pl.when(head == 2)(third_head)

    def store(value, row, size, half, add):
        s, at = row
        lo = half * 128
        if add:
            o_refs[s][at : at + size, lo : lo + 128] = (
                o_refs[s][at : at + size, lo : lo + 128] + value
            )
        else:
            o_refs[s][at : at + size, lo : lo + 128] = value

    for i in range(chunk // sub):
        at = i * sub
        mask = prow[0:1, :] <= pcol[at : at + sub, :]
        top, total, acc = begin(q_ref[0, at : at + sub, :], kv_ref[0, 0:chunk, :], mask)
        m_s[at : at + sub, :], l_s[at : at + sub, :], acc_s[at : at + sub, :] = top, total, acc
        at_b = chunk + at
        top, total, acc = begin(
            q_ref[0, at_b : at_b + sub, :], kv_ref[0, 0 : base_b + chunk, :], mask
        )
        m_s[at_b : at_b + sub, :], l_s[at_b : at_b + sub, :] = top, total
        acc_s[at_b : at_b + sub, :] = acc
    my_row = sc[5]
    for t in range(1, rows):
        before = lax.rem(my_row + t, rows) < my_row
        q_at = jnp.where(before, 0, chunk)
        k_at = jnp.where(before, t * chunk, base_b + t * chunk)
        keys = kv_ref[0, pl.ds(pl.multiple_of(k_at, 128), chunk), :]
        for i in range(chunk // sub):
            at = pl.ds(pl.multiple_of(q_at + i * sub, 128), sub)
            scores = nt(q_ref[0, at, :], keys)
            old = m_s[at, :]
            top = jnp.maximum(old, jnp.max(scores, axis=1, keepdims=True))
            scale = jnp.exp(old - top)
            prob = jnp.exp(scores - top)
            m_s[at, :] = top
            l_s[at, :] = l_s[at, :] * scale + jnp.sum(prob, axis=1, keepdims=True)
            acc_s[at, :] = acc_s[at, :] * scale + nn(prob.astype(BF16), keys)
    for half in range(2):
        for s in range(4):
            at = half * chunk + s * piece
            total = l_s[at : at + piece, :]
            put(acc_s[at : at + piece, :] / total, (s, half * piece), piece)
        for i in range(chunk // sub):
            at = half * chunk + i * sub
            column = m_s[at : at + sub, :] + jnp.log(l_s[at : at + sub, :])
            lse_ref[0, half, :, i * sub : (i + 1) * sub] = to_row(column)
    mask = (crow[0:1, :] <= ccol[...]) & (srow[0:1, :] == scol[...])
    query = q_ref[0, 2 * chunk : 2 * chunk + cont, :]
    top, total, acc = begin(query, kv_ref[0], mask)
    out = acc / total
    for s in range(4):
        put(out[s * cpiece : (s + 1) * cpiece], (s, 2 * piece), cpiece)
    lsec_ref[0] = to_row(top + jnp.log(total))


def attn_inputs(pos):
    return [pl.BlockSpec(v.shape, lambda i, sc: (0, 0)) for v in pos]


def attn_fwd(layer, sc, own, oth, w_all, b_all, pos, dims, deps=()):
    single = w_all.shape[0] == 1
    rows, piece, cpiece, chunk, cont = dims
    tok = own[0].shape[0]
    nq, nk = 2 * chunk + cont, 2 * chunk * rows + cont
    shapes = [jax.ShapeDtypeStruct((tok, 256), BF16)] * 4 + [
        jax.ShapeDtypeStruct((3, nq, 128), BF16),
        jax.ShapeDtypeStruct((3, nk, 128), BF16),
        jax.ShapeDtypeStruct((3, 2, 1, chunk), F32),
        jax.ShapeDtypeStruct((3, 1, cont), F32),
    ]
    out_specs = [whole_spec((tok, 256))] * 4 + [
        pl.BlockSpec((1, nq, 128), lambda i, sc: (i, 0, 0)),
        pl.BlockSpec((1, nk, 128), lambda i, sc: (i, 0, 0)),
        pl.BlockSpec((1, 2, 1, chunk), lambda i, sc: (i, 0, 0, 0)),
        pl.BlockSpec((1, 1, cont), lambda i, sc: (i, 0, 0)),
    ]
    at = layer * 8
    count = len(own) + len(oth) + 2 + len(pos)
    return pl.pallas_call(
        strip(functools.partial(attn_fwd_kernel, dims), layer, count, len(deps)),
        grid_spec=pltpu.PrefetchScalarGridSpec(
            num_scalar_prefetch=1,
            grid=(3,),
            in_specs=[whole_spec(v.shape) for v in [*own, *oth]]
            + [
                pl.BlockSpec((1, D, 256), lambda i, sc: (0 if single else sc[at + 1], 0, i)),
                pl.BlockSpec((1, 1, 256), lambda i, sc: (sc[at], 0, i)),
            ]
            + attn_inputs(pos)
            + [ANY] * len(deps),
            out_specs=out_specs,
            scratch_shapes=[
                pltpu.VMEM((2 * chunk, 1), F32),
                pltpu.VMEM((2 * chunk, 1), F32),
                pltpu.VMEM((2 * chunk, 128), F32),
            ],
        ),
        out_shape=shapes,
        compiler_params=params(52),
        cost_estimate=cost(2 * nq * D * 768 * 2 + 8 * 3 * nq * nk * 64, 12e6, 3 * nq * nk),
        name="attn_fwd",
    )(sc, *own, *oth, w_all, b_all, *pos, *deps)


def attn_bwd_kernel(dims, sc, *refs):
    rows, piece, cpiece, chunk, cont = dims
    do_refs, o_refs = refs[:4], refs[4:8]
    q_ref, kv_ref, lse_ref, lsec_ref, w_ref = refs[8:13]
    prow, pcol, crow, ccol, srow, scol = refs[13:19]
    outs = refs[19:]
    npc = 4 * rows
    mine_out, theirs_out = outs[:2]
    dq_out, dkv_out, bias_out = outs[2:5]
    do_s, drow, drowc, dq_s, dkv_s = outs[5:]
    head = pl.program_id(0)
    base_b = chunk * rows
    base_c = 2 * chunk * rows
    tok = 2 * piece + cpiece
    upper = lax.broadcasted_iota(jnp.int32, (1, 128), 1) >= 64

    def take(ref):
        value = ref[...].astype(F32)
        left, right = value[:, 0:128], value[:, 128:256]
        pick = jnp.where(head == 2, pltpu.roll(right, 64, 1), left)
        pick = jnp.where(head == 0, pltpu.roll(left, 64, 1), pick)
        return jnp.where(upper, pick, 0.0)

    for s in range(4):
        dout = take(do_refs[s])
        low = dout.astype(BF16)
        do_s[s * piece : (s + 1) * piece, :] = low[0:piece]
        do_s[chunk + s * piece : chunk + (s + 1) * piece, :] = low[piece : 2 * piece]
        do_s[2 * chunk + s * cpiece : 2 * chunk + (s + 1) * cpiece, :] = low[2 * piece :]
        dot = dout * take(o_refs[s])
        dq_s[s * piece : (s + 1) * piece, :] = dot[0:piece]
        dq_s[chunk + s * piece : chunk + (s + 1) * piece, :] = dot[piece : 2 * piece]
        dq_s[2 * chunk + s * cpiece : 2 * chunk + (s + 1) * cpiece, :] = dot[2 * piece :]
    sub = min(128, chunk)
    for half in range(2):
        for i in range(chunk // sub):
            at = half * chunk + i * sub
            column = jnp.sum(dq_s[at : at + sub, :], axis=1, keepdims=True)
            drow[half, :, i * sub : (i + 1) * sub] = to_row(column)
    column = jnp.sum(dq_s[2 * chunk :, :], axis=1, keepdims=True)
    drowc[...] = to_row(column)
    dq_s[...] = jnp.zeros_like(dq_s)
    dkv_s[...] = jnp.zeros_like(dkv_s)

    def pair(q_at, k_at, lse, dot, mask):
        query = q_ref[0, q_at, :]
        keys = kv_ref[0, k_at, :]
        dout = do_s[q_at, :]
        prob = jnp.exp(nt(keys, query) - lse)
        if mask is not None:
            prob = jnp.where(mask, prob, 0.0)
        dprob = nt(keys, dout)
        dscore = (prob * (dprob - dot)).astype(BF16)
        dkv_s[k_at, :] += nn(prob.astype(BF16), dout) + nn(dscore, query)
        dq_s[q_at, :] += tn(dscore, keys)

    kb = min(512, chunk)
    at_a, at_b = pl.ds(0, chunk), pl.ds(chunk, chunk)
    lse_a, lse_b, dot_a, dot_b = lse_ref[0, 0], lse_ref[0, 1], drow[0], drow[1]
    for j in range(chunk // kb):
        mask = pcol[j * kb : (j + 1) * kb, :] <= prow[0:1, :]
        pair(at_a, pl.ds(j * kb, kb), lse_a, dot_a, mask)
        pair(at_b, pl.ds(base_b + j * kb, kb), lse_b, dot_b, mask)
    for j in range(base_b // kb):
        pair(at_b, pl.ds(j * kb, kb), lse_b, dot_b, None)
    my_row = sc[5]
    for t in range(1, rows):
        before = lax.rem(my_row + t, rows) < my_row
        which = jnp.where(before, 0, 1)
        q_at = pl.ds(pl.multiple_of(which * chunk, 128), chunk)
        k_base = jnp.where(before, t * chunk, base_b + t * chunk)
        for j in range(chunk // kb):
            k_at = pl.ds(pl.multiple_of(k_base + j * kb, 128), kb)
            pair(q_at, k_at, lse_ref[0, which], drow[which], None)
    at_c = pl.ds(2 * chunk, cont)
    for j in range(base_c // 512):
        pair(at_c, pl.ds(j * 512, 512), lsec_ref[0], drowc[...], None)
    mask = (ccol[...] <= crow[0:1, :]) & (scol[...] == srow[0:1, :])
    pair(at_c, pl.ds(base_c, cont), lsec_ref[0], drowc[...], mask)

    lower = jnp.logical_not(upper)
    dq_all = jnp.where(lower, dq_s[...] * 0.125, 0.0).astype(BF16)
    q_sum = colsum(dq_all.astype(F32))
    kv_sum = jnp.zeros((1, 128), F32)
    lanes_q = pl.ds(pl.multiple_of(head * 256, 128), 128)
    lanes_kv = pl.ds(pl.multiple_of(head * 256 + 128, 128), 128)
    lanes_oth = pl.ds(pl.multiple_of(head * 128, 128), 128)
    for s in range(4):
        spots = (
            (s * tok, piece, s * piece, s * piece),
            (s * tok + piece, piece, chunk + s * piece, base_b + s * piece),
            (s * tok + 2 * piece, cpiece, 2 * chunk + s * cpiece, base_c + s * cpiece),
        )
        for to, size, q_row, k_row in spots:
            dkv = dkv_s[k_row : k_row + size, :].astype(BF16)
            kv_sum = kv_sum + colsum(dkv.astype(F32))
            dq_out[to : to + size, lanes_q] = dq_all[q_row : q_row + size]
            dq_out[to : to + size, lanes_kv] = dkv
    for t in range(1, rows):
        for s in range(4):
            at = t * chunk + s * piece
            to = ((t - 1) * 4 + s) * 2 * piece
            for k_row in (at, base_b + at):
                dkv = dkv_s[k_row : k_row + piece, :].astype(BF16)
                kv_sum = kv_sum + colsum(dkv.astype(F32))
                dkv_out[to : to + piece, lanes_oth] = dkv
                to += piece

    def finish():
        weight = w_ref[0]
        for s in range(4):
            side = mine_out if s % 2 == 0 else theirs_out
            term = nt(dq_out[s * tok : (s + 1) * tok, :], weight)
            side[(s // 2) * tok : (s // 2 + 1) * tok, :] = term.astype(BF16)
        narrow = jnp.concatenate([weight[:, h * 256 + 128 : (h + 1) * 256] for h in range(3)], axis=1)
        for k in range(npc - 4):
            side = mine_out if k % 2 == 0 else theirs_out
            row = 2 * tok + (k // 2) * 2 * piece
            term = nt(dkv_out[k * 2 * piece : (k + 1) * 2 * piece, :], narrow)
            side[row : row + 2 * piece, :] = term.astype(BF16)

    pl.when(head == 2)(finish)
    bias_out[0] = jnp.broadcast_to(jnp.concatenate([q_sum, kv_sum], axis=1), (8, 256))


def attn_bwd(layer, sc, do_parts, o_parts, q, kv, lse, lsec, w_all, pos, dims, deps=()):
    rows, piece, cpiece, chunk, cont = dims
    tok = 2 * piece + cpiece
    nq, nk = 2 * chunk + cont, 2 * chunk * rows + cont
    noth = 4 * (rows - 1)
    shapes = (
        [jax.ShapeDtypeStruct((2 * tok + noth * piece, D), BF16)] * 2
        + [
            jax.ShapeDtypeStruct((4 * tok, D), BF16),
            jax.ShapeDtypeStruct((noth * 2 * piece, 384), BF16),
            jax.ShapeDtypeStruct((3, 8, 256), F32),
        ]
    )
    out_specs = [whole_spec(s.shape) for s in shapes[:4]] + [
        pl.BlockSpec((1, 8, 256), lambda i, sc: (i, 0, 0)),
    ]
    at = layer * 8
    return pl.pallas_call(
        strip(functools.partial(attn_bwd_kernel, dims), layer, 13 + len(pos), len(deps)),
        grid_spec=pltpu.PrefetchScalarGridSpec(
            num_scalar_prefetch=1,
            grid=(3,),
            in_specs=[whole_spec((tok, 256))] * 8
            + [
                pl.BlockSpec((1, nq, 128), lambda i, sc: (i, 0, 0)),
                pl.BlockSpec((1, nk, 128), lambda i, sc: (i, 0, 0)),
                pl.BlockSpec((1, 2, 1, chunk), lambda i, sc: (i, 0, 0, 0)),
                pl.BlockSpec((1, 1, cont), lambda i, sc: (i, 0, 0)),
                pl.BlockSpec((1, D, D), lambda i, sc: (sc[at + 1], 0, 0)),
            ]
            + attn_inputs(pos)
            + [ANY] * len(deps),
            out_specs=out_specs,
            scratch_shapes=[
                pltpu.VMEM((nq, 128), BF16),
                pltpu.VMEM((2, 1, chunk), F32),
                pltpu.VMEM((1, cont), F32),
                pltpu.VMEM((nq, 128), F32),
                pltpu.VMEM((nk, 128), F32),
            ],
        ),
        out_shape=shapes,
        compiler_params=params(56),
        cost_estimate=cost(2 * nq * D * 768 * 2 + 20 * 3 * nq * nk * 64, 14e6, 3 * nq * nk),
        name="attn_bwd",
    )(sc, *do_parts, *o_parts, q, kv, lse, lsec, w_all, *pos, *deps)


def dw_qkv_kernel(rows, sc, *refs):
    npc = 4 * rows
    srcs, (dq_hbm, dkv_hbm) = refs[:npc], refs[npc : npc + 2]
    new_ref, token = refs[npc + 2 : npc + 4]
    own, oth, dq_s, dkv_s, asem, dsem = refs[npc + 4 :]
    token[...] = jnp.zeros_like(token)
    tok, two = srcs[0].shape[0], srcs[4].shape[0]

    def rows_of(k):
        dst = own.at[pl.ds(k * tok, tok)] if k < 4 else oth.at[pl.ds((k - 4) * two, two)]
        return pltpu.make_async_copy(srcs[k], dst, asem.at[k])

    loads = [rows_of(k) for k in range(npc)]
    grads = [
        pltpu.make_async_copy(dq_hbm, dq_s, dsem.at[0]),
        pltpu.make_async_copy(dkv_hbm, dkv_s, dsem.at[1]),
    ]
    for copy in [grads[0], *loads[:4], grads[1], *loads[4:]]:
        copy.start()
    for copy in [grads[0], *loads[:4]]:
        copy.wait()
    total = tn(own[...], dq_s[...])
    for copy in [grads[1], *loads[4:]]:
        copy.wait()
    right = tn(oth[...], dkv_s[...])
    for h in range(HEADS_COL):
        lo = h * 256
        new_ref[:, lo : lo + 128] = total[:, lo : lo + 128].astype(BF16)
        both = total[:, lo + 128 : lo + 256] + right[:, h * 128 : (h + 1) * 128]
        new_ref[:, lo + 128 : lo + 256] = both.astype(BF16)


def dw_qkv(layer, sc, own, oth, dq, dkv, deps=()):
    rows = (4 + len(oth)) // 4
    tok, two = own[0].shape[0], oth[0].shape[0]
    noth = len(oth)
    ins = [*own, *oth, dq, dkv]
    return pl.pallas_call(
        strip(functools.partial(dw_qkv_kernel, rows), layer, len(ins), len(deps)),
        grid_spec=pltpu.PrefetchScalarGridSpec(
            num_scalar_prefetch=1,
            grid=(1,),
            in_specs=[ANY] * len(ins) + [ANY] * len(deps),
            out_specs=[whole_spec((D, D)), whole_spec((8, 128))],
            scratch_shapes=[
                pltpu.VMEM((4 * tok, D), BF16),
                pltpu.VMEM((noth * two, D), BF16),
                pltpu.VMEM(dq.shape, BF16),
                pltpu.VMEM(dkv.shape, BF16),
                pltpu.SemaphoreType.DMA((4 * rows,)),
                pltpu.SemaphoreType.DMA((2,)),
            ],
        ),
        out_shape=[
            jax.ShapeDtypeStruct((D, D), BF16),
            jax.ShapeDtypeStruct((8, 128), F32),
        ],
        compiler_params=params(56),
        cost_estimate=cost(2 * 3 * D * (4 * tok * 256 + noth * two * 128), 10e6),
        name="dw_qkv",
    )(sc, *ins, *deps)


class Loads:

    def __init__(self, refs, tok, side, outp, sems):
        tok_m, tok_r, mine, got, o0, o2, r1, r3 = refs
        size = tok_m.shape[1]
        low, high = pl.ds(0, size), pl.ds(size, size)
        pairs = {}
        for k in range(3):
            pairs["tok", k] = [(tok_m.at[k], tok.at[k, low]), (tok_r.at[k], tok.at[k, high])]
        for k in range(4):
            pairs["side", k] = [(mine.at[k], side.at[k, low]), (got.at[k], side.at[k, high])]
        pairs["outp", 0] = [(o0, outp.at[0, low]), (r1, outp.at[0, high])]
        pairs["outp", 1] = [(o2, outp.at[1, low]), (r3, outp.at[1, high])]
        self.copies, n = {}, 0
        for key, both in pairs.items():
            self.copies[key] = []
            for a, b in both:
                self.copies[key].append(pltpu.make_async_copy(a, b, sems.at[n]))
                n += 1

    def start(self):
        first = [("tok", 0), ("side", 0), ("tok", 1), ("side", 2), ("tok", 2), ("outp", 0)]
        for key in [*first, ("side", 1), ("side", 3), ("outp", 1)]:
            for copy in self.copies[key]:
                copy.start()

    def wait(self, *key):
        for copy in self.copies[key]:
            copy.wait()

    def wait_tile(self, tile, name, index):
        tokens = {"up": 0, "down": 1, "out": 2}[index]

        def first():
            self.wait("tok", tokens)
            self.wait(name, 2 if index == "down" else 0)

        pl.when(tile == 0)(first)
        pl.when(tile == 1)(lambda: self.wait(name, 3 if index == "down" else 1))


def dw_products(tile, loads, tok, side, outp, put, splits=((0, 256), (256, 512), (512, 768))):
    loads.wait_tile(tile, "side", "up")
    for j in range(3):
        put(j * 256, tn(tok[0], side[tile, :, j * 256 : (j + 1) * 256]))
    loads.wait_tile(tile, "side", "down")
    for lo, hi in splits:
        put(768 + lo, tn(tok[1], side[2 + tile, :, lo:hi]))
    loads.wait_tile(tile, "outp", "out")
    put(1536, tn(tok[2], outp[tile]))


def dw_mlp_kernel(sc, *refs):
    old_ref, new_ref, token = refs[8:11]
    tok, side, outp, sems = refs[11:]
    token[...] = jnp.zeros_like(token)
    tile = pl.program_id(0)
    keep = sc[6] == 0

    loads = Loads(refs[:8], tok, side, outp, sems)
    pl.when(tile == 0)(loads.start)

    def put(lo, value):
        size = value.shape[1]
        old = old_ref[0, 0, :, lo : lo + size].astype(F32)
        new_ref[0, 0, :, lo : lo + size] = (value + jnp.where(keep, old, 0.0)).astype(BF16)

    dw_products(tile, loads, tok, side, outp, put)


def dw_scratch(tok):
    return [
        pltpu.VMEM((3, 2 * tok, D), BF16),
        pltpu.VMEM((4, 2 * tok, D), BF16),
        pltpu.VMEM((2, 2 * tok, 256), BF16),
        pltpu.SemaphoreType.DMA((18,)),
    ]


def dw_mlp(layer, sc, ins, acc, deps=()):
    tok = ins[0].shape[1]
    at = layer * 8
    acc_spec = pl.BlockSpec((1, 1, D, PACK), lambda i, sc: (sc[at + 1], i, 0, 0))
    return pl.pallas_call(
        strip(dw_mlp_kernel, layer, 9, len(deps)),
        grid_spec=pltpu.PrefetchScalarGridSpec(
            num_scalar_prefetch=1,
            grid=(2,),
            in_specs=[ANY] * 8 + [acc_spec] + [ANY] * len(deps),
            out_specs=[acc_spec, whole_spec((8, 128))],
            scratch_shapes=dw_scratch(tok),
        ),
        out_shape=[jax.ShapeDtypeStruct(acc.shape, acc.dtype), jax.ShapeDtypeStruct((8, 128), F32)],
        input_output_aliases={9: 0},
        compiler_params=params(56),
        cost_estimate=cost(2 * tok * D * 4 * PACK, 20e6),
        name="dw_mlp",
    )(sc, *ins, acc, *deps)


def dw_last_kernel(rank, groups, slot, sc, *refs):
    keep_a, give_a, keep_b, give_b, acc, token = refs[9:15]
    tok, side, outp, sems, done, other, dsem, osem, out_a, out_b, asem, bsem = refs[15:]
    token[...] = jnp.zeros_like(token)
    tile = pl.program_id(0)
    same = sc[1] == rank
    keep = sc[6] == 0
    used = jnp.logical_or(jnp.logical_not(same), keep)

    def load(t):
        return pltpu.make_async_copy(acc.at[rank, t], done.at[t], dsem.at[t])

    loads = Loads(refs[:8], tok, side, outp, sems)

    def begin():
        loads.start()
        load(0).start()
        load(1).start()

    pl.when(tile == 0)(begin)
    load(tile).wait()

    def fetch_other():
        copy = pltpu.make_async_copy(acc.at[sc[1], tile], other, osem)
        copy.start()
        copy.wait()

    pl.when(jnp.logical_not(same))(fetch_other)

    def put(lo, value):
        size = value.shape[1]
        cols = slice(lo, lo + size)
        old = jnp.where(used, done[tile, :, cols].astype(F32), 0.0)
        total = (old + jnp.where(same, value, 0.0)).astype(BF16)
        if lo < HALF:
            out_a[tile, :, cols] = total
        else:
            out_b[tile, :, lo - HALF : lo - HALF + size] = total

        def add_other():
            before = jnp.where(keep, other[:, cols].astype(F32), 0.0)
            other[:, cols] = (value + before).astype(BF16)

        pl.when(jnp.logical_not(same))(add_other)

    splits = ((0, HALF - D), (HALF - D, 384), (384, 640), (640, 768))
    dw_products(tile, loads, tok, side, outp, put, splits)

    def store_other():
        copy = pltpu.make_async_copy(other, acc.at[sc[1], tile], osem)
        copy.start()
        copy.wait()

    pl.when(jnp.logical_not(same))(store_other)
    size = D // (2 * groups)
    bit = sc[slot]

    def copies(t):
        both = [pltpu.make_async_copy(out_a.at[t], (keep_a, give_a)[t], asem.at[t])]
        for g in range(groups):
            for k, (ref, part) in enumerate(((keep_b, bit), (give_b, 1 - bit))):
                src = pl.ds(pl.multiple_of((2 * g + part) * size, size), size)
                dst = pl.ds((t * groups + g) * size, size)
                both.append(pltpu.make_async_copy(out_b.at[t, src], ref.at[dst], bsem.at[t, 2 * g + k]))
        return both

    def leave(t):
        for copy in copies(t):
            copy.start()

    pl.when(tile == 0)(functools.partial(leave, 0))

    def finish():
        leave(1)
        for t in range(2):
            for copy in copies(t):
                copy.wait()

    pl.when(tile == 1)(finish)


def dw_last(layer, sc, ins, acc, groups, deps=()):
    tok = ins[0].shape[1]
    slot = LAYERS * 8 + 1 + len(bits_of("dp")) - layer * 8
    halves = [jax.ShapeDtypeStruct((D, n), BF16) for n in (HALF, HALF, PACK - HALF, PACK - HALF)]
    return pl.pallas_call(
        strip(functools.partial(dw_last_kernel, layer, groups, slot), layer, 9, len(deps)),
        grid_spec=pltpu.PrefetchScalarGridSpec(
            num_scalar_prefetch=1,
            grid=(2,),
            in_specs=[ANY] * 9 + [ANY] * len(deps),
            out_specs=[ANY] * 4 + [ANY, whole_spec((8, 128))],
            scratch_shapes=dw_scratch(tok)
            + [
                pltpu.VMEM((2, D, PACK), BF16),
                pltpu.VMEM((D, PACK), BF16),
                pltpu.SemaphoreType.DMA((2,)),
                pltpu.SemaphoreType.DMA(()),
                pltpu.VMEM((2, D, HALF), BF16),
                pltpu.VMEM((2, D, PACK - HALF), BF16),
                pltpu.SemaphoreType.DMA((2,)),
                pltpu.SemaphoreType.DMA((2, 2 * groups)),
            ],
        ),
        out_shape=halves
        + [
            jax.ShapeDtypeStruct(acc.shape, acc.dtype),
            jax.ShapeDtypeStruct((8, 128), F32),
        ],
        input_output_aliases={9: 4},
        compiler_params=params(56),
        cost_estimate=cost(2 * tok * D * 4 * PACK, 20e6),
        name="dw_last",
    )(sc, *ins, acc, *deps)


def qkv_total(sc, rank, parts, groups, deps):
    size = D // (2 * groups)
    slot = LAYERS * 8 + 1 + len(bits_of("dp"))

    def add(sc, *refs):
        keep, give = refs[-2:]
        bit = sc[slot]
        for g in range(groups):
            for out, side in ((keep, bit), (give, 1 - bit)):
                at = pl.ds(pl.multiple_of((2 * g + side) * size, size), size)
                total = jnp.zeros((size, D), F32)
                for k, ref in enumerate(refs[:-2]):
                    used = sc[(rank + k) * 8 + 1] == rank
                    total = total + jnp.where(used, ref[at, :].astype(F32), 0.0)
                out[g * size : (g + 1) * size, :] = total.astype(BF16)

    shape = jax.ShapeDtypeStruct((D // 2, D), BF16)
    return simple_call(add, sc, parts, [shape] * 2, name="qkv_total", deps=deps)


def blank(shape, dtype):
    def body(out):
        del out

    return pl.pallas_call(
        body,
        out_shape=jax.ShapeDtypeStruct(shape, dtype),
        out_specs=pl.BlockSpec(memory_space=pl.ANY),
        name="blank",
    )()


SWAP = [(0, 1), (1, 0)]


def swap_core(value):
    return lax.ppermute(value, "core", SWAP)


def swap_x(value):
    return lax.ppermute(value, "x", SWAP)


def shift_row(value, t):
    rows = lax.axis_size("row")
    return lax.ppermute(value, "row", [(i, (i - t) % rows) for i in range(rows)])


def shift_row_x(value, t):
    rows = lax.axis_size("row")
    pairs = [(i * 2 + j, ((i - t) % rows) * 2 + (1 - j)) for i in range(rows) for j in range(2)]
    return lax.ppermute(value, ("row", "x"), pairs)


def spread(low, low_prompt):
    rows = lax.axis_size("row")
    from_x = swap_x(low)
    far = []
    for t in range(1, rows):
        far += [shift_row(low_prompt, t), shift_row_x(low_prompt, t)]
    own = [low, swap_core(low), from_x, swap_core(from_x)]
    oth = []
    for t in range(1, rows):
        near, diag = far[2 * t - 2], far[2 * t - 1]
        oth += [near, swap_core(near), diag, swap_core(diag)]
    return own, oth


def exchange_heads(parts):
    flip = {1: [1, 0, 3, 2], 2: [2, 3, 0, 1], 3: [3, 2, 1, 0]}
    out = [parts[0]]
    for s in (1, 2, 3):
        pairs = [(c, flip[s][c]) for c in range(4)]
        out.append(lax.ppermute(parts[s], ("x", "core"), pairs))
    return out


def add_low(a, b):
    return (a.astype(F32) + b.astype(F32)).astype(BF16)


def sum_kernel(sizes, a, b, *outs):
    at = 0
    for size, out in zip(sizes, outs):
        out[...] = add_low(a[at : at + size, :], b[at : at + size, :])
        at += size


def collect(mine, theirs, tok, prompt, deps=()):
    rows = lax.axis_size("row")
    sizes = [tok, tok] + [prompt] * (2 * (rows - 1))
    vmem = pl.BlockSpec(memory_space=pltpu.VMEM)
    count = len(deps)
    sums = pl.pallas_call(
        lambda a, b, *refs: sum_kernel(sizes, a, b, *refs[count:]),
        in_specs=[vmem] * 2 + [ANY] * count,
        out_specs=[vmem] * len(sizes),
        out_shape=[jax.ShapeDtypeStruct((n, D), BF16) for n in sizes],
        compiler_params=params(24),
        cost_estimate=cost(1e6, 4e6),
        name="sum_cores",
    )(mine, swap_core(theirs), *deps)
    got = swap_x(sums[1])
    rest = []
    for t in range(1, rows):
        rest += [shift_row(sums[2 * t], -t), shift_row_x(sums[2 * t + 1], -t)]
    return sums[0], got, rest


def behind(values, deps):
    if not deps:
        return list(values)
    count = len(values)

    def body(*refs):
        del refs

    return pl.pallas_call(
        body,
        in_specs=[ANY] * (count + len(deps)),
        out_specs=[ANY] * count,
        out_shape=[jax.ShapeDtypeStruct(v.shape, v.dtype) for v in values],
        input_output_aliases={k: k for k in range(count)},
        name="behind",
    )(*values, *deps)


def held(value, deps):
    def body(src, *rest):
        rest[-1][...] = src[...]

    vmem = pl.BlockSpec(memory_space=pltpu.VMEM)
    return pl.pallas_call(
        body,
        in_specs=[vmem] + [ANY] * len(deps),
        out_specs=vmem,
        out_shape=jax.ShapeDtypeStruct(value.shape, value.dtype),
        name="held",
    )(value, *deps)


def gather_begin(value, names):
    total = 1
    for a in names:
        total *= lax.axis_size(a)
    return [lax.ppermute(value, names, [(i, i ^ t) for i in range(total)]) for t in range(1, total)]


def gather_end(sc, pieces, index, ahead=(), deps=()):
    lead, n, width = pieces[0].shape
    count = len(pieces)

    def place(sc, *refs):
        out = refs[-1]
        for block in refs[count:-1]:
            out[0:1] = block[...]
        base = len(ahead)
        for t in range(count):
            at = pl.ds(pl.multiple_of((sc[index] ^ t) * n, n), n)
            out[base : base + lead, at, :] = refs[t][...]

    shape = jax.ShapeDtypeStruct((lead + len(ahead), count * n, width), BF16)
    return simple_call(place, sc, [*pieces, *ahead], [shape], name="place", deps=deps)[0]


def zig(j, rows):
    return j if j < rows else 2 * rows - 1 - j


def split_kernel(piece, cpiece, sc, even, odd, cont, *outs):
    for s, out in enumerate(outs):
        place = sc[3] ^ s
        at = pl.ds(pl.multiple_of(place * piece, piece), piece)

        def fill(first, second, out=out, at=at):
            out[0:piece, :] = first[at, :]
            out[piece : 2 * piece, :] = second[at, :]

        pl.when(sc[7] == 0)(functools.partial(fill, even, odd))
        pl.when(sc[7] == 1)(functools.partial(fill, odd, even))
        out[2 * piece :, :] = cont[pl.ds(pl.multiple_of(place * cpiece, cpiece), cpiece), :]


def merge_kernel(piece, cpiece, sc, p0, p1, p2, p3, even, odd, cont):
    for s, part in enumerate((p0, p1, p2, p3)):
        place = sc[3] ^ s
        at = pl.ds(pl.multiple_of(place * piece, piece), piece)

        def fill(first, second, part=part, at=at):
            first[at, :] = part[0:piece, :]
            second[at, :] = part[piece : 2 * piece, :]

        pl.when(sc[7] == 0)(functools.partial(fill, even, odd))
        pl.when(sc[7] == 1)(functools.partial(fill, odd, even))
        cont[pl.ds(pl.multiple_of(place * cpiece, cpiece), cpiece), :] = part[2 * piece :, :]


def join_kernel(prompt, normed, sc, p0, p1, p2, p3, vec_ref, h_ref, *outs):
    width = p0.shape[1]
    for s, part in enumerate((p0, p1, p2, p3)):
        value = part[...].astype(F32)
        for c in range(4):

            def put(value=value, c=c):
                h_ref[:, c * width : (c + 1) * width] = value

            pl.when((sc[3] ^ s) == c)(put)
    if normed:
        a_ref, ap_ref = outs
        centered, _ = stats(h_ref[...])
        low = (centered * vec_ref[0, 4:5, :] + vec_ref[0, 5:6, :]).astype(BF16)
        a_ref[...] = low
        ap_ref[...] = low[:prompt]


def simple_call(kernel, sc, ins, shapes, specs=None, name="small", deps=()):
    return pl.pallas_call(
        strip(kernel, 0, len(ins), len(deps)),
        grid_spec=pltpu.PrefetchScalarGridSpec(
            num_scalar_prefetch=1,
            grid=(1,),
            in_specs=(specs or [whole_spec(v.shape) for v in ins]) + [ANY] * len(deps),
            out_specs=[whole_spec(v.shape) for v in shapes],
        ),
        out_shape=shapes,
        compiler_params=params(24),
        cost_estimate=cost(1e6, 3e6),
        name=name,
    )(sc, *ins, *deps)


def enter(prompt, cont, sc, vecs, normed):
    parts = enter_begin(prompt, cont, sc)
    return parts, enter_end(exchange_heads(parts), sc, vecs, normed, prompt.shape[0] // 4)


def enter_begin(prompt, cont, sc, deps=()):
    rows = lax.axis_size("row")
    half, width = prompt.shape[0] // 2, prompt.shape[1]
    piece, cpiece = half // 4, cont.shape[0] // 4
    tok = 2 * piece + cpiece
    even = prompt[:half]
    odd = prompt[half:]
    if rows > 2:
        even = lax.ppermute(even, "row", [(i, zig(2 * i, rows)) for i in range(rows)])
    odd = lax.ppermute(odd, "row", [(i, zig(2 * i + 1, rows)) for i in range(rows)])
    part = jax.ShapeDtypeStruct((tok, width), BF16)
    parts = simple_call(
        functools.partial(split_kernel, piece, cpiece), sc, [even, odd, cont], [part] * 4, name="split", deps=deps
    )
    return parts


def enter_end(parts, sc, vecs, normed, prompt, deps=()):
    tok, width = parts[0].shape
    shapes = [jax.ShapeDtypeStruct((tok, D), F32)]
    if normed:
        shapes += [jax.ShapeDtypeStruct((tok, D), BF16), jax.ShapeDtypeStruct((prompt, D), BF16)]
    specs = [whole_spec((tok, width))] * 4 + [pl.BlockSpec((1, 8, D), lambda i, sc: (sc[0], 0, 0))]
    return simple_call(
        functools.partial(join_kernel, prompt, normed), sc, [*parts, vecs], shapes, specs, "join", deps
    )


def leave(parts, sc, prompt_rows):
    return leave_end(sc, *leave_begin(exchange_heads(parts), sc, prompt_rows))


def leave_begin(parts, sc, prompt_rows, deps=()):
    width = parts[0].shape[1]
    half = prompt_rows // 2
    piece = half // 4
    cpiece = parts[0].shape[0] - 2 * piece
    shapes = [jax.ShapeDtypeStruct((n, width), BF16) for n in (half, half, 4 * cpiece)]
    even, odd, cont = simple_call(
        functools.partial(merge_kernel, piece, cpiece), sc, parts, shapes, name="merge", deps=deps
    )
    return even, odd, cont


def leave_end(sc, even, odd, cont, deps=()):
    rows = lax.axis_size("row")
    if rows > 2:
        even = lax.ppermute(even, "row", [(zig(2 * i, rows), i) for i in range(rows)])
    odd = lax.ppermute(odd, "row", [(zig(2 * i + 1, rows), i) for i in range(rows)])
    half, width = even.shape

    def stack(sc, first, second, out):
        out[0, 0:half, :] = first[...]
        out[0, half:, :] = second[...]

    shape = jax.ShapeDtypeStruct((1, 2 * half, width), BF16)
    return simple_call(stack, sc, [even, odd], [shape], name="rows", deps=deps)[0], cont[None]


def final_kernel(prompt, others, sc, *refs):
    g_ref, h_ref, p0_ref, rx_ref = refs[:4]
    rest = refs[4 : 4 + others]
    vec_ref = refs[4 + others]
    outs, small, da_ref, out_ref = refs[5 + others : 9 + others], refs[9 + others], refs[10 + others], refs[11 + others]
    da_ref[...] = p0_ref[...].astype(F32) + rx_ref[...].astype(F32)
    for ref in rest:
        da_ref[0:prompt, :] += ref[...].astype(F32)
    da1 = da_ref[...]
    centered, inverse = stats(h_ref[...])
    small[0:1, :] = colsum(da1 * centered)
    small[1:2, :] = colsum(da1)
    out_ref[...] = g_ref[...] + norm_back(da1, vec_ref[0, 4:5, :], centered, inverse)
    send_features(sc, out_ref, outs)


def final_norm(sc, grad, back, vecs, prompt, width, deps):
    tok = grad.shape[0]
    h_in, base, got, rest = back
    ins = [grad, h_in, base, got, *rest, vecs]
    shapes = [jax.ShapeDtypeStruct((tok, width), BF16)] * 4 + [
        jax.ShapeDtypeStruct((8, D), F32),
        jax.ShapeDtypeStruct((tok, D), F32),
        jax.ShapeDtypeStruct((tok, D), F32),
    ]
    specs = [whole_spec(v.shape) for v in ins[:-1]] + [
        pl.BlockSpec((1, 8, D), lambda i, sc: (sc[0], 0, 0))
    ]
    return simple_call(
        functools.partial(final_kernel, prompt, len(rest)), sc, ins, shapes, specs, "final_norm", deps
    )


class Reduce:

    def __init__(self, sc, keep, give, name, names, plan):
        self.sc, self.keep, self.give = sc, keep, give
        self.names, self.plan = list(names), list(plan)
        self.ready, self.waiting = 0, None
        self.send(name)

    def send(self, name):
        axis, bit = name
        count = lax.axis_size(axis)
        self.got = lax.ppermute(self.give, axis, [(i, i ^ bit) for i in range(count)])

    def step(self, deps=(), hold=False):
        rows, width = self.keep.shape
        if not self.plan:
            return []
        name = self.plan.pop(0)
        where = self.names.index(name)
        self.names.pop(where)
        before, size = 2**where, rows // 2 ** (where + 1)
        if name[0] == "x":
            slot = None
        else:
            slot = LAYERS * 8 + 1 + (bits_of("dp") + bits_of("row")).index(name)

        def add(sc, keep, got, new_keep, new_give):
            bit = 0 if slot is None else sc[slot]
            for a in range(before):
                for out, side in ((new_keep, bit), (new_give, 1 - bit)):
                    lo = (2 * a + side) * size
                    at = pl.ds(lo if slot is None else pl.multiple_of(lo, size), size)
                    out[a * size : (a + 1) * size, :] = add_low(keep[at, :], got[at, :])

        if size % 16:
            total = add_low(self.keep, self.got).reshape(before, 2, size, width)
            bit = 0 if slot is None else self.sc[slot]
            self.keep, self.give = (
                lax.dynamic_index_in_dim(total, side, 1, keepdims=False).reshape(rows // 2, width)
                for side in (bit, 1 - bit)
            )
        else:
            shape = jax.ShapeDtypeStruct((rows // 2, width), BF16)
            self.keep, self.give = simple_call(
                add, self.sc, [self.keep, self.got], [shape] * 2, name="add", deps=deps
            )
        if hold and name[0] != "dp":
            self.waiting = name
        else:
            self.send(name)
        return [self.give]

    def release(self, deps):
        if self.waiting is not None:
            self.give = behind([self.give], deps)[0]
            self.send(self.waiting)
            self.waiting = None

    def finish(self):
        while self.plan:
            self.step()
        return [self.keep, self.got]


def bits_of(axis):
    bits, bit = [], lax.axis_size(axis) // 2
    while bit:
        bits.append((axis, bit))
        bit //= 2
    return bits


def reorder(value):
    shape = value.shape
    value = value.reshape((2, 2) + shape[1:])
    value = jnp.where(lax.axis_index("core") == 1, value[:, ::-1], value)
    value = jnp.where(lax.axis_index("x") == 1, value[::-1], value)
    return value.reshape(shape)


def narrow_kernel(width, sc, *refs):
    smalls, qkvs, last_ref, out = refs[:LAYERS], refs[LAYERS : 2 * LAYERS], refs[2 * LAYERS], refs[-1]
    out[...] = jnp.zeros_like(out)
    for b in range(NB):
        total = jnp.zeros((16, D), F32)
        qkv = jnp.zeros((HEADS_COL, 256), F32)
        for i in range(LAYERS):
            mine = sc[i * 8] == b
            total = total + jnp.where(mine, smalls[i][...], 0.0)
            qkv = qkv + jnp.where(mine, qkvs[i][:, 0, :], 0.0)
        gain = jnp.where(sc[0] == b, last_ref[0:2, :], 0.0)
        for i in range(1, LAYERS):
            gain = gain + jnp.where(sc[i * 8] == b, smalls[i - 1][8:10, :], 0.0)
        rows = jnp.concatenate([total[5:6], total[4:5], total[6:8], gain], axis=0)
        for s in range(4):
            out[s, b, 0:1, :] = total[s : s + 1]
            for c in range(4):

                def put(s=s, b=b, c=c, rows=rows):
                    out[s, b, 1:7, 0:width] = rows[:, c * width : (c + 1) * width]

                pl.when((sc[3] ^ s) == c)(put)
        for h in range(HEADS_COL):
            out[0, b, 7:8, h * 256 : (h + 1) * 256] = qkv[h : h + 1]


def end_slot():
    return LAYERS * 8 + 1 + len(bits_of("dp")) + len(bits_of("row"))


def pack_end(sc, parts, width):
    slot = end_slot()
    share = parts[0].shape[0]

    def end(sc, *refs):
        up, down, out = refs[-3:]
        for k in range(NB):
            ka, ga, kb, gb = refs[4 * k : 4 * k + 4]
            left = ka[...].astype(F32) + ga[...].astype(F32)
            right = kb[...].astype(F32) + gb[...].astype(F32)
            for b in range(NB):

                def put(b=b, left=left, right=right):
                    up[b] = left[:, 0:D]
                    down[b, :, 0 : HALF - D] = left[:, D:]
                    down[b, :, HALF - D :] = right[:, 0 : 2 * D - HALF]
                    out[b] = right[:, 2 * D - HALF : 2 * D - HALF + width]

                pl.when(sc[slot + b] == k)(put)

    shapes = [jax.ShapeDtypeStruct((NB, share, n), F32) for n in (D, D, width)]
    return simple_call(end, sc, parts, shapes, name="pack_end")


def qkv_end(sc, parts, width):
    slot = end_slot()
    share = parts[0].shape[0]

    def end(sc, *refs):
        out = refs[-1]
        for k in range(NB):
            total = refs[2 * k][...].astype(F32) + refs[2 * k + 1][...].astype(F32)
            for b in range(NB):

                def put(b=b, total=total):
                    for h in range(HEADS_COL):
                        for j, lane in enumerate((0, 128, 192)):
                            at = h * 256 + lane
                            out[b, j, :, h * HD : (h + 1) * HD] = total[:, at : at + HD]

                pl.when(sc[slot + b] == k)(put)

    shape = jax.ShapeDtypeStruct((NB, 3, share, width), F32)
    return simple_call(end, sc, parts, [shape], name="qkv_end")[0].transpose(0, 2, 1, 3)


def narrow_end(sc, value, got, width):
    def end(sc, value, got, bup, qv, *vecs):
        for b in range(NB):
            total = value[b] + got[b]
            bup[b : b + 1, :] = total[0:1]
            for k, out in enumerate(vecs):
                out[b : b + 1, :] = total[1 + k : 2 + k, 0:width]
            for h in range(HEADS_COL):
                for j, lane in enumerate((0, 192)):
                    at = h * 256 + lane
                    qv[b, j : j + 1, h * HD : (h + 1) * HD] = total[7:8, at : at + HD]

    shapes = [jax.ShapeDtypeStruct((NB, D), F32), jax.ShapeDtypeStruct((NB, 2, width), F32)]
    shapes += [jax.ShapeDtypeStruct((NB, width), F32)] * 6
    return simple_call(end, sc, [value, got], shapes, name="narrow_end")


def sum_small(value):
    got = swap_core(jnp.stack([value[1], value[3]]))
    near, far = value[0] + got[0], value[2] + got[1]
    value = near + swap_x(far)
    steps = bits_of("row") + bits_of("dp")
    for k, (axis, bit) in enumerate(steps):
        got = lax.ppermute(value, axis, [(i, i ^ bit) for i in range(lax.axis_size(axis))])
        if k + 1 < len(steps):
            value = value + got
    return value, got


def per_device(
    x_prompt,
    x_cont,
    seg_ids,
    layer_map,
    w_qkv,
    bias_qv,
    w_out,
    b_out,
    w_up,
    b_up,
    w_down,
    b_down,
    ln1_gain,
    ln1_bias,
    ln2_gain,
    ln2_bias,
    cot_prompt,
    cot_cont,
):
    rows, dps = lax.axis_size("row"), lax.axis_size("dp")
    prompt_row, cont = x_prompt.shape[1], x_cont.shape[1]
    width = x_prompt.shape[2]
    chunk = prompt_row // 2
    piece, cpiece = chunk // 4, cont // 4
    prompt = 2 * piece
    dims = (rows, piece, cpiece, chunk, cont)
    my_row, my_x = lax.axis_index("row"), lax.axis_index("x")
    my_col = my_x * 2 + lax.axis_index("core")

    layer_map = layer_map.astype(jnp.int32)
    places = jnp.arange(LAYERS, dtype=jnp.int32)
    blocks = jnp.arange(NB, dtype=jnp.int32)
    first_use = jnp.min(jnp.where(layer_map[None] == blocks[:, None], places[None], 99), axis=1)
    rank_of = jnp.sum((first_use[None] < first_use[:, None]).astype(jnp.int32), axis=1)
    rank_layer = jnp.sum(jnp.where(layer_map[:, None] == blocks[None], rank_of[None], 0), axis=1)
    later = (rank_layer[None] == rank_layer[:, None]) & (places[None] > places[:, None])
    fresh = 1 - jnp.max(later.astype(jnp.int32), axis=1)
    after = jnp.concatenate([layer_map[1:], layer_map[-1:]])

    def fill(value):
        return jnp.broadcast_to(value, (LAYERS,)).astype(jnp.int32)

    sc = jnp.stack(
        [layer_map, rank_layer, after, fill(my_col), fill(my_x), fill(my_row), fresh, fill(my_row % 2)],
        axis=1,
    ).reshape(-1)
    my_dp = lax.axis_index("dp")
    extra = [my_dp * rows + my_row]
    ends = [rank_of[b] for b in range(NB)]
    extra += [(lax.axis_index(a) // b) % 2 for a, b in bits_of("dp") + bits_of("row")]
    sc = jnp.concatenate([sc, jnp.stack(extra + ends).astype(jnp.int32)])

    heads = w_qkv.reshape(NB, -1, 3, HEADS_COL, HD)
    zero = jnp.zeros_like(heads[:, :, 0])
    packed = jnp.stack([heads[:, :, 0], zero, heads[:, :, 1], heads[:, :, 2]], axis=3)
    packed = packed.reshape(NB, -1, D)

    def by_block(stacked):
        nothing = jnp.zeros((), stacked.dtype)
        return [
            sum(jnp.where(rank_of[b] == k, stacked[b], nothing) for b in range(NB)) for k in range(NB)
        ]

    packed = by_block(packed)
    pair = bias_qv.astype(F32).reshape(NB, 2, HEADS_COL, HD)
    none = jnp.zeros((NB, HEADS_COL, 2, HD), F32)
    bqkv = jnp.concatenate([pair[:, 0][:, :, None], none, pair[:, 1][:, :, None]], axis=2).reshape(NB, 1, D)

    def flat(value):
        return value.reshape(NB, -1)

    narrow = jnp.concatenate(
        [flat(v) for v in (b_out, b_down, ln2_gain, ln2_bias, ln1_gain, ln1_bias, b_up)], axis=1
    )
    narrow = jnp.stack(exchange_heads([narrow] * 4))
    narrow = reorder(narrow.astype(F32))
    vecs = narrow[:, :, : 6 * width].reshape(4, NB, 6, width).transpose(1, 2, 0, 3).reshape(NB, 6, D)
    vecs = jnp.concatenate([vecs, jnp.zeros((NB, 2, D), F32)], axis=1)
    bup = narrow[:, :, 6 * width :].transpose(1, 0, 2).reshape(NB, 4, 1, D)

    pack_local = jnp.concatenate(
        [w_up, w_down, w_out, jnp.zeros(w_out.shape[:2] + (64,), BF16)], axis=2
    )
    share = D // (dps * rows)
    packs = []
    for local in by_block(pack_local):
        pack = lax.all_gather(local, ("x", "core", "dp", "row"), axis=0)
        if share % 16:
            packs.append(pack.reshape(4, 1, D, PACK))
        else:
            packs.append(pack.reshape(4, dps * rows, share, PACK))

    def places_of(size):
        index = jnp.arange(4 * size, dtype=jnp.int32)
        return size * ((index // size) ^ my_col) + index % size

    ppos, cpos = places_of(piece), places_of(cpiece)
    seg = reorder(seg_ids[0].astype(jnp.int32).reshape(4, cpiece)).reshape(cont)
    pos = [ppos[None], ppos[:, None], cpos[None], cpos[:, None], seg[None], seg[:, None]]

    tok = prompt + cpiece
    direct = dps * rows <= 8
    parts, (hidden, low, low_prompt) = enter(x_prompt[0], x_cont[0], sc, vecs, True)
    if direct:
        first = held(packed[0][None], [parts[0]])
        first = [first] + gather_begin(first, ("dp", "row"))
        wqkv_first = gather_end(sc, first, LAYERS * 8, deps=[low])
    else:
        wqkv_all = lax.all_gather(jnp.stack(packed), ("dp", "row"), axis=1, tiled=True)
        wqkv_first = wqkv_all
    saved = []
    for i in range(LAYERS):
        last = i == LAYERS - 1
        own, oth = spread(low, low_prompt)
        if i == 1 and direct:
            wqkv_all = gather_end(sc, rest, LAYERS * 8, [wqkv_first], deps=[low])
        weight = wqkv_first if i == 0 else wqkv_all
        res = attn_fwd(i, sc, own, oth, weight, bqkv, pos, dims)
        o_send, (q, kv, lse, lsec) = res[:4], res[4:]
        if i == 0 and direct:
            rest = held(jnp.stack(packed[1:]), [lsec])
            rest = [rest] + gather_begin(rest, ("dp", "row"))
        deps = []
        if i == 2:
            cot_parts = enter_begin(cot_prompt[0], cot_cont[0], sc, [lsec])
            deps = [cot_parts[0]]
        if i == 3:
            grad = enter_end(cot_got, sc, vecs, False, prompt, [lsec])[0]
            deps = [grad]
        o_got = exchange_heads(o_send)
        avail = packs[: min(i, NB - 1) + 1]
        res = mlp_fwd(i, sc, hidden, o_got, vecs, bup, avail, prompt, last, width, deps)
        if i == 2:
            cot_got = exchange_heads(cot_parts)
        saved.append((hidden, own, oth, o_send, q, kv, lse, lsec, o_got, res[0], res[1]))
        hidden = res[2]
        if not last:
            low, low_prompt = res[3], res[4]
    y_send = exchange_heads(res[3:7])

    acc_pack = blank((NB, 2, D, PACK), BF16)
    back = None
    small = [None] * LAYERS
    small_qkv = [None] * LAYERS
    sums = []
    done_pack = [None] * NB
    done_qkv = [None] * NB
    dws = [None] * LAYERS
    dp_bits, row_bits = bits_of("dp"), bits_of("row")
    bits = dp_bits + row_bits
    top, x_bit = row_bits[0], ("x", 1)
    fence = []
    for i in reversed(range(LAYERS)):
        h_in, own, oth, o_send, q, kv, lse, lsec, o_got, h1, up = saved[i]
        res = mlp_bwd(i, sc, grad, back, h1, up, vecs, packs, prompt, fence)
        tokens, mine, theirs, grad = res[:4]
        do_send, small[i] = res[4:8], res[8]
        fence = []
        for part in sums:
            if part.ready <= 2 * (LAYERS - i):
                fence += part.step([small[i]])
        if i == LAYERS - 1:
            y_parts = leave_begin(y_send, sc, prompt_row, [small[i]])
            fence.append(y_parts[0])
        *do_send, tokens, theirs = behind([*do_send, tokens, theirs], fence)
        do_got = exchange_heads(do_send)
        ins = [tokens, swap_core(tokens), mine, swap_core(theirs)]
        ins += [o_got[0], o_got[2], swap_core(o_got[1]), swap_core(o_got[3])]
        if i < NB:
            res = dw_last(i, sc, ins, acc_pack, dps)
            keep_a, give_a, keep_b, give_b, acc_pack, token = res
            give_a, give_b = behind([give_a, give_b], do_got[1:])
            left = [n for n in bits if n != top]
            done_pack[i] = [
                Reduce(sc, keep_a, give_a, x_bit, bits, row_bits + dp_bits[::-1]),
                Reduce(sc, keep_b, give_b, top, [x_bit] + left, [x_bit] + row_bits[1:] + dp_bits[::-1]),
            ]
            sums += done_pack[i]
            fence = [token]
            if i + 1 < NB:
                fence += done_qkv[i + 1].step([token])
        else:
            fence = []
        fence += [part.give for part in sums]
        res = attn_bwd(i, sc, do_got, o_send, q, kv, lse, lsec, wqkv_all, pos, dims, fence)
        da_mine, da_theirs, dq, dkv, small_qkv[i] = res
        fence = []
        for part in sums if i > 0 else done_pack[0]:
            if part.ready <= 2 * (LAYERS - i) + 1:
                fence += part.step([small_qkv[i]], i > 0)
        if i == LAYERS - 1:
            y_prompt, y_cont = leave_end(sc, *y_parts, deps=[small_qkv[i]])
            fence.append(y_prompt)
        if i > 0:
            base, got, rest = collect(da_mine, behind([da_theirs], fence)[0], tok, prompt)
            dws[i], token = dw_qkv(i, sc, own, oth, dq, dkv)
        else:
            dws[i], token = dw_qkv(i, sc, own, oth, dq, dkv, fence)
            fence = []
            for part in done_pack[0]:
                fence += part.step([token])
            base, got, rest = collect(da_mine, behind([da_theirs], fence)[0], tok, prompt)
        fence = [token]
        if i >= NB:
            acc_pack, token = dw_mlp(i, sc, ins, acc_pack, [base])
            fence.append(token)
        for part in sums:
            part.release([got, *rest, token])
        if i < NB:
            keep, give = qkv_total(sc, i, dws[i:], dps, [got])
            done_qkv[i] = Reduce(sc, keep, give, top, left, row_bits[1:] + dp_bits[::-1])
            done_qkv[i].ready = 2 * (LAYERS - i) + 3
            sums.append(done_qkv[i])
            fence.append(give)
        back = (h_in, base, got, rest)
        sums = [part for part in sums if part.plan]

    for part in sums:
        if part.ready <= 2 * LAYERS + 2:
            step = part.step([got])
            if part not in done_pack[0]:
                continue
            fence += step
    res = final_norm(sc, grad, back, vecs, prompt, width, fence)
    dx_parts = leave_begin(exchange_heads(res[:4]), sc, prompt_row)
    for part in sums:
        part.step([dx_parts[0]])
    dx_prompt, dx_cont = leave_end(sc, *dx_parts)
    for part in sums:
        part.step([dx_prompt])
    for part in sums:
        part.step()
    g_up, g_down, g_out = pack_end(sc, [v for parts in done_pack for p in parts for v in p.finish()], width)
    g_qkv = qkv_end(sc, [v for part in done_qkv for v in part.finish()], width)

    shape = jax.ShapeDtypeStruct((4, NB, 8, D), F32)
    narrow = simple_call(
        functools.partial(narrow_kernel, width), sc, [*small, *small_qkv, res[4]], [shape], name="narrow"
    )[0]
    g_bup, g_qv, *g_vec = narrow_end(sc, *sum_small(narrow), width)
    return (
        y_prompt,
        y_cont,
        dx_prompt,
        dx_cont,
        g_qkv,
        g_qv,
        g_out,
        g_vec[0],
        g_up,
        g_bup,
        g_down,
        g_vec[1],
        g_vec[4],
        g_vec[5],
        g_vec[2],
        g_vec[3],
    )


def solution(mesh):
    dps, rows = mesh.shape["dp"], mesh.shape["row"]
    fine = Mesh(mesh.devices.reshape(dps, rows, 2, 2), ("dp", "row", "x", "core"))
    col = ("x", "core")
    both = ("dp", "row")
    tokens = P("dp", "row", col)
    narrow = P(None, col)
    wide = P(None, both, col)
    in_specs = (
        tokens,
        tokens,
        P("dp", "row"),
        P(),
        P(None, both, None, col),
        P(None, None, col),
        wide,
        narrow,
        wide,
        narrow,
        wide,
        narrow,
        narrow,
        narrow,
        narrow,
        narrow,
        tokens,
        tokens,
    )
    out_specs = (
        tokens,
        tokens,
        tokens,
        tokens,
        P(None, both, None, col),
        P(None, None, col),
        wide,
        narrow,
        wide,
        narrow,
        wide,
        narrow,
        narrow,
        narrow,
        narrow,
        narrow,
    )
    return jax.shard_map(
        per_device, mesh=fine, in_specs=in_specs, out_specs=out_specs, check_vma=False
    )
```
